32 devices in a mesh: pipe: 4 (over y, core), section: 2 (over x), tp: 4 (over z).
Axes of the slice: x: 2, y: 2, z: 4, core: 2. Of those that a mesh axis runs over, the one named last changes fastest.
Arguments:
- weights: bfloat16 [4, 2, 2, 4096, 512], P('pipe', 'section', None, 'tp'), may hold values from -6 to 6
- first_moment: float32 [4, 2, 2, 4096, 512], P('pipe', 'section', None, 'tp'), may hold values from -4 to 4
- second_moment: float32 [4, 2, 2, 4096, 512], P('pipe', 'section', None, 'tp'), may hold values from 0.1 to 2
- gradients: bfloat16 [4, 2, 2, 4096, 512], P('pipe', 'section', None, 'tp'), may hold values from -6 to 6
- old_section: int32 [4, 3], replicated, may hold values from 0 to 1, as said below
- new_section: int32 [3], replicated, may hold values from 0 to 1, as said below
- lost_pipe: int32 [4], replicated, may hold values from 0 to 3, each once
- donor_offset: int32 [3], replicated, may hold values from 1 to 3
Outputs:
- new_weights: bfloat16 [4, 2, 2, 4096, 512], P('pipe', 'section', None, 'tp')
- new_first: float32 [4, 2, 2, 4096, 512], P('pipe', 'section', None, 'tp')
- new_second: float32 [4, 2, 2, 4096, 512], P('pipe', 'section', None, 'tp')
The draws below stay inside these ranges and needn't reach their ends.
Inputs may be any that keep to these rules, and one draw needn't show every extreme that they name: `old_section`: each row places layers in section order (a layer's section never falls with the layer); 1 section of each row hold exactly 2 layers and the others one each. `new_section`: layers in any order; no section holds more than 2 layers, and some section holds exactly 2.
All inputs are finite; a program needn't handle non-finite values.
Results may differ from the reference program's by a relative error of at most 0.0075.
Values may be sent and summed in bfloat16 or wider, within the bound.
No kernel may reach another device: no remote copies, remote signals or barrier semaphores. Data moves between devices by JAX's collectives and lax.ppermute only.
A program may use at most 64 MiB of HBM per device.

```python
import math
import jax
import jax.numpy as jnp
from jax import lax

ROWS = 4096
KV_COLS = 512
CAP = 2
PIPES = 4
SECTIONS = 2
LAYERS = 3


def section_rows(key, doubles, singles):
    order = jax.random.permutation(key, SECTIONS)
    ranking = jnp.argsort(order).astype(jnp.int32)
    counts = jnp.where(ranking < doubles, 2, jnp.where(ranking < doubles + singles, 1, 0)).astype(jnp.int32)
    ending = jnp.cumsum(counts).astype(jnp.int32)
    layer_ids = jnp.arange(LAYERS, dtype=jnp.int32)
    return jnp.sum((ending[None, :] <= layer_ids[:, None]).astype(jnp.int32), axis=1).astype(jnp.int32)


def draw_old_section(key, part):
    base = jax.random.fold_in(key, 11)
    row_keys = jax.random.split(base, PIPES)
    return jax.vmap(lambda row_key: section_rows(row_key, SECTIONS // 2, SECTIONS // 2))(row_keys)


def draw_new_section(key, part):
    base = jax.random.fold_in(key, 23)
    slots = jax.random.permutation(base, SECTIONS * CAP).astype(jnp.int32)
    return (slots[:LAYERS] // CAP).astype(jnp.int32)


def shard_levels(key, extent, cuts, low, high):
    level, own = 1.0, jax.random.fold_in(key, 6)
    for dim, shards_of in cuts:
        steps = jnp.exp(jax.random.uniform(jax.random.fold_in(own, dim), (shards_of,), jnp.float32, low / len(cuts), high / len(cuts)))
        level = level * jnp.repeat(steps, extent[dim] // shards_of).reshape([-1 if axis == dim else 1 for axis in range(len(extent))])
    return level


def scatter_about(rng, extent, deviation, reach, pieces=(), held_as=jnp.bfloat16):
    array = jax.random.normal(rng, extent, jnp.float32) * deviation
    if len(pieces) > 0:
        array = shard_levels(rng, extent, pieces, -0.22, 0.18) * array
    return jnp.clip(array, min=-reach, max=reach).astype(held_as)


def setup_inputs(seed: int = 0) -> dict:
    streams_of = jax.random.split(jax.random.key(seed), 9)
    weights = scatter_about(streams_of[0], (PIPES, SECTIONS, CAP, ROWS, KV_COLS), 1.0, 6.0, ((0, 4), (1, 2), (3, 4)))
    first_moment = scatter_about(streams_of[1], (PIPES, SECTIONS, CAP, ROWS, KV_COLS), 0.5, 4.0, ((0, 4), (1, 2), (3, 4)), jnp.float32)
    second_moment = jnp.clip(jnp.exp(math.log(2.0) - 2.9957323 * jax.random.uniform(streams_of[2], (PIPES, SECTIONS, CAP, ROWS, KV_COLS), jnp.float32) ** shard_levels(streams_of[2], (PIPES, SECTIONS, CAP, ROWS, KV_COLS), ((0, 4), (1, 2), (3, 4)), -0.2, 0.2)), 0.1, 2.0)
    gradients = scatter_about(streams_of[3], (PIPES, SECTIONS, CAP, ROWS, KV_COLS), 1.0, 6.0, ((0, 4), (1, 2), (3, 4)))
    old_section = draw_old_section(jax.random.fold_in(streams_of[8], 71), 0)
    new_section = draw_new_section(jax.random.fold_in(streams_of[8], 71), 0)
    lost_pipe = jax.random.permutation(streams_of[6], PIPES).astype(jnp.int32)
    donor_offset = jax.random.randint(streams_of[7], (LAYERS,), 1, PIPES).astype(jnp.int32)
    return dict(weights=weights, first_moment=first_moment, second_moment=second_moment, gradients=gradients, old_section=old_section, new_section=new_section, lost_pipe=lost_pipe, donor_offset=donor_offset)


LEARN_RATE = 0.01
BETA_ONE = 0.9
BETA_TWO = 0.95
EPSILON = 1e-08
DECAY_RATE = 0.1

def slot_ranks(section_map):
    layer_ids = jnp.arange(section_map.shape[-1], dtype=jnp.int32)
    same_section = section_map[..., :, None] == section_map[..., None, :]
    before = layer_ids[None, :] < layer_ids[:, None]
    return lax.optimization_barrier(jnp.sum((same_section & before).astype(jnp.int32), axis=-1)).astype(jnp.int32)

def reference(weights, first_moment, second_moment, gradients, old_section, new_section, lost_pipe, donor_offset):
    pipe_ids = jnp.arange(PIPES, dtype=jnp.int32)
    layer_ids = jnp.arange(LAYERS, dtype=jnp.int32)
    is_lost = pipe_ids == lost_pipe[0]
    now_section = jnp.where(is_lost[:, None], new_section[None, :], old_section).astype(jnp.int32)
    now_slot = slot_ranks(now_section)
    old_slot = slot_ranks(old_section)
    donors = lost_pipe[donor_offset].astype(jnp.int32)
    source = jnp.where(is_lost[:, None], donors[None, :], pipe_ids[:, None]).astype(jnp.int32)
    source_section = old_section[source, layer_ids[None, :]]
    source_slot = old_slot[source, layer_ids[None, :]]
    grad_rows = gradients[pipe_ids[:, None], now_section, now_slot].astype(jnp.float32)
    mean_grad = lax.optimization_barrier(jnp.sum(grad_rows, axis=0)) / PIPES
    weight_now = weights[source, source_section, source_slot].astype(jnp.float32)
    moment_one = first_moment[source, source_section, source_slot]
    moment_two = second_moment[source, source_section, source_slot]
    next_one = BETA_ONE * moment_one + (1.0 - BETA_ONE) * mean_grad[None]
    next_two = BETA_TWO * moment_two + (1.0 - BETA_TWO) * mean_grad[None] * mean_grad[None]
    update = next_one / (jnp.sqrt(next_two) + EPSILON) + DECAY_RATE * weight_now
    next_weight = (weight_now - LEARN_RATE * update).astype(jnp.bfloat16)
    out_weight = jnp.zeros(weights.shape, jnp.bfloat16).at[pipe_ids[:, None], now_section, now_slot].set(next_weight)
    out_one = jnp.zeros(first_moment.shape, jnp.float32).at[pipe_ids[:, None], now_section, now_slot].set(next_one)
    out_two = jnp.zeros(second_moment.shape, jnp.float32).at[pipe_ids[:, None], now_section, now_slot].set(next_two)
    return (out_weight, out_one, out_two)
```

```python
import math

import jax
import jax.numpy as jnp
from jax import lax
from jax.experimental import pallas as pl
from jax.experimental.pallas import tpu as pltpu
from jax.sharding import PartitionSpec as P

LEARN_RATE = 0.01
BETA_ONE = 0.9
BETA_TWO = 0.95
EPSILON = 1e-08
DECAY_RATE = 0.1

CORES = 2
TABLE = 8192
VMEM = 48 * 1024 * 1024
AXES = ("pipe", "section")


def both(*terms):
    out = terms[0]
    for term in terms[1:]:
        out = jnp.logical_and(out, term)
    return out


def as_int(flag):
    return jnp.where(flag, 1, 0).astype(jnp.int32)


def total(terms):
    out = jnp.int32(0)
    for term in terms:
        out = out + term
    return out


class Sizes:
    def __init__(self, weights, new_section):
        self.pipes = lax.axis_size("pipe")
        self.sections = lax.axis_size("section")
        self.groups = self.pipes // CORES
        self.slots = weights.shape[2]
        self.rows = weights.shape[3]
        self.cols = weights.shape[4]
        self.layers = new_section.shape[0]
        self.half = self.rows // CORES
        self.band = self.half // self.sections
        self.grad_band = self.half // self.groups
        doubles = self.layers - self.sections
        widest = 0
        for at in range(self.sections):
            low = at + max(0, doubles - (self.sections - at))
            high = min(self.layers - self.sections + at, at + min(at, doubles) + 1)
            widest = max(widest, high - low + 1)
        self.channels = min(widest, CORES * self.slots)

    def pairs(self, target):
        out = []
        for pipe in range(self.pipes):
            for section in range(self.sections):
                group, core, to = target(pipe // CORES, pipe % CORES, section)
                pipe_to = group * CORES + core
                out.append((pipe * self.sections + section, pipe_to * self.sections + to))
        return out

    def to_core(self, value):
        return lax.ppermute(value, AXES, self.pairs(lambda g, c, s: (g, 1 - c, s)))

    def to_group(self, value, shift):
        return lax.ppermute(value, AXES, self.pairs(lambda g, c, s: ((g + shift) % self.groups, c, s)))

    def to_section(self, value, shift):
        return lax.ppermute(value, AXES, self.pairs(lambda g, c, s: (g, c, (s + shift) % self.sections)))


def plan_tables(z, pipe, section, old, new, lost_pipe, offset):
    layers = range(z.layers)
    lost = lost_pipe(0)
    group, core = pipe // CORES, pipe % CORES
    sibling = group * CORES + (1 - core)
    lost_group = lost // CORES
    tables = {}

    def now_of(at):
        return [jnp.where(at == lost, new(l), old(at, l)) for l in layers]

    def slots_of(sections):
        return [total(as_int(sections[k] == sections[l]) for k in range(l)) for l in layers]

    def layer_at(sections, slots, at, slot):
        hits = [both(sections[l] == at, slots[l] == slot) for l in layers]
        index = total(jnp.where(hits[l], l, 0) for l in layers)
        return index, total(as_int(hit) for hit in hits)

    def lookup(values, index):
        out = values[0]
        for l in layers[1:]:
            out = jnp.where(index == l, values[l], out)
        return out

    my_now = now_of(pipe)
    my_slot = slots_of(my_now)
    sib_now = now_of(sibling)
    sib_slot = slots_of(sib_now)
    new_list = [new(l) for l in layers]
    new_slot = slots_of(new_list)

    def grad_unit(l, band):
        return [
            (as_int(my_now[l] == section), my_slot[l], core * z.groups + band),
            (as_int(sib_now[l] == section), sib_slot[l], band),
        ]

    for shift in range(1, z.groups):
        band = lax.rem(group + shift, z.groups)
        tables["grad_out", shift] = [grad_unit(l, band) for l in layers]
    tables["grad_sum"] = [
        grad_unit(l, group) + [(1, l, 0)] * (z.groups - 1) for l in layers
    ]
    tables["grad_mean"] = [[(1, l, 0)] * z.sections for l in layers]
    for name, sections, slots in (("mean_mine", my_now, my_slot), ("mean_sibling", sib_now, sib_slot)):
        units = []
        for slot in range(z.slots):
            index, found = layer_at(sections, slots, section, slot)
            for band in range(z.groups):
                unit = []
                for shift in range(z.groups):
                    from_group = lax.rem(group + z.groups - shift, z.groups)
                    unit.append((found * as_int(from_group == band), index, 0))
                units.append(unit)
        tables[name] = units

    donor = [lost_pipe(offset(l)) for l in layers]
    source_section = [old(donor[l], l) for l in layers]
    source_slot = [
        total(as_int(old(donor[l], k) == source_section[l]) for k in range(l)) for l in layers
    ]
    source_group = [donor[l] // CORES for l in layers]
    channel = [
        total(
            as_int(both(source_group[k] == source_group[l], source_section[k] == source_section[l]))
            for k in range(l)
        )
        for l in layers
    ]
    here = [as_int(source_group[l] == group) for l in layers]
    my_chip = [here[l] * as_int(source_section[l] == section) for l in layers]
    from_me = [as_int(donor[l] == pipe) for l in layers]
    slot_here = source_slot

    for shift in range(1, z.sections):
        band = lax.rem(section + shift, z.sections)
        units = []
        for k in range(z.channels):
            hit = [my_chip[l] * as_int(channel[l] == k) for l in layers]
            slot = total(hit[l] * slot_here[l] for l in layers)
            mine = total(hit[l] * from_me[l] for l in layers)
            found = total(hit)
            units.append([(mine, slot, core * z.sections + band), (found - mine, slot, band)])
        tables["spread", shift] = units

    def held(l_my_chip, l_from_me, l_slot, l_here, l_channel, l_section):
        unit = [
            (l_my_chip * l_from_me, l_slot, core * z.sections + section),
            (l_my_chip * (1 - l_from_me), l_slot, section),
        ]
        for shift in range(1, z.sections):
            sender = lax.rem(section + z.sections - shift, z.sections)
            unit.append((l_here * as_int(l_section == sender), l_channel, 0))
        return unit

    tables["across"] = [
        held(my_chip[l], from_me[l], slot_here[l], here[l], channel[l], source_section[l])
        for l in layers
    ]

    def arrived(index, found):
        unit = held(
            *(
                lookup(values, index)
                for values in (my_chip, from_me, slot_here, here, channel, source_section)
            )
        )
        unit = [(flag * found, at, block) for flag, at, block in unit]
        from_group = lookup(source_group, index)
        for shift in range(1, z.groups):
            sender = lax.rem(group + z.groups - shift, z.groups)
            unit.append((found * as_int(from_group == sender), index, 0))
        return unit

    for shift in range(1, z.sections):
        target = lax.rem(section + shift, z.sections)
        tables["deliver", shift] = [
            arrived(*layer_at(new_list, new_slot, target, slot)) for slot in range(z.slots)
        ]
    units = []
    for slot in range(z.slots):
        own = arrived(*layer_at(new_list, new_slot, section, slot))
        for band in range(z.sections):
            mine = as_int(section == band)
            unit = [(flag * mine, at, block) for flag, at, block in own]
            for shift in range(1, z.sections):
                sender = lax.rem(section + z.sections - shift, z.sections)
                unit.append((as_int(sender == band), slot, 0))
            units.append(unit)
    tables["collect"] = units

    last = [as_int(pipe == lost), core]
    for slot in range(z.slots):
        last.append(layer_at(my_now, my_slot, section, slot)[1])
    tables["update"] = [[tuple(last)]]
    return tables


def make_plan(z, old_section, new_section, lost_pipe, donor_offset):
    starts = {}
    place = jnp.stack([lax.axis_index("pipe"), lax.axis_index("section")]).astype(jnp.int32)

    def kernel(place_ref, old_ref, new_ref, lost_ref, offset_ref, table_ref):
        tables = plan_tables(
            z,
            place_ref[0],
            place_ref[1],
            lambda at, l: old_ref[at, l],
            lambda l: new_ref[l],
            lambda rank: lost_ref[rank],
            lambda l: offset_ref[l],
        )
        at = 0
        for name, units in tables.items():
            starts[name] = at
            for unit in units:
                for entry in unit:
                    for value in entry:
                        table_ref[at] = jnp.int32(value)
                        at += 1
        assert at <= TABLE

    smem = pl.BlockSpec(memory_space=pltpu.SMEM)
    table = pl.pallas_call(
        kernel,
        out_shape=jax.ShapeDtypeStruct((TABLE,), jnp.int32),
        in_specs=[smem] * 5,
        out_specs=smem,
        name="plan",
    )(place, old_section, new_section, lost_pipe, donor_offset)
    return table, starts


def pack(z, table, start, units, block, sources, name):
    count = len(sources)

    def entry(table_ref, unit, source, field):
        return table_ref[start + (unit * count + source) * 3 + field]

    def kernel(table_ref, *refs):
        unit = pl.program_id(0)
        out_ref = refs[-1]
        out = None
        for source, ref in enumerate(refs[:-1]):
            flag = entry(table_ref, unit, source, 0) != 0
            term = jnp.where(flag, ref[...].astype(jnp.float32), 0.0)
            out = term if out is None else out + term
        out_ref[...] = out.astype(out_ref.dtype)

    def index(source):
        def index_map(unit, table_ref):
            return (
                entry(table_ref, unit, source, 1),
                entry(table_ref, unit, source, 2),
                0,
            )

        return index_map

    moved = units * block * z.cols * (2 + sum(array.dtype.itemsize for array in sources))
    return pl.pallas_call(
        kernel,
        grid_spec=pltpu.PrefetchScalarGridSpec(
            num_scalar_prefetch=1,
            grid=(units,),
            in_specs=[pl.BlockSpec((1, block, z.cols), index(i)) for i in range(count)],
            out_specs=pl.BlockSpec((1, block, z.cols), lambda unit, table_ref: (unit, 0, 0)),
        ),
        out_shape=jax.ShapeDtypeStruct((units, block, z.cols), jnp.bfloat16),
        compiler_params=pltpu.CompilerParams(vmem_limit_bytes=VMEM),
        cost_estimate=pl.CostEstimate(
            flops=units * block * z.cols * count, bytes_accessed=moved, transcendentals=0
        ),
        name=name,
    )(table, *sources)


def update(z, table, start, state, rebuilt, mean):
    block = math.gcd(z.half, 256)
    per_half = z.half // block

    def kernel(table_ref, w_ref, one_ref, two_ref, *refs):
        mine_refs, other_refs = refs[:4], refs[4:8]
        out_w, out_one, out_two = refs[8:]
        slot, row = pl.program_id(0), pl.program_id(1)
        is_lost = table_ref[start] != 0
        mine = row // per_half == table_ref[start + 1]
        found = table_ref[start + 2 + slot] != 0

        def from_halves(at):
            return jnp.where(mine, mine_refs[at][...], other_refs[at][...]).astype(jnp.float32)

        grad = from_halves(3) * (1.0 / z.pipes)
        weight = jnp.where(is_lost, from_halves(0), w_ref[...].astype(jnp.float32))
        one = jnp.where(is_lost, from_halves(1), one_ref[...])
        two = jnp.where(is_lost, from_halves(2), two_ref[...])
        next_one = BETA_ONE * one + (1.0 - BETA_ONE) * grad
        next_two = BETA_TWO * two + (1.0 - BETA_TWO) * grad * grad
        step = next_one / (jnp.sqrt(next_two) + EPSILON) + DECAY_RATE * weight
        out_w[...] = jnp.where(found, weight - LEARN_RATE * step, 0.0).astype(out_w.dtype)
        out_one[...] = jnp.where(found, next_one, 0.0)
        out_two[...] = jnp.where(found, next_two, 0.0)

    def local(slot, row, table_ref):
        keep = 1 - table_ref[start]
        return (slot * keep, row * keep, 0)

    def half_of(own, needs_lost):
        def index_map(slot, row, table_ref):
            use = as_int((row // per_half == table_ref[start + 1]) == own)
            if needs_lost:
                use = use * table_ref[start]
            return (slot * use, lax.rem(row, per_half) * use, 0)

        return index_map

    def spec(index_map):
        return pl.BlockSpec((1, block, z.cols), index_map)

    def halves(own):
        return [spec(half_of(own, True))] * 3 + [spec(half_of(own, False))]

    shape = (z.slots, z.rows, z.cols)
    elements = z.slots * z.rows * z.cols
    return pl.pallas_call(
        kernel,
        grid_spec=pltpu.PrefetchScalarGridSpec(
            num_scalar_prefetch=1,
            grid=(z.slots, z.rows // block),
            in_specs=[spec(local)] * 3 + halves(True) + halves(False),
            out_specs=[spec(lambda slot, row, table_ref: (slot, row, 0))] * 3,
        ),
        out_shape=(
            jax.ShapeDtypeStruct(shape, jnp.bfloat16),
            jax.ShapeDtypeStruct(shape, jnp.float32),
            jax.ShapeDtypeStruct(shape, jnp.float32),
        ),
        compiler_params=pltpu.CompilerParams(vmem_limit_bytes=VMEM),
        cost_estimate=pl.CostEstimate(
            flops=elements * 14, bytes_accessed=elements * 22, transcendentals=elements * 2
        ),
        name="update",
    )(table, *state, *(r[0] for r in rebuilt), mean[0], *(r[1] for r in rebuilt), mean[1])


def per_device(
    weights,
    first_moment,
    second_moment,
    gradients,
    old_section,
    new_section,
    lost_pipe,
    donor_offset,
):
    z = Sizes(weights, new_section)
    core = lax.rem(lax.axis_index("pipe"), CORES)
    state = (weights[0, 0], first_moment[0, 0], second_moment[0, 0])
    grads = gradients[0, 0]

    def sibling_half(array):
        part = lax.dynamic_slice_in_dim(array, (1 - core) * z.half, z.half, axis=1)
        return z.to_core(part.astype(jnp.bfloat16))

    grads_sib = sibling_half(grads)
    state_sib = [sibling_half(array) for array in state]
    table, starts = make_plan(z, old_section, new_section, lost_pipe, donor_offset)

    def packed(name, units, block, sources):
        label = name if isinstance(name, str) else name[0]
        return pack(z, table, starts[name], units, block, sources, label)

    arrived = [
        z.to_group(packed(("grad_out", shift), z.layers, z.grad_band, [grads, grads_sib]), shift)
        for shift in range(1, z.groups)
    ]
    summed = packed("grad_sum", z.layers, z.grad_band, [grads, grads_sib] + arrived)
    others = [z.to_section(summed, shift) for shift in range(1, z.sections)]
    mean_band = packed("grad_mean", z.layers, z.grad_band, [summed] + others)
    bands = [mean_band] + [z.to_group(mean_band, shift) for shift in range(1, z.groups)]
    mean_units = z.slots * z.groups
    halves_shape = (z.slots, z.half, z.cols)
    mean_mine = packed("mean_mine", mean_units, z.grad_band, bands).reshape(halves_shape)
    mean_theirs = packed("mean_sibling", mean_units, z.grad_band, bands).reshape(halves_shape)
    mean = (mean_mine, z.to_core(mean_theirs))

    rebuilt = []
    for own, sib in zip(state, state_sib):
        held = [own, sib]
        for shift in range(1, z.sections):
            sent = packed(("spread", shift), z.channels, z.band, [own, sib])
            held.append(z.to_section(sent, shift))
        crossing = packed("across", z.layers, z.band, held)
        held = held + [z.to_group(crossing, shift) for shift in range(1, z.groups)]
        delivered = [
            z.to_section(packed(("deliver", shift), z.slots, z.band, held), shift)
            for shift in range(1, z.sections)
        ]
        half = packed("collect", z.slots * z.sections, z.band, held + delivered)
        half = half.reshape(halves_shape)
        rebuilt.append((half, z.to_core(half)))

    outs = update(z, table, starts["update"], state, rebuilt, mean)
    return tuple(out[None, None] for out in outs)


def solution(mesh):
    split = P("pipe", "section", None, "tp", None)
    return jax.shard_map(
        per_device,
        mesh=mesh,
        in_specs=(split,) * 4 + (P(),) * 4,
        out_specs=(split,) * 3,
        check_vma=False,
    )
```

```python
import math

import jax
import jax.numpy as jnp
from jax import lax
from jax.experimental import pallas as pl
from jax.experimental.pallas import tpu as pltpu
from jax.sharding import PartitionSpec as P

LEARN_RATE = 0.01
BETA_ONE = 0.9
BETA_TWO = 0.95
EPSILON = 1e-08
DECAY_RATE = 0.1

CORES = 2
CHUNKS = 4
VMEM = 24 * 1024 * 1024
AXES = ("pipe", "section")


def both(*terms):
    out = terms[0]
    for term in terms[1:]:
        out = jnp.logical_and(out, term)
    return out


def as_int(flag):
    return jnp.where(flag, 1, 0).astype(jnp.int32)


def total(terms):
    out = jnp.int32(0)
    for term in terms:
        out = out + term
    return out


class Sizes:
    def __init__(self, weights, new_section):
        self.pipes = lax.axis_size("pipe")
        self.sections = lax.axis_size("section")
        self.groups = self.pipes // CORES
        self.slots = weights.shape[2]
        self.rows = weights.shape[3]
        self.cols = weights.shape[4]
        self.layers = new_section.shape[0]
        self.half = self.rows // CORES
        self.band = self.half // self.sections
        self.chunks = max(1, min(CHUNKS, self.band // 32))
        self.sub = self.band // self.chunks
        doubles = self.layers - self.sections
        widest = 0
        for at in range(self.sections):
            low = at + max(0, doubles - (self.sections - at))
            high = min(self.layers - self.sections + at, at + min(at, doubles) + 1)
            widest = max(widest, high - low + 1)
        self.channels = min(widest, CORES * self.slots)

    def send(self, value, target, group=None):
        pairs = []
        for pipe in range(self.pipes):
            if group is not None and pipe // CORES != group:
                continue
            for section in range(self.sections):
                group_to, core, to = target(pipe // CORES, pipe % CORES, section)
                pipe_to = group_to * CORES + core
                pairs.append((pipe * self.sections + section, pipe_to * self.sections + to))
        return lax.ppermute(value, AXES, pairs)

    def to_core(self, value, group=None):
        return self.send(value, lambda g, c, s: (g, 1 - c, s), group)

    def to_group(self, value, shift, group=None):
        return self.send(value, lambda g, c, s: ((g + shift) % self.groups, c, s), group)

    def to_section(self, value, shift, group=None):
        return self.send(value, lambda g, c, s: (g, c, (s + shift) % self.sections), group)


def plan_tables(z, pipe, section, old, new, lost_pipe, offset):
    layers = range(z.layers)
    lost = lost_pipe(0)
    group, core = pipe // CORES, pipe % CORES
    sibling = group * CORES + (1 - core)
    lost_group = lost // CORES
    tables = {}

    def now_of(at):
        return [jnp.where(at == lost, new(l), old(at, l)) for l in layers]

    def slots_of(sections):
        return [total(as_int(sections[k] == sections[l]) for k in range(l)) for l in layers]

    def layer_at(sections, slots, at, slot):
        hits = [both(sections[l] == at, slots[l] == slot) for l in layers]
        index = total(jnp.where(hits[l], l, 0) for l in layers)
        return index, total(as_int(hit) for hit in hits)

    def lookup(values, index):
        out = values[0]
        for l in layers[1:]:
            out = jnp.where(index == l, values[l], out)
        return out

    my_now = now_of(pipe)
    my_slot = slots_of(my_now)
    sib_now = now_of(sibling)
    sib_slot = slots_of(sib_now)
    new_list = [new(l) for l in layers]
    new_slot = slots_of(new_list)

    donor = [lost_pipe(offset(l)) for l in layers]
    source_section = [old(donor[l], l) for l in layers]
    source_slot = [
        total(as_int(old(donor[l], k) == source_section[l]) for k in range(l)) for l in layers
    ]
    source_group = [donor[l] // CORES for l in layers]
    crosses = [as_int(source_group[l] != lost_group) for l in layers]
    rank = [total(crosses[k] for k in range(l)) for l in layers]
    channel = [
        total(
            as_int(both(source_group[k] == source_group[l], source_section[k] == source_section[l]))
            for k in range(l)
        )
        for l in layers
    ]
    tables["branch"] = [[(lost_group, total(crosses))]]

    for first, parts, me in (("group", z.groups, group), ("section", z.sections, section)):

        def grad_unit(l, band):
            return [
                (as_int(my_now[l] == section), my_slot[l] * parts + band),
                (as_int(sib_now[l] == section), sib_slot[l] * parts + band),
            ]

        for shift in range(1, parts):
            band = lax.rem(me + shift, parts)
            tables["grad_out", first, shift] = [grad_unit(l, band) for l in layers]
        tables["grad_sum", first] = [
            grad_unit(l, me) + [(1, l)] * (parts - 1) for l in layers
        ]
        other = z.sections if first == "group" else z.groups
        tables["grad_mean", first] = [[(1, l)] * other for l in layers]
        for name, sections, slots in (("mine", my_now, my_slot), ("sibling", sib_now, sib_slot)):
            units = []
            for slot in range(z.slots):
                index, found = layer_at(sections, slots, section, slot)
                for band in range(parts):
                    unit = []
                    for shift in range(parts):
                        sender = lax.rem(me + parts - shift, parts)
                        unit.append((found * as_int(sender == band), index))
                    units.append(unit)
            tables[name, first] = units

    here = [as_int(source_group[l] == group) for l in layers]
    my_chip = [here[l] * as_int(source_section[l] == section) for l in layers]
    from_me = [as_int(donor[l] == pipe) for l in layers]

    for shift in range(1, z.sections):
        band = lax.rem(section + shift, z.sections)
        units = []
        for k in range(z.channels):
            hit = [my_chip[l] * as_int(channel[l] == k) for l in layers]
            slot = total(hit[l] * source_slot[l] for l in layers)
            mine = total(hit[l] * from_me[l] for l in layers)
            found = total(hit)
            index = slot * z.sections + band
            units.append([(mine, index), (found - mine, index)])
        tables["spread", shift] = units

    def held(l_my_chip, l_from_me, l_slot, l_here, l_channel, l_section):
        index = l_slot * z.sections + section
        unit = [(l_my_chip * l_from_me, index), (l_my_chip * (1 - l_from_me), index)]
        for shift in range(1, z.sections):
            sender = lax.rem(section + z.sections - shift, z.sections)
            unit.append((l_here * as_int(l_section == sender), l_channel))
        return unit

    def held_at(index):
        return held(
            *(
                lookup(values, index)
                for values in (my_chip, from_me, source_slot, here, channel, source_section)
            )
        )

    units = []
    for u in range(z.layers):
        hit = [crosses[l] * as_int(rank[l] == u) for l in layers]
        index = total(hit[l] * l for l in layers)
        found = total(hit)
        units.append([(flag * found, at) for flag, at in held_at(index)])
    tables["across"] = units

    def arrived(index, found):
        found = found * as_int(group == lost_group)
        unit = [(flag * found, at) for flag, at in held_at(index)]
        from_group = lookup(source_group, index)
        for shift in range(1, z.groups):
            sender = lax.rem(group + z.groups - shift, z.groups)
            unit.append((found * as_int(from_group == sender), lookup(rank, index)))
        return unit

    for shift in range(1, z.sections):
        target = lax.rem(section + shift, z.sections)
        tables["deliver", shift] = [
            arrived(*layer_at(new_list, new_slot, target, slot)) for slot in range(z.slots)
        ]
    units = []
    for slot in range(z.slots):
        own = arrived(*layer_at(new_list, new_slot, section, slot))
        for band in range(z.sections):
            mine = as_int(section == band)
            unit = [(flag * mine, at) for flag, at in own]
            for shift in range(1, z.sections):
                sender = lax.rem(section + z.sections - shift, z.sections)
                unit.append((as_int(both(sender == band, group == lost_group)), slot))
            units.append(unit)
    tables["collect"] = units

    last = [as_int(pipe == lost), core]
    for slot in range(z.slots):
        last.append(layer_at(my_now, my_slot, section, slot)[1])
    tables["update"] = [[tuple(last)]]
    return tables


def table_size(z):
    sources = z.sections + z.groups + z.sections + 2
    units = (z.sections + z.groups) * (4 * z.layers + 4 * z.slots)
    units += z.sections * (z.channels + 2 * z.slots) + z.layers
    return -(-(2 * units * sources + z.slots + 8) // 1024) * 1024


def make_plan(z, place, old_section, new_section, lost_pipe, donor_offset):
    starts = {}
    size = table_size(z)

    def kernel(place_ref, old_ref, new_ref, lost_ref, offset_ref, table_ref):
        tables = plan_tables(
            z,
            place_ref[0],
            place_ref[1],
            lambda at, l: old_ref[at, l],
            lambda l: new_ref[l],
            lambda rank: lost_ref[rank],
            lambda l: offset_ref[l],
        )
        at = 0
        for name, units in tables.items():
            starts[name] = at
            for unit in units:
                for entry in unit:
                    for value in entry:
                        table_ref[at] = jnp.int32(value)
                        at += 1
        assert at <= size

    smem = pl.BlockSpec(memory_space=pltpu.SMEM)
    table = pl.pallas_call(
        kernel,
        out_shape=jax.ShapeDtypeStruct((size,), jnp.int32),
        in_specs=[smem] * 5,
        out_specs=smem,
        name="plan",
    )(place, old_section, new_section, lost_pipe, donor_offset)
    return table, starts


SMEM_SPEC = pl.BlockSpec(memory_space=pltpu.SMEM)
VMEM_SPEC = pl.BlockSpec(memory_space=pltpu.VMEM)


def cost(operands, results):
    moved = sum(math.prod(a.shape) * a.dtype.itemsize for a in (*operands, *results))
    return pl.CostEstimate(flops=moved // 4, bytes_accessed=moved, transcendentals=0)


def pack(z, table, start, units, sources, name):
    count = len(sources)
    arrays, _, rows, cols = sources[0].shape

    def kernel(table_ref, *refs):
        out_ref = refs[-1]
        for unit in range(units):
            for source, ref in enumerate(refs[:-1]):
                at = start + (unit * count + source) * 2

                @pl.when(table_ref[at] != 0)
                def _(unit=unit, ref=ref, at=at):
                    out_ref[:, pl.ds(unit, 1)] = ref[:, pl.ds(table_ref[at + 1], 1)]

    out = jax.ShapeDtypeStruct((arrays, units, rows, cols), jnp.bfloat16)
    return pl.pallas_call(
        kernel,
        out_shape=out,
        in_specs=[SMEM_SPEC] + [VMEM_SPEC] * count,
        out_specs=VMEM_SPEC,
        compiler_params=pltpu.CompilerParams(vmem_limit_bytes=VMEM),
        cost_estimate=cost([out], [out]),
        name=name,
    )(table, *sources)


def add_up(z, table, start, units, sources, name):
    count = len(sources)
    _, rows, cols = sources[0].shape

    def kernel(table_ref, *refs):
        out_ref = refs[-1]
        for unit in range(units):
            out = jnp.zeros((rows, cols), jnp.float32)
            for source, ref in enumerate(refs[:-1]):
                at = start + (unit * count + source) * 2
                block = ref[table_ref[at + 1]].astype(jnp.float32)
                out = out + jnp.where(table_ref[at] != 0, block, 0.0)
            out_ref[unit] = out.astype(out_ref.dtype)

    out = jax.ShapeDtypeStruct((units, rows, cols), jnp.bfloat16)
    return pl.pallas_call(
        kernel,
        out_shape=out,
        in_specs=[SMEM_SPEC] + [VMEM_SPEC] * count,
        out_specs=VMEM_SPEC,
        compiler_params=pltpu.CompilerParams(vmem_limit_bytes=VMEM),
        cost_estimate=cost([out] * 2, [out]),
        name=name,
    )(table, *sources)


def halve(z, place, arrays, chunk, chunks, name):
    sub = z.band // chunks
    count = len(arrays)
    views = [a.reshape(z.slots, CORES, z.sections, chunks, sub, z.cols) for a in arrays]

    def kernel(place_ref, *refs):
        own_refs, their_refs, (own_out, their_out) = refs[:count], refs[count:-2], refs[-2:]
        for at in range(count):
            own_out[at] = own_refs[at][:, 0, :, 0].astype(jnp.bfloat16)
            their_out[at] = their_refs[at][:, 0, :, 0].astype(jnp.bfloat16)

    def spec(own):
        def index_map(step, place_ref):
            core = lax.rem(place_ref[0], CORES)
            return (0, core if own else 1 - core, 0, chunk, 0, 0)

        return pl.BlockSpec((z.slots, 1, z.sections, 1, sub, z.cols), index_map)

    shape = (count, z.slots, z.sections, sub, z.cols)
    out = jax.ShapeDtypeStruct(shape, jnp.bfloat16)
    out_spec = pl.BlockSpec(shape, lambda step, place_ref: (0, 0, 0, 0, 0))
    return pl.pallas_call(
        kernel,
        grid_spec=pltpu.PrefetchScalarGridSpec(
            num_scalar_prefetch=1,
            grid=(1,),
            in_specs=[spec(True)] * count + [spec(False)] * count,
            out_specs=[out_spec] * 2,
        ),
        out_shape=(out, out),
        compiler_params=pltpu.CompilerParams(vmem_limit_bytes=VMEM),
        cost_estimate=cost([out] * 4, [out] * 2),
        name=name,
    )(place, *views, *views)


def update(z, table, start, chunk, state, rebuilt, mean, outs):
    views = [a.reshape(z.slots, CORES, z.sections, z.chunks, z.sub, z.cols) for a in state]
    rebuilt = [a.reshape(3, z.slots, z.sections, z.sub, z.cols) for a in rebuilt]
    mean = [a.reshape(z.slots, z.sections, z.chunks, z.sub, z.cols) for a in mean]
    outs = [] if outs is None else list(outs)

    def kernel(table_ref, *refs):
        local_refs, lost_refs, mean_refs = refs[:3], refs[3:5], refs[5:7]
        out_w, out_one, out_two = refs[-3:]
        slot = pl.program_id(0)
        is_lost = table_ref[start] != 0
        core = table_ref[start + 1]
        found = table_ref[start + 2 + slot] != 0

        def step(half, band, weight, one, two, grad):
            grad = grad.astype(jnp.float32) * (1.0 / z.pipes)
            weight = weight.astype(jnp.float32)
            next_one = BETA_ONE * one.astype(jnp.float32) + (1.0 - BETA_ONE) * grad
            next_two = BETA_TWO * two.astype(jnp.float32) + (1.0 - BETA_TWO) * grad * grad
            move = next_one / (jnp.sqrt(next_two) + EPSILON) + DECAY_RATE * weight
            out_w[0, half, band, 0] = (weight - LEARN_RATE * move).astype(out_w.dtype)
            out_one[0, half, band, 0] = next_one
            out_two[0, half, band, 0] = next_two

        for half in range(CORES):
            for source in range(2):
                mine = both(found, (core == half) == (source == 0))

                @pl.when(both(mine, is_lost))
                def _(half=half, source=source):
                    for band in range(z.sections):
                        ref = lost_refs[source]
                        step(
                            half, band, ref[0, 0, band], ref[1, 0, band], ref[2, 0, band],
                            mean_refs[source][0, band, 0],
                        )

                @pl.when(both(mine, jnp.logical_not(is_lost)))
                def _(half=half, source=source):
                    for band in range(z.sections):
                        step(
                            half, band, *(ref[0, half, band, 0] for ref in local_refs),
                            mean_refs[source][0, band, 0],
                        )

        @pl.when(jnp.logical_not(found))
        def _():
            for ref in (out_w, out_one, out_two):
                ref[...] = jnp.zeros(ref.shape, ref.dtype)

    def local(slot, table_ref):
        return (slot * (1 - table_ref[start]), 0, 0, chunk, 0, 0)

    def lost(slot, table_ref):
        return (0, slot * table_ref[start], 0, 0, 0)

    state_block = (1, CORES, z.sections, 1, z.sub, z.cols)
    state_spec = pl.BlockSpec(state_block, local)
    lost_spec = pl.BlockSpec((3, 1, z.sections, z.sub, z.cols), lost)
    mean_spec = pl.BlockSpec(
        (1, z.sections, 1, z.sub, z.cols), lambda slot, table_ref: (slot, 0, chunk, 0, 0)
    )
    out_spec = pl.BlockSpec(state_block, lambda slot, table_ref: (slot, 0, 0, chunk, 0, 0))
    shape = views[0].shape
    elements = z.slots * z.rows * z.cols // z.chunks
    return pl.pallas_call(
        kernel,
        grid_spec=pltpu.PrefetchScalarGridSpec(
            num_scalar_prefetch=1,
            grid=(z.slots,),
            in_specs=[state_spec] * 3
            + [lost_spec] * 2
            + [mean_spec] * 2
            + [pl.BlockSpec(memory_space=pl.ANY)] * len(outs),
            out_specs=[out_spec] * 3,
        ),
        out_shape=(
            jax.ShapeDtypeStruct(shape, jnp.bfloat16),
            jax.ShapeDtypeStruct(shape, jnp.float32),
            jax.ShapeDtypeStruct(shape, jnp.float32),
        ),
        input_output_aliases={8 + at: at for at in range(len(outs))},
        compiler_params=pltpu.CompilerParams(vmem_limit_bytes=VMEM),
        cost_estimate=pl.CostEstimate(
            flops=elements * 14, bytes_accessed=elements * 22, transcendentals=elements * 2
        ),
        name="update",
    )(table, *views, *rebuilt, *mean, *outs)


def average(z, table, starts, first, own, theirs):
    if first == "group":
        parts, other, send_first, send_other = z.groups, z.sections, z.to_group, z.to_section
    else:
        parts, other, send_first, send_other = z.sections, z.groups, z.to_section, z.to_group
    rows = z.half // parts
    held = [a.reshape(z.slots * parts, rows, z.cols) for a in (own, theirs)]

    def summed(name, sources):
        return add_up(z, table, starts[name], z.layers, sources, name[0])

    arrived = [
        send_first(summed(("grad_out", first, shift), held), shift) for shift in range(1, parts)
    ]
    part = summed(("grad_sum", first), held + arrived)
    others = [send_other(part, shift) for shift in range(1, other)]
    whole = summed(("grad_mean", first), [part] + others)
    bands = [whole] + [send_first(whole, shift) for shift in range(1, parts)]
    bands = [band[None] for band in bands]
    mine, theirs = (
        pack(z, table, starts[name, first], z.slots * parts, bands, name + "_mean")
        for name in ("mine", "sibling")
    )
    return mine, z.to_core(theirs)


def per_device(
    weights,
    first_moment,
    second_moment,
    gradients,
    old_section,
    new_section,
    lost_pipe,
    donor_offset,
):
    z = Sizes(weights, new_section)
    place = jnp.stack([lax.axis_index("pipe"), lax.axis_index("section")]).astype(jnp.int32)
    state = (weights[0, 0], first_moment[0, 0], second_moment[0, 0])

    def swap(arrays, chunk, chunks, name):
        own, theirs = halve(z, place, arrays, chunk, chunks, name)
        return own, z.to_core(theirs)

    grads = swap((gradients[0, 0],), 0, 1, "halve_gradients")
    first_chunk = swap(state, 0, z.chunks, "halve_state")
    table, starts = make_plan(z, place, old_section, new_section, lost_pipe, donor_offset)

    def run(lost_group, crossing, first):
        exact = z.layers <= 3
        donor_channels = min(z.channels, crossing) if exact else z.channels
        kept = z.layers if crossing == 1 else z.layers - crossing
        kept_channels = min(z.channels, kept) if exact else z.channels
        others = [g for g in range(z.groups) if g != lost_group]

        def packed(name, units, sources):
            label = name if isinstance(name, str) else name[0]
            return pack(z, table, starts[name], units, sources, label)

        mean = average(z, table, starts, first, *grads)
        outs = None
        for chunk in range(z.chunks):
            pair = first_chunk if chunk == 0 else swap(state, chunk, z.chunks, "halve_state")
            held = [a.reshape(3, z.slots * z.sections, z.sub, z.cols) for a in pair]
            spread_here, spread_lost = [], []
            for shift in range(1, z.sections):
                sent = packed(("spread", shift), donor_channels, held[:2])
                parts = [z.to_section(sent, shift, g) for g in others]
                spread_here.append(parts[0])
                for part in parts[1:]:
                    spread_here[-1] = spread_here[-1] + part
                if kept_channels:
                    if kept_channels != donor_channels:
                        sent = packed(("spread", shift), kept_channels, held[:2])
                    spread_lost.append(z.to_section(sent, shift, lost_group))
            crossed = packed("across", crossing, held + spread_here)
            from_groups = [
                z.to_group(crossed, shift, (lost_group - shift) % z.groups)
                for shift in range(1, z.groups)
            ]
            if not spread_lost:
                spread_lost = spread_here
            held = held + spread_lost + from_groups
            delivered = [
                z.to_section(packed(("deliver", shift), z.slots, held), shift, lost_group)
                for shift in range(1, z.sections)
            ]
            half = packed("collect", z.slots * z.sections, held + delivered)
            rebuilt = (half, z.to_core(half, lost_group))
            outs = update(z, table, starts["update"], chunk, state, rebuilt, mean, outs)
        return tuple(outs)

    counts = list(range(1, z.layers + 1)) if z.layers <= 3 else [z.layers]
    branches = [
        lambda lost_group=lost_group, crossing=crossing: run(
            lost_group, crossing, "section" if crossing == z.layers else "group"
        )
        for lost_group in range(z.groups)
        for crossing in counts
    ]
    at = starts["branch"]
    lost_group, crossing = table[at], table[at + 1]
    chosen = lost_group * len(counts)
    if len(counts) > 1:
        chosen = chosen + jnp.maximum(crossing, 1) - 1
    outs = lax.switch(chosen, branches)
    return tuple(out.reshape((1, 1) + (z.slots, z.rows, z.cols)) for out in outs)


def solution(mesh):
    split = P("pipe", "section", None, "tp", None)
    return jax.shard_map(
        per_device,
        mesh=mesh,
        in_specs=(split,) * 4 + (P(),) * 4,
        out_specs=(split,) * 3,
        check_vma=False,
    )
```

```python
import math

import jax
import jax.numpy as jnp
from jax import lax
from jax.experimental import pallas as pl
from jax.experimental.pallas import tpu as pltpu
from jax.sharding import PartitionSpec as P

LEARN_RATE = 0.01
BETA_ONE = 0.9
BETA_TWO = 0.95
EPSILON = 1e-08
DECAY_RATE = 0.1

CORES = 2
CHUNKS = 4
VMEM = 24 * 1024 * 1024
AXES = ("pipe", "section")


def both(*terms):
    out = terms[0]
    for term in terms[1:]:
        out = jnp.logical_and(out, term)
    return out


def as_int(flag):
    return jnp.where(flag, 1, 0).astype(jnp.int32)


def total(terms):
    out = jnp.int32(0)
    for term in terms:
        out = out + term
    return out


class Sizes:
    def __init__(self, weights, new_section):
        self.pipes = lax.axis_size("pipe")
        self.sections = lax.axis_size("section")
        self.groups = self.pipes // CORES
        self.slots = weights.shape[2]
        self.rows = weights.shape[3]
        self.cols = weights.shape[4]
        self.layers = new_section.shape[0]
        self.half = self.rows // CORES
        self.band = self.half // self.sections
        self.chunks = max(1, min(CHUNKS, self.band // 32))
        self.sub = self.band // self.chunks
        doubles = self.layers - self.sections
        widest = 0
        for at in range(self.sections):
            low = at + max(0, doubles - (self.sections - at))
            high = min(self.layers - self.sections + at, at + min(at, doubles) + 1)
            widest = max(widest, high - low + 1)
        self.channels = min(widest, CORES * self.slots)

    def send(self, value, target, group=None):
        pairs = []
        for pipe in range(self.pipes):
            if group is not None and pipe // CORES != group:
                continue
            for section in range(self.sections):
                group_to, core, to = target(pipe // CORES, pipe % CORES, section)
                pipe_to = group_to * CORES + core
                pairs.append((pipe * self.sections + section, pipe_to * self.sections + to))
        return lax.ppermute(value, AXES, pairs)

    def to_core(self, value, group=None):
        return self.send(value, lambda g, c, s: (g, 1 - c, s), group)

    def to_group(self, value, shift, group=None):
        return self.send(value, lambda g, c, s: ((g + shift) % self.groups, c, s), group)

    def to_section(self, value, shift, group=None):
        return self.send(value, lambda g, c, s: (g, c, (s + shift) % self.sections), group)


def plan_tables(z, pipe, section, old, new, lost_pipe, offset):
    layers = range(z.layers)
    lost = lost_pipe(0)
    group, core = pipe // CORES, pipe % CORES
    sibling = group * CORES + (1 - core)
    lost_group = lost // CORES
    tables = {}

    def now_of(at):
        return [jnp.where(at == lost, new(l), old(at, l)) for l in layers]

    def slots_of(sections):
        return [total(as_int(sections[k] == sections[l]) for k in range(l)) for l in layers]

    def layer_at(sections, slots, at, slot):
        hits = [both(sections[l] == at, slots[l] == slot) for l in layers]
        index = total(jnp.where(hits[l], l, 0) for l in layers)
        return index, total(as_int(hit) for hit in hits)

    def lookup(values, index):
        out = values[0]
        for l in layers[1:]:
            out = jnp.where(index == l, values[l], out)
        return out

    my_now = now_of(pipe)
    my_slot = slots_of(my_now)
    sib_now = now_of(sibling)
    sib_slot = slots_of(sib_now)
    new_list = [new(l) for l in layers]
    new_slot = slots_of(new_list)

    donor = [lost_pipe(offset(l)) for l in layers]
    source_section = [old(donor[l], l) for l in layers]
    source_slot = [
        total(as_int(old(donor[l], k) == source_section[l]) for k in range(l)) for l in layers
    ]
    source_group = [donor[l] // CORES for l in layers]
    crosses = [as_int(source_group[l] != lost_group) for l in layers]
    rank = [total(crosses[k] for k in range(l)) for l in layers]
    channel = [
        total(
            as_int(both(source_group[k] == source_group[l], source_section[k] == source_section[l]))
            for k in range(l)
        )
        for l in layers
    ]
    tables["branch"] = [[(lost_group, total(crosses))]]

    for first, parts, me in (("group", z.groups, group), ("section", z.sections, section)):

        def grad_unit(l, band):
            return [
                (as_int(my_now[l] == section), my_slot[l] * parts + band),
                (as_int(sib_now[l] == section), sib_slot[l] * parts + band),
            ]

        for shift in range(1, parts):
            band = lax.rem(me + shift, parts)
            tables["grad_out", first, shift] = [grad_unit(l, band) for l in layers]
        tables["grad_sum", first] = [
            grad_unit(l, me) + [(1, l)] * (parts - 1) for l in layers
        ]
        other = z.sections if first == "group" else z.groups
        tables["grad_mean", first] = [[(1, l)] * other for l in layers]
        for name, sections, slots in (("mine", my_now, my_slot), ("sibling", sib_now, sib_slot)):
            units = []
            for slot in range(z.slots):
                index, found = layer_at(sections, slots, section, slot)
                for band in range(parts):
                    unit = []
                    for shift in range(parts):
                        sender = lax.rem(me + parts - shift, parts)
                        unit.append((found * as_int(sender == band), index))
                    units.append(unit)
            tables[name, first] = units

    here = [as_int(source_group[l] == group) for l in layers]
    my_chip = [here[l] * as_int(source_section[l] == section) for l in layers]
    from_me = [as_int(donor[l] == pipe) for l in layers]

    for shift in range(1, z.sections):
        band = lax.rem(section + shift, z.sections)
        units = []
        for k in range(z.channels):
            hit = [my_chip[l] * as_int(channel[l] == k) for l in layers]
            slot = total(hit[l] * source_slot[l] for l in layers)
            mine = total(hit[l] * from_me[l] for l in layers)
            found = total(hit)
            index = slot * z.sections + band
            units.append([(mine, index), (found - mine, index)])
        tables["spread", shift] = units

    def held(l_my_chip, l_from_me, l_slot, l_here, l_channel, l_section):
        index = l_slot * z.sections + section
        unit = [(l_my_chip * l_from_me, index), (l_my_chip * (1 - l_from_me), index)]
        for shift in range(1, z.sections):
            sender = lax.rem(section + z.sections - shift, z.sections)
            unit.append((l_here * as_int(l_section == sender), l_channel))
        return unit

    def held_at(index):
        return held(
            *(
                lookup(values, index)
                for values in (my_chip, from_me, source_slot, here, channel, source_section)
            )
        )

    units = []
    for u in range(z.layers):
        hit = [crosses[l] * as_int(rank[l] == u) for l in layers]
        index = total(hit[l] * l for l in layers)
        found = total(hit)
        units.append([(flag * found, at) for flag, at in held_at(index)])
    tables["across"] = units

    def arrived(index, found):
        found = found * as_int(group == lost_group)
        unit = [(flag * found, at) for flag, at in held_at(index)]
        from_group = lookup(source_group, index)
        for shift in range(1, z.groups):
            sender = lax.rem(group + z.groups - shift, z.groups)
            unit.append((found * as_int(from_group == sender), lookup(rank, index)))
        return unit

    for shift in range(1, z.sections):
        target = lax.rem(section + shift, z.sections)
        tables["deliver", shift] = [
            arrived(*layer_at(new_list, new_slot, target, slot)) for slot in range(z.slots)
        ]
    units = []
    for slot in range(z.slots):
        own = arrived(*layer_at(new_list, new_slot, section, slot))
        for band in range(z.sections):
            mine = as_int(section == band)
            unit = [(flag * mine, at) for flag, at in own]
            for shift in range(1, z.sections):
                sender = lax.rem(section + z.sections - shift, z.sections)
                unit.append((as_int(both(sender == band, group == lost_group)), slot))
            units.append(unit)
    tables["collect"] = units

    last = [as_int(pipe == lost), core]
    for slot in range(z.slots):
        last.append(layer_at(my_now, my_slot, section, slot)[1])
    tables["update"] = [[tuple(last)]]
    return tables


def table_size(z):
    sources = z.sections + z.groups + z.sections + 2
    units = (z.sections + z.groups) * (4 * z.layers + 4 * z.slots)
    units += z.sections * (z.channels + 2 * z.slots) + z.layers
    return -(-(2 * units * sources + z.slots + 8) // 1024) * 1024


def make_plan(z, place, old_section, new_section, lost_pipe, donor_offset):
    starts = {}
    size = table_size(z)

    def kernel(place_ref, old_ref, new_ref, lost_ref, offset_ref, table_ref):
        tables = plan_tables(
            z,
            place_ref[0],
            place_ref[1],
            lambda at, l: old_ref[at, l],
            lambda l: new_ref[l],
            lambda rank: lost_ref[rank],
            lambda l: offset_ref[l],
        )
        at = 0
        for name, units in tables.items():
            starts[name] = at
            for unit in units:
                for entry in unit:
                    for value in entry:
                        table_ref[at] = jnp.int32(value)
                        at += 1
        assert at <= size

    smem = pl.BlockSpec(memory_space=pltpu.SMEM)
    table = pl.pallas_call(
        kernel,
        out_shape=jax.ShapeDtypeStruct((size,), jnp.int32),
        in_specs=[smem] * 5,
        out_specs=smem,
        name="plan",
    )(place, old_section, new_section, lost_pipe, donor_offset)
    return table, starts


SMEM_SPEC = pl.BlockSpec(memory_space=pltpu.SMEM)
VMEM_SPEC = pl.BlockSpec(memory_space=pltpu.VMEM)


def cost(operands, results):
    moved = sum(math.prod(a.shape) * a.dtype.itemsize for a in (*operands, *results))
    return pl.CostEstimate(flops=moved // 4, bytes_accessed=moved, transcendentals=0)


class Order:
    def __init__(self):
        self.last = []

    def specs(self):
        return [pl.BlockSpec(memory_space=pl.ANY)] * len(self.last)

    def then(self, result):
        self.last = [result[-1] if isinstance(result, (tuple, list)) else result]
        return result


def pack(z, order, table, start, units, sources, name):
    count = len(sources)
    arrays, _, rows, cols = sources[0].shape

    def kernel(table_ref, *refs):
        out_ref = refs[-1]
        for unit in range(units):
            for source, ref in enumerate(refs[:count]):
                at = start + (unit * count + source) * 2

                @pl.when(table_ref[at] != 0)
                def _(unit=unit, ref=ref, at=at):
                    out_ref[:, pl.ds(unit, 1)] = ref[:, pl.ds(table_ref[at + 1], 1)]

    out = jax.ShapeDtypeStruct((arrays, units, rows, cols), jnp.bfloat16)
    call = pl.pallas_call(
        kernel,
        out_shape=out,
        in_specs=[SMEM_SPEC] + [VMEM_SPEC] * count + order.specs(),
        out_specs=VMEM_SPEC,
        compiler_params=pltpu.CompilerParams(vmem_limit_bytes=VMEM),
        cost_estimate=cost([out], [out]),
        name=name,
    )
    return order.then(call(table, *sources, *order.last))


def add_up(z, order, table, start, units, sources, name):
    count = len(sources)
    _, rows, cols = sources[0].shape

    def kernel(table_ref, *refs):
        out_ref = refs[-1]
        for unit in range(units):
            out = jnp.zeros((rows, cols), jnp.float32)
            for source, ref in enumerate(refs[:count]):
                at = start + (unit * count + source) * 2
                block = ref[table_ref[at + 1]].astype(jnp.float32)
                out = out + jnp.where(table_ref[at] != 0, block, 0.0)
            out_ref[unit] = out.astype(out_ref.dtype)

    out = jax.ShapeDtypeStruct((units, rows, cols), jnp.bfloat16)
    call = pl.pallas_call(
        kernel,
        out_shape=out,
        in_specs=[SMEM_SPEC] + [VMEM_SPEC] * count + order.specs(),
        out_specs=VMEM_SPEC,
        compiler_params=pltpu.CompilerParams(vmem_limit_bytes=VMEM),
        cost_estimate=cost([out] * 2, [out]),
        name=name,
    )
    return order.then(call(table, *sources, *order.last))


def halve(z, order, place, arrays, chunk, chunks, name):
    sub = z.band // chunks
    count = len(arrays)
    views = [a.reshape(z.slots, CORES, z.sections, chunks, sub, z.cols) for a in arrays]

    def kernel(place_ref, *refs):
        own_refs, their_refs = refs[:count], refs[count : 2 * count]
        own_out, their_out = refs[-2:]
        for at in range(count):
            own_out[at] = own_refs[at][:, 0, :, 0].astype(jnp.bfloat16)
            their_out[at] = their_refs[at][:, 0, :, 0].astype(jnp.bfloat16)

    def spec(own):
        def index_map(step, place_ref):
            core = lax.rem(place_ref[0], CORES)
            return (0, core if own else 1 - core, 0, chunk, 0, 0)

        return pl.BlockSpec((z.slots, 1, z.sections, 1, sub, z.cols), index_map)

    shape = (count, z.slots, z.sections, sub, z.cols)
    out = jax.ShapeDtypeStruct(shape, jnp.bfloat16)
    out_spec = pl.BlockSpec(shape, lambda step, place_ref: (0, 0, 0, 0, 0))
    call = pl.pallas_call(
        kernel,
        grid_spec=pltpu.PrefetchScalarGridSpec(
            num_scalar_prefetch=1,
            grid=(1,),
            in_specs=[spec(True)] * count + [spec(False)] * count + order.specs(),
            out_specs=[out_spec] * 2,
        ),
        out_shape=(out, out),
        compiler_params=pltpu.CompilerParams(vmem_limit_bytes=VMEM),
        cost_estimate=cost([out] * 4, [out] * 2),
        name=name,
    )
    return order.then(call(place, *views, *views, *order.last))


def update(z, order, table, start, chunk, state, rebuilt, mean, outs):
    views = [a.reshape(z.slots, CORES, z.sections, z.chunks, z.sub, z.cols) for a in state]
    rebuilt = [a.reshape(3, z.slots, z.sections, z.sub, z.cols) for a in rebuilt]
    mean = [a.reshape(z.slots, z.sections, z.chunks, z.sub, z.cols) for a in mean]
    outs = [] if outs is None else list(outs)

    def kernel(table_ref, *refs):
        local_refs, lost_refs, mean_refs = refs[:3], refs[3:5], refs[5:7]
        out_w, out_one, out_two = refs[-3:]
        slot = pl.program_id(0)
        is_lost = table_ref[start] != 0
        core = table_ref[start + 1]
        found = table_ref[start + 2 + slot] != 0

        def step(half, band, weight, one, two, grad):
            grad = grad.astype(jnp.float32) * (1.0 / z.pipes)
            weight = weight.astype(jnp.float32)
            next_one = BETA_ONE * one.astype(jnp.float32) + (1.0 - BETA_ONE) * grad
            next_two = BETA_TWO * two.astype(jnp.float32) + (1.0 - BETA_TWO) * grad * grad
            move = next_one / (jnp.sqrt(next_two) + EPSILON) + DECAY_RATE * weight
            out_w[0, half, band, 0] = (weight - LEARN_RATE * move).astype(out_w.dtype)
            out_one[0, half, band, 0] = next_one
            out_two[0, half, band, 0] = next_two

        for half in range(CORES):
            for source in range(2):
                mine = both(found, (core == half) == (source == 0))

                @pl.when(both(mine, is_lost))
                def _(half=half, source=source):
                    for band in range(z.sections):
                        ref = lost_refs[source]
                        step(
                            half, band, ref[0, 0, band], ref[1, 0, band], ref[2, 0, band],
                            mean_refs[source][0, band, 0],
                        )

                @pl.when(both(mine, jnp.logical_not(is_lost)))
                def _(half=half, source=source):
                    for band in range(z.sections):
                        step(
                            half, band, *(ref[0, half, band, 0] for ref in local_refs),
                            mean_refs[source][0, band, 0],
                        )

        @pl.when(jnp.logical_not(found))
        def _():
            for ref in (out_w, out_one, out_two):
                ref[...] = jnp.zeros(ref.shape, ref.dtype)

    def local(slot, table_ref):
        return (slot * (1 - table_ref[start]), 0, 0, chunk, 0, 0)

    def lost(slot, table_ref):
        return (0, slot * table_ref[start], 0, 0, 0)

    state_block = (1, CORES, z.sections, 1, z.sub, z.cols)
    state_spec = pl.BlockSpec(state_block, local)
    lost_spec = pl.BlockSpec((3, 1, z.sections, z.sub, z.cols), lost)
    mean_spec = pl.BlockSpec(
        (1, z.sections, 1, z.sub, z.cols), lambda slot, table_ref: (slot, 0, chunk, 0, 0)
    )
    out_spec = pl.BlockSpec(state_block, lambda slot, table_ref: (slot, 0, 0, chunk, 0, 0))
    shape = views[0].shape
    elements = z.slots * z.rows * z.cols // z.chunks
    call = pl.pallas_call(
        kernel,
        grid_spec=pltpu.PrefetchScalarGridSpec(
            num_scalar_prefetch=1,
            grid=(z.slots,),
            in_specs=[state_spec] * 3
            + [lost_spec] * 2
            + [mean_spec] * 2
            + [pl.BlockSpec(memory_space=pl.ANY)] * len(outs)
            + order.specs(),
            out_specs=[out_spec] * 3,
        ),
        out_shape=(
            jax.ShapeDtypeStruct(shape, jnp.bfloat16),
            jax.ShapeDtypeStruct(shape, jnp.float32),
            jax.ShapeDtypeStruct(shape, jnp.float32),
        ),
        input_output_aliases={8 + at: at for at in range(len(outs))},
        compiler_params=pltpu.CompilerParams(vmem_limit_bytes=VMEM),
        cost_estimate=pl.CostEstimate(
            flops=elements * 14, bytes_accessed=elements * 22, transcendentals=elements * 2
        ),
        name="update",
    )
    return call(table, *views, *rebuilt, *mean, *outs, *order.last)


class Gradients:
    def __init__(self, z, order, table, starts, first, pair):
        self.z, self.order, self.table, self.starts, self.first = z, order, table, starts, first
        if first == "group":
            self.parts, self.other = z.groups, z.sections
            self.send_first, self.send_other = z.to_group, z.to_section
        else:
            self.parts, self.other = z.sections, z.groups
            self.send_first, self.send_other = z.to_section, z.to_group
        rows = z.half // self.parts
        self.held = [a.reshape(z.slots * self.parts, rows, z.cols) for a in pair]

    def summed(self, name, sources):
        return add_up(
            self.z, self.order, self.table, self.starts[name], self.z.layers, sources, name[0]
        )

    def scatter(self):
        self.arrived = []
        for shift in range(1, self.parts):
            part = self.summed(("grad_out", self.first, shift), self.held)
            self.arrived.append(self.send_first(part, shift))

    def exchange(self):
        part = self.summed(("grad_sum", self.first), self.held + self.arrived)
        self.whole = [part] + [self.send_other(part, shift) for shift in range(1, self.other)]

    def gather(self):
        whole = self.summed(("grad_mean", self.first), self.whole)
        bands = [whole] + [self.send_first(whole, shift) for shift in range(1, self.parts)]
        self.bands = [band[None] for band in bands]

    def finish(self):
        z = self.z
        theirs, mine = (
            pack(
                z,
                self.order,
                self.table,
                self.starts[name, self.first],
                z.slots * self.parts,
                self.bands,
                name + "_mean",
            )
            for name in ("sibling", "mine")
        )
        return mine, z.to_core(theirs)


class Donated:
    def __init__(self, z, order, table, starts, pair):
        self.z, self.order, self.table, self.starts = z, order, table, starts
        self.held = [a.reshape(3, z.slots * z.sections, z.sub, z.cols) for a in pair]

    def packed(self, name, units, sources):
        label = name if isinstance(name, str) else name[0]
        return pack(self.z, self.order, self.table, self.starts[name], units, sources, label)

    def spread(self):
        z = self.z
        own = self.held[:2]
        for shift in range(1, z.sections):
            sent = self.packed(("spread", shift), z.channels, own)
            self.held.append(z.to_section(sent, shift))

    def across(self):
        crossed = self.packed("across", self.z.layers, self.held)
        for shift in range(1, self.z.groups):
            self.held.append(self.z.to_group(crossed, shift))

    def deliver(self):
        z = self.z
        arrived = []
        for shift in range(1, z.sections):
            sent = self.packed(("deliver", shift), z.slots, self.held)
            arrived.append(z.to_section(sent, shift))
        self.held = self.held + arrived

    def collect(self):
        z = self.z
        half = self.packed("collect", z.slots * z.sections, self.held)
        self.rebuilt = (half, z.to_core(half))


def per_device(
    weights,
    first_moment,
    second_moment,
    gradients,
    old_section,
    new_section,
    lost_pipe,
    donor_offset,
):
    z = Sizes(weights, new_section)
    order = Order()
    place = jnp.stack([lax.axis_index("pipe"), lax.axis_index("section")]).astype(jnp.int32)
    state = (weights[0, 0], first_moment[0, 0], second_moment[0, 0])

    def swap(arrays, chunk, chunks, name):
        own, theirs = halve(z, order, place, arrays, chunk, chunks, name)
        return own, z.to_core(theirs)

    pair = swap((gradients[0, 0],), 0, 1, "halve_gradients")
    chunk_pairs = [swap(state, 0, z.chunks, "halve_state")]
    table, starts = make_plan(z, place, old_section, new_section, lost_pipe, donor_offset)

    grads = Gradients(z, order, table, starts, "group", pair)
    grads.scatter()
    parts = []

    def spread(chunk):
        if chunk >= len(chunk_pairs):
            chunk_pairs.append(swap(state, chunk, z.chunks, "halve_state"))
        parts.append(Donated(z, order, table, starts, chunk_pairs[chunk]))
        parts[chunk].spread()

    early = min(2, z.chunks)
    for chunk in range(early):
        spread(chunk)
    while len(chunk_pairs) < z.chunks:
        chunk_pairs.append(swap(state, len(chunk_pairs), z.chunks, "halve_state"))
    parts[0].across()
    grads.exchange()
    for chunk in range(1, early):
        parts[chunk].across()
    grads.gather()
    for chunk in range(early, z.chunks):
        spread(chunk)
    delivered = 0
    for chunk in range(early, z.chunks):
        parts[delivered].deliver()
        delivered += 1
        parts[chunk].across()
    mean = grads.finish()
    outs = None
    for chunk in range(z.chunks):
        while delivered < min(chunk + early, z.chunks):
            parts[delivered].deliver()
            delivered += 1
        parts[chunk].collect()
        if chunk:
            outs = advance(z, order, table, starts, chunk - 1, state, parts, mean, outs)
    outs = advance(z, order, table, starts, z.chunks - 1, state, parts, mean, outs)
    return tuple(out.reshape((1, 1, z.slots, z.rows, z.cols)) for out in outs)


def advance(z, order, table, starts, chunk, state, parts, mean, outs):
    rebuilt = parts[chunk].rebuilt
    return update(z, order, table, starts["update"], chunk, state, rebuilt, mean, outs)


def solution(mesh):
    split = P("pipe", "section", None, "tp", None)
    return jax.shard_map(
        per_device,
        mesh=mesh,
        in_specs=(split,) * 4 + (P(),) * 4,
        out_specs=(split,) * 3,
        check_vma=False,
    )
```

```python
import jax
import jax.numpy as jnp
from jax import lax
from jax.experimental import pallas as pl
from jax.experimental.pallas import tpu as pltpu
from jax.sharding import PartitionSpec as P

LEARN_RATE = 0.01
BETA_ONE = 0.9
BETA_TWO = 0.95
EPSILON = 1e-08
DECAY_RATE = 0.1

CORES = 2
CHUNKS = (3, 3, 2)
SEQUENCE = (
    *("ge", "e0", "gs", "s0", "e1", "s1", "a0", "gx", "a1", "e2", "gg", "s2"),
    *("d0", "a2", "d1", "gf", "c0", "u0", "c1", "d2", "u1", "c2", "u2"),
)
VMEM = 24 * 1024 * 1024
AXES = ("pipe", "section")


def both(*terms):
    out = terms[0]
    for term in terms[1:]:
        out = jnp.logical_and(out, term)
    return out


def as_int(flag):
    return jnp.where(flag, 1, 0).astype(jnp.int32)


def total(terms):
    out = jnp.int32(0)
    for term in terms:
        out = out + term
    return out


class Sizes:
    def __init__(self, weights, new_section):
        self.pipes = lax.axis_size("pipe")
        self.sections = lax.axis_size("section")
        self.groups = self.pipes // CORES
        self.slots = weights.shape[2]
        self.rows = weights.shape[3]
        self.cols = weights.shape[4]
        self.layers = new_section.shape[0]
        self.half = self.rows // CORES
        self.band = self.half // self.sections
        units = sum(CHUNKS)
        self.chunks = CHUNKS if self.band % (16 * units) == 0 else (1,)
        self.units = sum(self.chunks)
        self.unit = self.band // self.units
        self.grad_band = self.half // self.groups
        doubles = self.layers - self.sections
        widest = 0
        for at in range(self.sections):
            low = at + max(0, doubles - (self.sections - at))
            high = min(self.layers - self.sections + at, at + min(at, doubles) + 1)
            widest = max(widest, high - low + 1)
        self.channels = min(widest, CORES * self.slots)

    def send(self, value, target):
        pairs = []
        for pipe in range(self.pipes):
            for section in range(self.sections):
                group_to, core, to = target(pipe // CORES, pipe % CORES, section)
                pipe_to = group_to * CORES + core
                pairs.append((pipe * self.sections + section, pipe_to * self.sections + to))
        return lax.ppermute(value, AXES, pairs)

    def to_core(self, value):
        return self.send(value, lambda g, c, s: (g, 1 - c, s))

    def to_group(self, value, shift):
        return self.send(value, lambda g, c, s: ((g + shift) % self.groups, c, s))

    def to_section(self, value, shift):
        return self.send(value, lambda g, c, s: (g, c, (s + shift) % self.sections))


def plan_tables(z, pipe, section, old, new, lost_pipe, offset):
    layers = range(z.layers)
    lost = lost_pipe(0)
    group, core = pipe // CORES, pipe % CORES
    sibling = group * CORES + (1 - core)
    lost_group = lost // CORES
    tables = {}

    def now_of(at):
        return [jnp.where(at == lost, new(l), old(at, l)) for l in layers]

    def slots_of(sections):
        return [total(as_int(sections[k] == sections[l]) for k in range(l)) for l in layers]

    def layer_at(sections, slots, at, slot):
        hits = [both(sections[l] == at, slots[l] == slot) for l in layers]
        index = total(jnp.where(hits[l], l, 0) for l in layers)
        return index, total(as_int(hit) for hit in hits)

    def lookup(values, index):
        out = values[0]
        for l in layers[1:]:
            out = jnp.where(index == l, values[l], out)
        return out

    my_now = now_of(pipe)
    my_slot = slots_of(my_now)
    sib_now = now_of(sibling)
    sib_slot = slots_of(sib_now)
    new_list = [new(l) for l in layers]
    new_slot = slots_of(new_list)

    donor = [lost_pipe(offset(l)) for l in layers]
    source_section = [old(donor[l], l) for l in layers]
    source_slot = [
        total(as_int(old(donor[l], k) == source_section[l]) for k in range(l)) for l in layers
    ]
    source_group = [donor[l] // CORES for l in layers]
    crosses = [as_int(source_group[l] != lost_group) for l in layers]
    rank = [total(crosses[k] for k in range(l)) for l in layers]
    channel = [
        total(
            as_int(both(source_group[k] == source_group[l], source_section[k] == source_section[l]))
            for k in range(l)
        )
        for l in layers
    ]

    def grad_unit(l, band):
        return [
            (as_int(my_now[l] == section), my_slot[l] * z.groups + band),
            (as_int(sib_now[l] == section), sib_slot[l] * z.groups + band),
        ]

    for shift in range(1, z.groups):
        band = lax.rem(group + shift, z.groups)
        tables["grad_out", shift] = [grad_unit(l, band) for l in layers]
    tables["grad_sum"] = [grad_unit(l, group) + [(1, l)] * (z.groups - 1) for l in layers]
    tables["grad_mean"] = [[(1, l)] * z.sections for l in layers]
    for name, sections, slots in (("mine", my_now, my_slot), ("sibling", sib_now, sib_slot)):
        units = []
        for slot in range(z.slots):
            index, found = layer_at(sections, slots, section, slot)
            for band in range(z.groups):
                unit = []
                for shift in range(z.groups):
                    sender = lax.rem(group + z.groups - shift, z.groups)
                    unit.append((found * as_int(sender == band), index))
                units.append(unit)
        tables[name] = units

    here = [as_int(source_group[l] == group) for l in layers]
    my_chip = [here[l] * as_int(source_section[l] == section) for l in layers]
    from_me = [as_int(donor[l] == pipe) for l in layers]

    for shift in range(1, z.sections):
        band = lax.rem(section + shift, z.sections)
        units = []
        for k in range(z.channels):
            hit = [my_chip[l] * as_int(channel[l] == k) for l in layers]
            slot = total(hit[l] * source_slot[l] for l in layers)
            mine = total(hit[l] * from_me[l] for l in layers)
            found = total(hit)
            index = slot * z.sections + band
            units.append([(mine, index), (found - mine, index)])
        tables["spread", shift] = units

    def held(l_my_chip, l_from_me, l_slot, l_here, l_channel, l_section):
        index = l_slot * z.sections + section
        unit = [(l_my_chip * l_from_me, index), (l_my_chip * (1 - l_from_me), index)]
        for shift in range(1, z.sections):
            sender = lax.rem(section + z.sections - shift, z.sections)
            unit.append((l_here * as_int(l_section == sender), l_channel))
        return unit

    def held_at(index):
        return held(
            *(
                lookup(values, index)
                for values in (my_chip, from_me, source_slot, here, channel, source_section)
            )
        )

    units = []
    for u in range(z.layers):
        hit = [crosses[l] * as_int(rank[l] == u) for l in layers]
        index = total(hit[l] * l for l in layers)
        found = total(hit)
        units.append([(flag * found, at) for flag, at in held_at(index)])
    tables["across"] = units

    def arrived(index, found):
        found = found * as_int(group == lost_group)
        unit = [(flag * found, at) for flag, at in held_at(index)]
        from_group = lookup(source_group, index)
        for shift in range(1, z.groups):
            sender = lax.rem(group + z.groups - shift, z.groups)
            unit.append((found * as_int(from_group == sender), lookup(rank, index)))
        return unit

    for shift in range(1, z.sections):
        target = lax.rem(section + shift, z.sections)
        tables["deliver", shift] = [
            arrived(*layer_at(new_list, new_slot, target, slot)) for slot in range(z.slots)
        ]
    units = []
    for slot in range(z.slots):
        own = arrived(*layer_at(new_list, new_slot, section, slot))
        for band in range(z.sections):
            mine = as_int(section == band)
            unit = [(flag * mine, at) for flag, at in own]
            for shift in range(1, z.sections):
                sender = lax.rem(section + z.sections - shift, z.sections)
                unit.append((as_int(both(sender == band, group == lost_group)), slot))
            units.append(unit)
    tables["collect"] = units

    last = [as_int(pipe == lost), core]
    for slot in range(z.slots):
        last.append(layer_at(my_now, my_slot, section, slot)[1])
    tables["update"] = [[tuple(last)]]
    return tables


def table_size(z):
    sources = z.sections + z.groups + z.sections + 2
    units = (z.sections + z.groups) * (4 * z.layers + 4 * z.slots)
    units += z.sections * (z.channels + 2 * z.slots) + z.layers
    return -(-(2 * units * sources + z.slots + 8) // 1024) * 1024


def make_plan(z, place, old_section, new_section, lost_pipe, donor_offset):
    starts = {}
    size = table_size(z)
    smem = pl.BlockSpec(memory_space=pltpu.SMEM)

    def kernel(place_ref, old_ref, new_ref, lost_ref, offset_ref, table_ref):
        tables = plan_tables(
            z,
            place_ref[0],
            place_ref[1],
            lambda at, l: old_ref[at, l],
            lambda l: new_ref[l],
            lambda rank: lost_ref[rank],
            lambda l: offset_ref[l],
        )
        at = 0
        for name, units in tables.items():
            starts[name] = at
            for unit in units:
                for entry in unit:
                    for value in entry:
                        table_ref[at] = jnp.int32(value)
                        at += 1
        assert at <= size

    table = pl.pallas_call(
        kernel,
        out_shape=jax.ShapeDtypeStruct((size,), jnp.int32),
        in_specs=[smem] * 5,
        out_specs=smem,
        name="plan",
    )(place, old_section, new_section, lost_pipe, donor_offset)
    return table, starts


SMEM_SPEC = pl.BlockSpec(memory_space=pltpu.SMEM)
VMEM_SPEC = pl.BlockSpec(memory_space=pltpu.VMEM)


def cost(operands, results):
    moved = sum(math.prod(a.shape) * a.dtype.itemsize for a in (*operands, *results))
    return pl.CostEstimate(flops=moved // 4, bytes_accessed=moved, transcendentals=0)


class Order:
    def __init__(self):
        self.last = []

    def specs(self):
        return [pl.BlockSpec(memory_space=pl.ANY)] * len(self.last)

    def then(self, result):
        self.last = [result[0]]
        return result


SMEM_SPEC = pl.BlockSpec(memory_space=pltpu.SMEM)
VMEM_SPEC = pl.BlockSpec(memory_space=pltpu.VMEM)
PARAMS = pltpu.CompilerParams(vmem_limit_bytes=VMEM)
COST = pl.CostEstimate(flops=1, bytes_accessed=1, transcendentals=0)


class Rows:
    def __init__(self, value, rows, count, arrays=1, base=0):
        self.value, self.rows, self.count = value, rows, count
        self.arrays, self.base = arrays, base

    def block(self, array, index):
        at = self.base + (array * self.count + index) * self.rows
        return pl.ds(at if isinstance(at, int) else pl.multiple_of(at, 16), self.rows)


class Copy:
    def __init__(self, start, units, sources):
        self.start, self.units, self.sources = start, units, sources
        self.arrays, self.rows = sources[0].arrays, sources[0].rows

    def write(self, table_ref, refs, out_ref, out):
        for unit in range(self.units):
            for at, source in enumerate(self.sources):
                entry = self.start + (unit * len(self.sources) + at) * 2

                @pl.when(table_ref[entry] != 0)
                def _(unit=unit, source=source, ref=refs[at], entry=entry):
                    index = table_ref[entry + 1]
                    for array in range(self.arrays):
                        out_ref[out.block(array, unit)] = ref[source.block(array, index)]


class Sum:
    def __init__(self, start, units, sources):
        self.start, self.units, self.sources = start, units, sources
        self.arrays, self.rows = 1, sources[0].rows

    def write(self, table_ref, refs, out_ref, out):
        for unit in range(self.units):
            total_here = None
            for at, source in enumerate(self.sources):
                entry = self.start + (unit * len(self.sources) + at) * 2
                block = refs[at][source.block(0, table_ref[entry + 1])].astype(jnp.float32)
                block = jnp.where(table_ref[entry] != 0, block, 0.0)
                total_here = block if total_here is None else total_here + block
            out_ref[out.block(0, unit)] = total_here.astype(out_ref.dtype)


def stage(z, order, table, outputs, name):
    operands, slots = [], {}
    for job in (job for jobs in outputs for job in jobs):
        for source in job.sources:
            if id(source.value) not in slots:
                slots[id(source.value)] = len(operands)
                operands.append(source.value)
    places, shapes = [], []
    for jobs in outputs:
        at, row = [], 0
        for job in jobs:
            at.append(Rows(None, job.rows, job.units, job.arrays, row))
            row += job.arrays * job.units * job.rows
        places.append(at)
        shapes.append(jax.ShapeDtypeStruct((row, z.cols), jnp.bfloat16))

    def kernel(table_ref, *refs):
        out_refs = refs[-len(outputs) :]
        for jobs, at, out_ref in zip(outputs, places, out_refs):
            for job, place in zip(jobs, at):
                inputs = [refs[slots[id(source.value)]] for source in job.sources]
                job.write(table_ref, inputs, out_ref, place)

    call = pl.pallas_call(
        kernel,
        out_shape=tuple(shapes),
        in_specs=[SMEM_SPEC] + [VMEM_SPEC] * len(operands) + order.specs(),
        out_specs=tuple([VMEM_SPEC] * len(outputs)),
        compiler_params=PARAMS,
        cost_estimate=COST,
        name=name,
    )
    return order.then(call(table, *operands, *order.last))


def halve(z, order, place, arrays, first, count, units):
    unit = z.band // units
    views = [a.reshape(z.slots, CORES, z.sections, units, unit, z.cols) for a in arrays]

    def kernel(place_ref, *refs):
        for part, out_ref in enumerate(refs[-2:]):
            row = 0
            for at in range(len(arrays)):
                ref = refs[part * len(arrays) + at]
                for slot in range(z.slots):
                    for band in range(z.sections):
                        for k in range(count):
                            out_ref[pl.ds(row, unit)] = ref[slot, 0, band, k].astype(jnp.bfloat16)
                            row += unit

    def spec(own):
        def index_map(step, place_ref):
            core = lax.rem(place_ref[0], CORES)
            return (0, core if own else 1 - core, 0, first // count, 0, 0)

        return pl.BlockSpec((z.slots, 1, z.sections, count, unit, z.cols), index_map)

    rows = len(arrays) * z.slots * z.sections * count * unit
    out = jax.ShapeDtypeStruct((rows, z.cols), jnp.bfloat16)
    out_spec = pl.BlockSpec(out.shape, lambda step, place_ref: (0, 0))
    call = pl.pallas_call(
        kernel,
        grid_spec=pltpu.PrefetchScalarGridSpec(
            num_scalar_prefetch=1,
            grid=(1,),
            in_specs=[spec(True)] * len(arrays) + [spec(False)] * len(arrays) + order.specs(),
            out_specs=[out_spec] * 2,
        ),
        out_shape=(out, out),
        compiler_params=PARAMS,
        cost_estimate=COST,
        name="halve_state" if len(arrays) > 1 else "halve_gradients",
    )
    return order.then(call(place, *views, *views, *order.last))


def update(z, order, table, start, first, count, state, halves, mean, outs):
    sub = count * z.unit
    per_slot = z.sections * sub
    views = [a.reshape(z.slots, CORES, z.sections, z.units, z.unit, z.cols) for a in state]
    outs = [] if outs is None else list(outs)

    def kernel(table_ref, *refs):
        local_refs, half_refs, mean_refs = refs[:3], refs[3:5], refs[5:7]
        out_w, out_one, out_two = refs[-3:]
        slot = pl.program_id(0)
        is_lost = table_ref[start] != 0
        core = table_ref[start + 1]
        found = table_ref[start + 2 + slot] != 0

        def step(half, band, unit, weight, one, two, grad):
            grad = grad.astype(jnp.float32) * (1.0 / z.pipes)
            weight = weight.astype(jnp.float32)
            next_one = BETA_ONE * one.astype(jnp.float32) + (1.0 - BETA_ONE) * grad
            next_two = BETA_TWO * two.astype(jnp.float32) + (1.0 - BETA_TWO) * grad * grad
            move = next_one / (jnp.sqrt(next_two) + EPSILON) + DECAY_RATE * weight
            out_w[0, half, band, unit] = (weight - LEARN_RATE * move).astype(out_w.dtype)
            out_one[0, half, band, unit] = next_one
            out_two[0, half, band, unit] = next_two

        def each(half, source, lost):
            for band in range(z.sections):
                for unit in range(count):
                    row = slot * per_slot + band * sub + unit * z.unit

                    def rows(at):
                        return pl.ds(pl.multiple_of(at, 16), z.unit)

                    mean_row = slot * z.half + band * z.band + (first + unit) * z.unit
                    grad = mean_refs[source][rows(mean_row)]
                    if lost:
                        ref = half_refs[source]
                        old = [ref[rows(a * z.slots * per_slot + row)] for a in range(3)]
                    else:
                        old = [ref[0, half, band, unit] for ref in local_refs]
                    step(half, band, unit, *old, grad)

        for half in range(CORES):
            for source in range(2):
                mine = both(found, (core == half) == (source == 0))

                @pl.when(both(mine, is_lost))
                def _(half=half, source=source):
                    each(half, source, True)

                @pl.when(both(mine, jnp.logical_not(is_lost)))
                def _(half=half, source=source):
                    each(half, source, False)

        @pl.when(jnp.logical_not(found))
        def _():
            for ref in (out_w, out_one, out_two):
                ref[...] = jnp.zeros(ref.shape, ref.dtype)

    def local(slot, table_ref):
        return (slot * (1 - table_ref[start]), 0, 0, first // count, 0, 0)

    block = (1, CORES, z.sections, count, z.unit, z.cols)
    out_spec = pl.BlockSpec(block, lambda slot, table_ref: (slot, 0, 0, first // count, 0, 0))
    shape = views[0].shape
    call = pl.pallas_call(
        kernel,
        grid_spec=pltpu.PrefetchScalarGridSpec(
            num_scalar_prefetch=1,
            grid=(z.slots,),
            in_specs=[pl.BlockSpec(block, local)] * 3
            + [VMEM_SPEC] * 4
            + [pl.BlockSpec(memory_space=pl.ANY)] * len(outs)
            + order.specs(),
            out_specs=[out_spec] * 3,
        ),
        out_shape=(
            jax.ShapeDtypeStruct(shape, jnp.bfloat16),
            jax.ShapeDtypeStruct(shape, jnp.float32),
            jax.ShapeDtypeStruct(shape, jnp.float32),
        ),
        input_output_aliases={8 + at: at for at in range(len(outs))},
        compiler_params=PARAMS,
        cost_estimate=COST,
        name="update",
    )
    return order.then(call(table, *views, *halves, *mean, *outs, *order.last))


class Gradients:
    def __init__(self, z, order, grads):
        self.z, self.order, self.grads = z, order, grads

    def run(self, outputs, name):
        return stage(self.z, self.order, self.table, outputs, name)

    def rows(self, value):
        return Rows(value, self.z.grad_band, self.z.layers)

    def enter(self, place):
        z = self.z
        own, theirs = halve(z, self.order, place, (self.grads,), 0, 1, 1)
        self.held = [
            Rows(flat, z.grad_band, z.slots * z.groups) for flat in (own, z.to_core(theirs))
        ]

    def scatter(self):
        z = self.z
        shifts = range(1, z.groups)
        jobs = [[Sum(self.starts["grad_out", s], z.layers, self.held)] for s in shifts]
        parts = self.run(jobs, "grad_out")
        self.held += [self.rows(z.to_group(part, s)) for s, part in zip(shifts, parts)]

    def exchange(self):
        z = self.z
        (part,) = self.run([[Sum(self.starts["grad_sum"], z.layers, self.held)]], "grad_sum")
        others = [z.to_section(part, s) for s in range(1, z.sections)]
        self.held = [self.rows(value) for value in (part, *others)]

    def gather(self):
        z = self.z
        (part,) = self.run([[Sum(self.starts["grad_mean"], z.layers, self.held)]], "grad_mean")
        others = [z.to_group(part, s) for s in range(1, z.groups)]
        self.held = [self.rows(value) for value in (part, *others)]

    def finish(self):
        z = self.z
        theirs, mine = self.run(
            [
                [Copy(self.starts[name], z.slots * z.groups, self.held)]
                for name in ("sibling", "mine")
            ],
            "mean",
        )
        self.mean = (mine, z.to_core(theirs))


class Chunk:
    def __init__(self, z, order, state, first, count):
        self.z, self.order, self.state = z, order, state
        self.first, self.count, self.sub = first, count, count * z.unit

    def run(self, outputs, name):
        return stage(self.z, self.order, self.table, outputs, name)

    def enter(self, place):
        z = self.z
        own, theirs = halve(z, self.order, place, self.state, self.first, self.count, z.units)
        held = z.slots * z.sections
        self.held = [Rows(flat, self.sub, held, 3) for flat in (own, z.to_core(theirs))]

    def spread(self):
        z = self.z
        shifts = range(1, z.sections)
        jobs = [[Copy(self.starts["spread", s], z.channels, self.held)] for s in shifts]
        parts = self.run(jobs, "spread")
        for s, part in zip(shifts, parts):
            self.held.append(Rows(z.to_section(part, s), self.sub, z.channels, 3))

    def across(self):
        z = self.z
        (part,) = self.run([[Copy(self.starts["across"], z.layers, self.held)]], "across")
        for s in range(1, z.groups):
            self.held.append(Rows(z.to_group(part, s), self.sub, z.layers, 3))

    def deliver(self):
        z = self.z
        shifts = range(1, z.sections)
        jobs = [[Copy(self.starts["deliver", s], z.slots, self.held)] for s in shifts]
        parts = self.run(jobs, "deliver")
        for s, part in zip(shifts, parts):
            self.held.append(Rows(z.to_section(part, s), self.sub, z.slots, 3))

    def collect(self):
        z = self.z
        units = z.slots * z.sections
        (half,) = self.run([[Copy(self.starts["collect"], units, self.held)]], "collect")
        self.halves = (half, z.to_core(half))

    def advance(self, mean, outs):
        return update(
            self.z,
            self.order,
            self.table,
            self.starts["update"],
            self.first,
            self.count,
            self.state,
            self.halves,
            mean,
            outs,
        )


def per_device(
    weights,
    first_moment,
    second_moment,
    gradients,
    old_section,
    new_section,
    lost_pipe,
    donor_offset,
):
    z = Sizes(weights, new_section)
    order = Order()
    place = jnp.stack([lax.axis_index("pipe"), lax.axis_index("section")]).astype(jnp.int32)
    state = (weights[0, 0], first_moment[0, 0], second_moment[0, 0])
    grads = Gradients(z, order, gradients[0, 0])
    chunks = [
        Chunk(z, order, state, sum(z.chunks[:at]), count) for at, count in enumerate(z.chunks)
    ]
    table, starts = make_plan(z, place, old_section, new_section, lost_pipe, donor_offset)
    for part in (grads, *chunks):
        part.table, part.starts = table, starts

    outs = None
    for name in SEQUENCE:
        if name[0] == "g":
            part = grads
        elif int(name[1]) < len(chunks):
            part = chunks[int(name[1])]
        else:
            continue
        if name in ("ge", "gs", "gx", "gg", "gf"):
            step = dict(e="enter", s="scatter", x="exchange", g="gather", f="finish")[name[1]]
        else:
            step = dict(e="enter", s="spread", a="across", d="deliver", c="collect", u="")[name[0]]
        if step == "enter":
            part.enter(place)
        elif step:
            getattr(part, step)()
        else:
            outs = part.advance(grads.mean, outs)
    return tuple(out.reshape((1, 1, z.slots, z.rows, z.cols)) for out in outs)


def solution(mesh):
    split = P("pipe", "section", None, "tp", None)
    return jax.shard_map(
        per_device,
        mesh=mesh,
        in_specs=(split,) * 4 + (P(),) * 4,
        out_specs=(split,) * 3,
        check_vma=False,
    )
```

```python
import math

import jax
import jax.numpy as jnp
from jax import lax
from jax.experimental import pallas as pl
from jax.experimental.pallas import tpu as pltpu
from jax.sharding import PartitionSpec as P

LEARN_RATE = 0.01
BETA_ONE = 0.9
BETA_TWO = 0.95
EPSILON = 1e-08
DECAY_RATE = 0.1

CORES = 2
CHUNKS = 1
AFTER = {}
VMEM = 40 * 1024 * 1024
AXES = ("pipe", "section")


def both(*terms):
    out = terms[0]
    for term in terms[1:]:
        out = jnp.logical_and(out, term)
    return out


def as_int(flag):
    return jnp.where(flag, 1, 0).astype(jnp.int32)


def total(terms):
    out = jnp.int32(0)
    for term in terms:
        out = out + term
    return out


class Sizes:
    def __init__(self, weights, new_section):
        self.pipes = lax.axis_size("pipe")
        self.sections = lax.axis_size("section")
        self.groups = self.pipes // CORES
        self.slots = weights.shape[2]
        self.rows = weights.shape[3]
        self.cols = weights.shape[4]
        self.layers = new_section.shape[0]
        self.half = self.rows // CORES
        self.band = self.half // self.sections
        self.units = CHUNKS if self.band % (16 * CHUNKS) == 0 else 1
        self.unit = self.band // self.units
        self.block = math.gcd(self.unit, 32)
        self.grad_band = self.half // self.groups
        doubles = self.layers - self.sections
        widest = 0
        for at in range(self.sections):
            low = at + max(0, doubles - (self.sections - at))
            high = min(self.layers - self.sections + at, at + min(at, doubles) + 1)
            widest = max(widest, high - low + 1)
        self.channels = min(widest, CORES * self.slots)

    def send(self, value, target):
        pairs = []
        for pipe in range(self.pipes):
            for section in range(self.sections):
                group_to, core, to = target(pipe // CORES, pipe % CORES, section)
                pipe_to = group_to * CORES + core
                pairs.append((pipe * self.sections + section, pipe_to * self.sections + to))
        return lax.ppermute(value, AXES, pairs)

    def to_core(self, value):
        return self.send(value, lambda g, c, s: (g, 1 - c, s))

    def to_group(self, value, shift):
        return self.send(value, lambda g, c, s: ((g + shift) % self.groups, c, s))

    def to_section(self, value, shift):
        return self.send(value, lambda g, c, s: (g, c, (s + shift) % self.sections))


def plan_tables(z, pipe, section, old, new, lost_pipe, offset):
    layers = range(z.layers)
    lost = lost_pipe(0)
    group, core = pipe // CORES, pipe % CORES
    sibling = group * CORES + (1 - core)
    lost_group = lost // CORES
    tables = {}

    def now_of(at):
        return [jnp.where(at == lost, new(l), old(at, l)) for l in layers]

    def slots_of(sections):
        return [total(as_int(sections[k] == sections[l]) for k in range(l)) for l in layers]

    def layer_at(sections, slots, at, slot):
        hits = [both(sections[l] == at, slots[l] == slot) for l in layers]
        index = total(jnp.where(hits[l], l, 0) for l in layers)
        return index, total(as_int(hit) for hit in hits)

    def lookup(values, index):
        out = values[0]
        for l in layers[1:]:
            out = jnp.where(index == l, values[l], out)
        return out

    my_now = now_of(pipe)
    my_slot = slots_of(my_now)
    sib_now = now_of(sibling)
    sib_slot = slots_of(sib_now)
    new_list = [new(l) for l in layers]
    new_slot = slots_of(new_list)

    donor = [lost_pipe(offset(l)) for l in layers]
    source_section = [old(donor[l], l) for l in layers]
    source_slot = [
        total(as_int(old(donor[l], k) == source_section[l]) for k in range(l)) for l in layers
    ]
    source_group = [donor[l] // CORES for l in layers]
    crosses = [as_int(source_group[l] != lost_group) for l in layers]
    rank = [total(crosses[k] for k in range(l)) for l in layers]
    channel = [
        total(
            as_int(both(source_group[k] == source_group[l], source_section[k] == source_section[l]))
            for k in range(l)
        )
        for l in layers
    ]

    def grad_unit(l, band):
        return [
            (as_int(my_now[l] == section), my_slot[l] * z.groups + band),
            (as_int(sib_now[l] == section), sib_slot[l] * z.groups + band),
        ]

    for shift in range(1, z.groups):
        band = lax.rem(group + shift, z.groups)
        tables["grad_out", shift] = [grad_unit(l, band) for l in layers]
    tables["grad_sum"] = [grad_unit(l, group) + [(1, l)] * (z.groups - 1) for l in layers]
    tables["grad_mean"] = [[(1, l)] * z.sections for l in layers]
    for name, sections, slots in (("mine", my_now, my_slot), ("sibling", sib_now, sib_slot)):
        units = []
        for slot in range(z.slots):
            index, found = layer_at(sections, slots, section, slot)
            for band in range(z.groups):
                unit = []
                for shift in range(z.groups):
                    sender = lax.rem(group + z.groups - shift, z.groups)
                    unit.append((found * as_int(sender == band), index))
                units.append(unit)
        tables[name] = units

    here = [as_int(source_group[l] == group) for l in layers]
    my_chip = [here[l] * as_int(source_section[l] == section) for l in layers]
    from_me = [as_int(donor[l] == pipe) for l in layers]

    for shift in range(1, z.sections):
        band = lax.rem(section + shift, z.sections)
        units = []
        for k in range(z.channels):
            hit = [my_chip[l] * as_int(channel[l] == k) for l in layers]
            slot = total(hit[l] * source_slot[l] for l in layers)
            mine = total(hit[l] * from_me[l] for l in layers)
            found = total(hit)
            index = slot * z.sections + band
            units.append([(mine, index), (found - mine, index)])
        tables["spread", shift] = units

    def held(l_my_chip, l_from_me, l_slot, l_here, l_channel, l_section):
        index = l_slot * z.sections + section
        unit = [(l_my_chip * l_from_me, index), (l_my_chip * (1 - l_from_me), index)]
        for shift in range(1, z.sections):
            sender = lax.rem(section + z.sections - shift, z.sections)
            unit.append((l_here * as_int(l_section == sender), l_channel))
        return unit

    def held_at(index):
        return held(
            *(
                lookup(values, index)
                for values in (my_chip, from_me, source_slot, here, channel, source_section)
            )
        )

    units = []
    for u in range(z.layers):
        hit = [crosses[l] * as_int(rank[l] == u) for l in layers]
        index = total(hit[l] * l for l in layers)
        found = total(hit)
        units.append([(flag * found, at) for flag, at in held_at(index)])
    tables["across"] = units

    def arrived(index, found):
        found = found * as_int(group == lost_group)
        unit = [(flag * found, at) for flag, at in held_at(index)]
        from_group = lookup(source_group, index)
        for shift in range(1, z.groups):
            sender = lax.rem(group + z.groups - shift, z.groups)
            unit.append((found * as_int(from_group == sender), lookup(rank, index)))
        return unit

    for shift in range(1, z.sections):
        target = lax.rem(section + shift, z.sections)
        tables["deliver", shift] = [
            arrived(*layer_at(new_list, new_slot, target, slot)) for slot in range(z.slots)
        ]
    units = []
    for slot in range(z.slots):
        own = arrived(*layer_at(new_list, new_slot, section, slot))
        for band in range(z.sections):
            mine = as_int(section == band)
            unit = [(flag * mine, at) for flag, at in own]
            for shift in range(1, z.sections):
                sender = lax.rem(section + z.sections - shift, z.sections)
                unit.append((as_int(both(sender == band, group == lost_group)), slot))
            units.append(unit)
    tables["collect"] = units

    last = [as_int(pipe == lost), core]
    for slot in range(z.slots):
        last.append(layer_at(my_now, my_slot, section, slot)[1])
    tables["update"] = [[tuple(last)]]
    return tables


def table_size(z):
    sources = z.sections + z.groups + z.sections + 2
    units = (z.sections + z.groups) * (4 * z.layers + 4 * z.slots)
    units += z.sections * (z.channels + 2 * z.slots) + z.layers
    return -(-(2 * units * sources + z.slots + 8) // 1024) * 1024


def make_plan(z, place, old_section, new_section, lost_pipe, donor_offset):
    starts = {}
    size = table_size(z)
    smem = pl.BlockSpec(memory_space=pltpu.SMEM)

    def kernel(place_ref, old_ref, new_ref, lost_ref, offset_ref, table_ref):
        tables = plan_tables(
            z,
            place_ref[0],
            place_ref[1],
            lambda at, l: old_ref[at, l],
            lambda l: new_ref[l],
            lambda rank: lost_ref[rank],
            lambda l: offset_ref[l],
        )
        at = 0
        for name, units in tables.items():
            starts[name] = at
            for unit in units:
                for entry in unit:
                    for value in entry:
                        table_ref[at] = jnp.int32(value)
                        at += 1
        assert at <= size

    table = pl.pallas_call(
        kernel,
        out_shape=jax.ShapeDtypeStruct((size,), jnp.int32),
        in_specs=[smem] * 5,
        out_specs=smem,
        name="plan",
    )(place, old_section, new_section, lost_pipe, donor_offset)
    return table, starts


SMEM_SPEC = pl.BlockSpec(memory_space=pltpu.SMEM)
VMEM_SPEC = pl.BlockSpec(memory_space=pltpu.VMEM)


def cost(operands, results):
    moved = sum(math.prod(a.shape) * a.dtype.itemsize for a in (*operands, *results))
    return pl.CostEstimate(flops=moved // 4, bytes_accessed=moved, transcendentals=0)


class Order:
    def __init__(self):
        self.results, self.last, self.name = {}, [], None

    def begin(self, name):
        self.name = name
        self.last = [self.results[at] for at in AFTER.get(name, ()) if at in self.results]

    def specs(self):
        return [pl.BlockSpec(memory_space=pl.ANY)] * len(self.last)

    def then(self, result):
        self.results[self.name] = result[0]
        return result


SMEM_SPEC = pl.BlockSpec(memory_space=pltpu.SMEM)
VMEM_SPEC = pl.BlockSpec(memory_space=pltpu.VMEM)
PARAMS = pltpu.CompilerParams(vmem_limit_bytes=VMEM)
COST = pl.CostEstimate(flops=1, bytes_accessed=1, transcendentals=0)

UPDATE_COST = pl.CostEstimate(flops=1, bytes_accessed=1, transcendentals=0)


class Rows:
    def __init__(self, value, rows, count, arrays=1, base=0):
        self.value, self.rows, self.count = value, rows, count
        self.arrays, self.base = arrays, base

    def block(self, array, index):
        at = self.base + (array * self.count + index) * self.rows
        return pl.ds(at if isinstance(at, int) else pl.multiple_of(at, 16), self.rows)


class Copy:
    def __init__(self, start, units, sources):
        self.start, self.units, self.sources = start, units, sources
        self.arrays, self.rows = sources[0].arrays, sources[0].rows

    def write(self, table_ref, refs, out_ref, out):
        for unit in range(self.units):
            for at, source in enumerate(self.sources):
                entry = self.start + (unit * len(self.sources) + at) * 2

                @pl.when(table_ref[entry] != 0)
                def _(unit=unit, source=source, ref=refs[at], entry=entry):
                    index = table_ref[entry + 1]
                    for array in range(self.arrays):
                        out_ref[out.block(array, unit)] = ref[source.block(array, index)]


class Sum:
    def __init__(self, start, units, sources):
        self.start, self.units, self.sources = start, units, sources
        self.arrays, self.rows = 1, sources[0].rows

    def write(self, table_ref, refs, out_ref, out):
        for unit in range(self.units):
            total_here = None
            for at, source in enumerate(self.sources):
                entry = self.start + (unit * len(self.sources) + at) * 2
                block = refs[at][source.block(0, table_ref[entry + 1])].astype(jnp.float32)
                block = jnp.where(table_ref[entry] != 0, block, 0.0)
                total_here = block if total_here is None else total_here + block
            out_ref[out.block(0, unit)] = total_here.astype(out_ref.dtype)


def stage(z, order, table, outputs, name):
    operands, slots = [], {}
    for job in (job for jobs in outputs for job in jobs):
        for source in job.sources:
            if id(source.value) not in slots:
                slots[id(source.value)] = len(operands)
                operands.append(source.value)
    places, shapes = [], []
    for jobs in outputs:
        at, row = [], 0
        for job in jobs:
            at.append(Rows(None, job.rows, job.units, job.arrays, row))
            row += job.arrays * job.units * job.rows
        places.append(at)
        shapes.append(jax.ShapeDtypeStruct((row, z.cols), jnp.bfloat16))

    def kernel(table_ref, *refs):
        out_refs = refs[-len(outputs) :]
        for jobs, at, out_ref in zip(outputs, places, out_refs):
            for job, place in zip(jobs, at):
                inputs = [refs[slots[id(source.value)]] for source in job.sources]
                job.write(table_ref, inputs, out_ref, place)

    call = pl.pallas_call(
        kernel,
        out_shape=tuple(shapes),
        in_specs=[SMEM_SPEC] + [VMEM_SPEC] * len(operands) + order.specs(),
        out_specs=tuple([VMEM_SPEC] * len(outputs)),
        compiler_params=PARAMS,
        cost_estimate=COST,
        name=name,
    )
    return order.then(call(table, *operands, *order.last))


def halve(z, order, place, arrays, first, count, units, name):
    unit = z.band // units
    views = [a.reshape(z.slots, CORES, z.sections, units, unit, z.cols) for a in arrays]

    def kernel(place_ref, *refs):
        for part, out_ref in enumerate(refs[-2:]):
            row = 0
            for at in range(len(arrays)):
                ref = refs[part * len(arrays) + at]
                for slot in range(z.slots):
                    for band in range(z.sections):
                        for k in range(count):
                            out_ref[pl.ds(row, unit)] = ref[slot, 0, band, k].astype(jnp.bfloat16)
                            row += unit

    def spec(own):
        def index_map(step, place_ref):
            core = lax.rem(place_ref[0], CORES)
            return (0, core if own else 1 - core, 0, first // count, 0, 0)

        return pl.BlockSpec((z.slots, 1, z.sections, count, unit, z.cols), index_map)

    rows = len(arrays) * z.slots * z.sections * count * unit
    out = jax.ShapeDtypeStruct((rows, z.cols), jnp.bfloat16)
    out_spec = pl.BlockSpec(out.shape, lambda step, place_ref: (0, 0))
    call = pl.pallas_call(
        kernel,
        grid_spec=pltpu.PrefetchScalarGridSpec(
            num_scalar_prefetch=1,
            grid=(1,),
            in_specs=[spec(True)] * len(arrays) + [spec(False)] * len(arrays) + order.specs(),
            out_specs=[out_spec] * 2,
        ),
        out_shape=(out, out),
        compiler_params=PARAMS,
        cost_estimate=COST,
        name="halve_" + name,
    )
    return order.then(call(place, *views, *views, *order.last))


def update(z, order, table, start, state, rebuilt, mean):
    views = [a.reshape(z.slots, CORES, z.half, z.cols) for a in state]
    halves = [chunk[part] for part in range(2) for chunk in rebuilt]

    def kernel(table_ref, *refs):
        local_refs, mean_refs, half_refs = refs[:3], refs[3:5], refs[5:-3]
        out_w, out_one, out_two = refs[-3:]
        slot, half = pl.program_id(0), pl.program_id(1)
        is_lost = table_ref[start] != 0
        mine = table_ref[start + 1] == half
        found = table_ref[start + 2 + slot] != 0

        def each(source, lost):
            @pl.loop(0, z.unit // z.block)
            def _(at):
                for band in range(z.sections):
                    for unit in range(z.units):
                        one_block(source, lost, band, unit, at)

        def one_block(source, lost, band, unit, at):
            place = at * z.block
            row = pl.ds(pl.multiple_of(band * z.band + unit * z.unit + place, 16), z.block)
            mean_row = pl.multiple_of(slot * z.half + band * z.band + unit * z.unit + place, 16)
            grad = mean_refs[source][pl.ds(mean_row, z.block)].astype(jnp.float32)
            grad = grad * (1.0 / z.pipes)
            if lost:
                here = half_refs[source * len(rebuilt) : (source + 1) * len(rebuilt)]
                from_row = (slot * z.sections + band) * z.unit + place
                from_row = pl.ds(pl.multiple_of(from_row, 16), z.block)
                old = [here[array * z.units + unit][from_row] for array in range(3)]
            else:
                old = [ref[0, 0, row] for ref in local_refs]
            weight, one, two = [value.astype(jnp.float32) for value in old]
            next_one = BETA_ONE * one + (1.0 - BETA_ONE) * grad
            next_two = BETA_TWO * two + (1.0 - BETA_TWO) * grad * grad
            move = next_one / (jnp.sqrt(next_two) + EPSILON) + DECAY_RATE * weight
            out_w[0, 0, row] = (weight - LEARN_RATE * move).astype(out_w.dtype)
            out_one[0, 0, row] = next_one
            out_two[0, 0, row] = next_two

        for source in range(2):
            ours = both(found, mine == (source == 0))

            @pl.when(both(ours, is_lost))
            def _(source=source):
                each(source, True)

            @pl.when(both(ours, jnp.logical_not(is_lost)))
            def _(source=source):
                each(source, False)

        @pl.when(jnp.logical_not(found))
        def _():
            for ref in (out_w, out_one, out_two):
                ref[...] = jnp.zeros(ref.shape, ref.dtype)

    def local(slot, half, table_ref):
        keep = 1 - table_ref[start]
        return (slot * keep, half * keep, 0, 0)

    block = (1, 1, z.half, z.cols)
    out_spec = pl.BlockSpec(block, lambda slot, half, table_ref: (slot, half, 0, 0))
    shape = views[0].shape
    call = pl.pallas_call(
        kernel,
        grid_spec=pltpu.PrefetchScalarGridSpec(
            num_scalar_prefetch=1,
            grid=(z.slots, CORES),
            in_specs=[pl.BlockSpec(block, local)] * 3
            + [VMEM_SPEC] * (2 + len(halves))
            + order.specs(),
            out_specs=[out_spec] * 3,
        ),
        out_shape=(
            jax.ShapeDtypeStruct(shape, jnp.bfloat16),
            jax.ShapeDtypeStruct(shape, jnp.float32),
            jax.ShapeDtypeStruct(shape, jnp.float32),
        ),
        compiler_params=PARAMS,
        cost_estimate=UPDATE_COST,
        name="update",
    )
    return order.then(call(table, *views, *mean, *halves, *order.last))


class Gradients:
    def __init__(self, z, order, grads):
        self.z, self.order, self.grads = z, order, grads

    def run(self, outputs, name):
        return stage(self.z, self.order, self.table, outputs, name)

    def rows(self, value):
        return Rows(value, self.z.grad_band, self.z.layers)

    def enter(self, place):
        z = self.z
        own, theirs = halve(z, self.order, place, (self.grads,), 0, 1, 1, "gradients")
        self.held = [
            Rows(flat, z.grad_band, z.slots * z.groups) for flat in (own, z.to_core(theirs))
        ]

    def scatter(self):
        z = self.z
        shifts = range(1, z.groups)
        jobs = [[Sum(self.starts["grad_out", s], z.layers, self.held)] for s in shifts]
        parts = self.run(jobs, "grad_out")
        self.held += [self.rows(z.to_group(part, s)) for s, part in zip(shifts, parts)]

    def exchange(self):
        z = self.z
        (part,) = self.run([[Sum(self.starts["grad_sum"], z.layers, self.held)]], "grad_sum")
        others = [z.to_section(part, s) for s in range(1, z.sections)]
        self.held = [self.rows(value) for value in (part, *others)]

    def gather(self):
        z = self.z
        (part,) = self.run([[Sum(self.starts["grad_mean"], z.layers, self.held)]], "grad_mean")
        others = [z.to_group(part, s) for s in range(1, z.groups)]
        self.held = [self.rows(value) for value in (part, *others)]

    def finish(self):
        z = self.z
        theirs, mine = self.run(
            [
                [Copy(self.starts[name], z.slots * z.groups, self.held)]
                for name in ("sibling", "mine")
            ],
            "mean",
        )
        self.mean = (mine, z.to_core(theirs))


class Chunk:
    def __init__(self, z, order, array, first):
        self.z, self.order, self.array, self.first = z, order, array, first

    def run(self, outputs, name):
        return stage(self.z, self.order, self.table, outputs, name)

    def enter(self, place):
        z = self.z
        own, theirs = halve(z, self.order, place, (self.array,), self.first, 1, z.units, "state")
        held = z.slots * z.sections
        self.held = [Rows(flat, z.unit, held) for flat in (own, z.to_core(theirs))]

    def spread(self):
        z = self.z
        shifts = range(1, z.sections)
        jobs = [[Copy(self.starts["spread", s], z.channels, self.held)] for s in shifts]
        parts = self.run(jobs, "spread")
        for s, part in zip(shifts, parts):
            self.held.append(Rows(z.to_section(part, s), z.unit, z.channels))

    def across(self):
        z = self.z
        (part,) = self.run([[Copy(self.starts["across"], z.layers, self.held)]], "across")
        for s in range(1, z.groups):
            self.held.append(Rows(z.to_group(part, s), z.unit, z.layers))

    def deliver(self):
        z = self.z
        shifts = range(1, z.sections)
        jobs = [[Copy(self.starts["deliver", s], z.slots, self.held)] for s in shifts]
        parts = self.run(jobs, "deliver")
        for s, part in zip(shifts, parts):
            self.held.append(Rows(z.to_section(part, s), z.unit, z.slots))

    def collect(self):
        z = self.z
        units = z.slots * z.sections
        (half,) = self.run([[Copy(self.starts["collect"], units, self.held)]], "collect")
        self.halves = (half, z.to_core(half))


def per_device(
    weights,
    first_moment,
    second_moment,
    gradients,
    old_section,
    new_section,
    lost_pipe,
    donor_offset,
):
    z = Sizes(weights, new_section)
    order = Order()
    place = jnp.stack([lax.axis_index("pipe"), lax.axis_index("section")]).astype(jnp.int32)
    state = (weights[0, 0], first_moment[0, 0], second_moment[0, 0])
    grads = Gradients(z, order, gradients[0, 0])
    chunks = [Chunk(z, order, array, at) for array in state for at in range(z.units)]
    table, starts = make_plan(z, place, old_section, new_section, lost_pipe, donor_offset)
    for part in (grads, *chunks):
        part.table, part.starts = table, starts

    def each(step, *args):
        for at, chunk in enumerate(chunks):
            order.begin(step[0] + str(at))
            getattr(chunk, step)(*args)

    order.begin("ge")
    grads.enter(place)
    each("enter", place)
    order.begin("gs")
    grads.scatter()
    each("spread")
    order.begin("gx")
    grads.exchange()
    each("across")
    order.begin("gg")
    grads.gather()
    each("deliver")
    order.begin("gf")
    grads.finish()
    each("collect")
    order.begin("u")
    rebuilt = [chunk.halves for chunk in chunks]
    outs = update(z, order, table, starts["update"], state, rebuilt, grads.mean)
    return tuple(out.reshape((1, 1, z.slots, z.rows, z.cols)) for out in outs)


def solution(mesh):
    split = P("pipe", "section", None, "tp", None)
    return jax.shard_map(
        per_device,
        mesh=mesh,
        in_specs=(split,) * 4 + (P(),) * 4,
        out_specs=(split,) * 3,
        check_vma=False,
    )
```

```python
import math

import jax
import jax.numpy as jnp
from jax import lax
from jax.experimental import pallas as pl
from jax.experimental.pallas import tpu as pltpu
from jax.sharding import PartitionSpec as P

LEARN_RATE = 0.01
BETA_ONE = 0.9
BETA_TWO = 0.95
EPSILON = 1e-08
DECAY_RATE = 0.1

CORES = 2
SEQUENCE = (
    *("ge", "e0", "gs", "s0", "e1", "e2", "s1", "s2", "gx", "a0", "a1", "a2"),
    *("gg", "d0", "d1", "d2", "gf", "c0", "c1", "c2"),
)
AFTER = {}
VMEM = 40 * 1024 * 1024
HALVE_VMEM = 60 * 1024 * 1024
AXES = ("pipe", "section")


def both(*terms):
    out = terms[0]
    for term in terms[1:]:
        out = jnp.logical_and(out, term)
    return out


def as_int(flag):
    return jnp.where(flag, 1, 0).astype(jnp.int32)


def total(terms):
    out = jnp.int32(0)
    for term in terms:
        out = out + term
    return out


class Sizes:
    def __init__(self, weights, new_section):
        self.pipes = lax.axis_size("pipe")
        self.sections = lax.axis_size("section")
        self.groups = self.pipes // CORES
        self.slots = weights.shape[2]
        self.rows = weights.shape[3]
        self.cols = weights.shape[4]
        self.layers = new_section.shape[0]
        self.half = self.rows // CORES
        self.band = self.half // self.sections
        self.block = math.gcd(self.band, 32)
        self.grad_band = self.half // self.groups
        doubles = self.layers - self.sections
        widest = 0
        for at in range(self.sections):
            low = at + max(0, doubles - (self.sections - at))
            high = min(self.layers - self.sections + at, at + min(at, doubles) + 1)
            widest = max(widest, high - low + 1)
        self.channels = min(widest, CORES * self.slots)

    def send(self, value, target):
        pairs = []
        for pipe in range(self.pipes):
            for section in range(self.sections):
                group_to, core, to = target(pipe // CORES, pipe % CORES, section)
                pipe_to = group_to * CORES + core
                pairs.append((pipe * self.sections + section, pipe_to * self.sections + to))
        return lax.ppermute(value, AXES, pairs)

    def to_core(self, value):
        return self.send(value, lambda g, c, s: (g, 1 - c, s))

    def to_group(self, value, shift):
        return self.send(value, lambda g, c, s: ((g + shift) % self.groups, c, s))

    def to_section(self, value, shift):
        return self.send(value, lambda g, c, s: (g, c, (s + shift) % self.sections))


def plan_tables(z, pipe, section, old, new, lost_pipe, offset):
    layers = range(z.layers)
    lost = lost_pipe(0)
    group, core = pipe // CORES, pipe % CORES
    sibling = group * CORES + (1 - core)
    lost_group = lost // CORES
    tables = {}

    def now_of(at):
        return [jnp.where(at == lost, new(l), old(at, l)) for l in layers]

    def slots_of(sections):
        return [total(as_int(sections[k] == sections[l]) for k in range(l)) for l in layers]

    def layer_at(sections, slots, at, slot):
        hits = [both(sections[l] == at, slots[l] == slot) for l in layers]
        index = total(jnp.where(hits[l], l, 0) for l in layers)
        return index, total(as_int(hit) for hit in hits)

    def lookup(values, index):
        out = values[0]
        for l in layers[1:]:
            out = jnp.where(index == l, values[l], out)
        return out

    my_now = now_of(pipe)
    my_slot = slots_of(my_now)
    sib_now = now_of(sibling)
    sib_slot = slots_of(sib_now)
    new_list = [new(l) for l in layers]
    new_slot = slots_of(new_list)

    donor = [lost_pipe(offset(l)) for l in layers]
    source_section = [old(donor[l], l) for l in layers]
    source_slot = [
        total(as_int(old(donor[l], k) == source_section[l]) for k in range(l)) for l in layers
    ]
    source_group = [donor[l] // CORES for l in layers]
    crosses = [as_int(source_group[l] != lost_group) for l in layers]
    rank = [total(crosses[k] for k in range(l)) for l in layers]
    channel = [
        total(
            as_int(both(source_group[k] == source_group[l], source_section[k] == source_section[l]))
            for k in range(l)
        )
        for l in layers
    ]

    def grad_unit(l, band):
        return [
            (as_int(my_now[l] == section), my_slot[l] * z.groups + band),
            (as_int(sib_now[l] == section), sib_slot[l] * z.groups + band),
        ]

    for shift in range(1, z.groups):
        band = lax.rem(group + shift, z.groups)
        tables["grad_out", shift] = [grad_unit(l, band) for l in layers]
    tables["grad_sum"] = [grad_unit(l, group) + [(1, l)] * (z.groups - 1) for l in layers]
    tables["grad_mean"] = [[(1, l)] * z.sections for l in layers]
    for name, sections, slots in (("mine", my_now, my_slot), ("sibling", sib_now, sib_slot)):
        units = []
        for slot in range(z.slots):
            index, found = layer_at(sections, slots, section, slot)
            for band in range(z.groups):
                unit = []
                for shift in range(z.groups):
                    sender = lax.rem(group + z.groups - shift, z.groups)
                    unit.append((found * as_int(sender == band), index))
                units.append(unit)
        tables[name] = units

    here = [as_int(source_group[l] == group) for l in layers]
    my_chip = [here[l] * as_int(source_section[l] == section) for l in layers]
    from_me = [as_int(donor[l] == pipe) for l in layers]

    for shift in range(1, z.sections):
        band = lax.rem(section + shift, z.sections)
        units = []
        for k in range(z.channels):
            hit = [my_chip[l] * as_int(channel[l] == k) for l in layers]
            slot = total(hit[l] * source_slot[l] for l in layers)
            mine = total(hit[l] * from_me[l] for l in layers)
            found = total(hit)
            index = slot * z.sections + band
            units.append([(mine, index), (found - mine, index)])
        tables["spread", shift] = units

    def held(l_my_chip, l_from_me, l_slot, l_here, l_channel, l_section):
        index = l_slot * z.sections + section
        unit = [(l_my_chip * l_from_me, index), (l_my_chip * (1 - l_from_me), index)]
        for shift in range(1, z.sections):
            sender = lax.rem(section + z.sections - shift, z.sections)
            unit.append((l_here * as_int(l_section == sender), l_channel))
        return unit

    def held_at(index):
        return held(
            *(
                lookup(values, index)
                for values in (my_chip, from_me, source_slot, here, channel, source_section)
            )
        )

    units = []
    for u in range(z.layers):
        hit = [crosses[l] * as_int(rank[l] == u) for l in layers]
        index = total(hit[l] * l for l in layers)
        found = total(hit)
        units.append([(flag * found, at) for flag, at in held_at(index)])
    tables["across"] = units

    def arrived(index, found):
        found = found * as_int(group == lost_group)
        unit = [(flag * found, at) for flag, at in held_at(index)]
        from_group = lookup(source_group, index)
        for shift in range(1, z.groups):
            sender = lax.rem(group + z.groups - shift, z.groups)
            unit.append((found * as_int(from_group == sender), lookup(rank, index)))
        return unit

    for shift in range(1, z.sections):
        target = lax.rem(section + shift, z.sections)
        tables["deliver", shift] = [
            arrived(*layer_at(new_list, new_slot, target, slot)) for slot in range(z.slots)
        ]
    units = []
    for slot in range(z.slots):
        own = arrived(*layer_at(new_list, new_slot, section, slot))
        for band in range(z.sections):
            mine = as_int(section == band)
            unit = [(flag * mine, at) for flag, at in own]
            for shift in range(1, z.sections):
                sender = lax.rem(section + z.sections - shift, z.sections)
                unit.append((as_int(both(sender == band, group == lost_group)), slot))
            units.append(unit)
    tables["collect"] = units

    last = [as_int(pipe == lost), core]
    for slot in range(z.slots):
        last.append(layer_at(my_now, my_slot, section, slot)[1])
    tables["update"] = [[tuple(last)]]
    return tables


def table_size(z):
    sources = z.sections + z.groups + z.sections + 2
    units = (z.sections + z.groups) * (4 * z.layers + 4 * z.slots)
    units += z.sections * (z.channels + 2 * z.slots) + z.layers
    return -(-(2 * units * sources + z.slots + 8) // 1024) * 1024


def make_plan(z, place, old_section, new_section, lost_pipe, donor_offset):
    starts = {}
    size = table_size(z)
    smem = pl.BlockSpec(memory_space=pltpu.SMEM)

    def kernel(place_ref, old_ref, new_ref, lost_ref, offset_ref, table_ref):
        tables = plan_tables(
            z,
            place_ref[0],
            place_ref[1],
            lambda at, l: old_ref[at, l],
            lambda l: new_ref[l],
            lambda rank: lost_ref[rank],
            lambda l: offset_ref[l],
        )
        at = 0
        for name, units in tables.items():
            starts[name] = at
            for unit in units:
                for entry in unit:
                    for value in entry:
                        table_ref[at] = jnp.int32(value)
                        at += 1
        assert at <= size

    table = pl.pallas_call(
        kernel,
        out_shape=jax.ShapeDtypeStruct((size,), jnp.int32),
        in_specs=[smem] * 5,
        out_specs=smem,
        name="plan",
    )(place, old_section, new_section, lost_pipe, donor_offset)
    return table, starts


SMEM_SPEC = pl.BlockSpec(memory_space=pltpu.SMEM)
VMEM_SPEC = pl.BlockSpec(memory_space=pltpu.VMEM)


def cost(operands, results):
    moved = sum(math.prod(a.shape) * a.dtype.itemsize for a in (*operands, *results))
    return pl.CostEstimate(flops=moved // 4, bytes_accessed=moved, transcendentals=0)


class Order:
    def __init__(self):
        self.results, self.last, self.name = {}, [], None

    def begin(self, name):
        self.name = name
        self.last = [self.results[at] for at in AFTER.get(name, ()) if at in self.results]

    def arrived(self, value):
        self.results[self.name + "r"] = value
        return value

    def specs(self):
        return [pl.BlockSpec(memory_space=pl.ANY)] * len(self.last)

    def then(self, result):
        self.results[self.name] = result[0]
        return result


SMEM_SPEC = pl.BlockSpec(memory_space=pltpu.SMEM)
VMEM_SPEC = pl.BlockSpec(memory_space=pltpu.VMEM)
PARAMS = pltpu.CompilerParams(vmem_limit_bytes=VMEM)
COST = pl.CostEstimate(flops=10**9, bytes_accessed=1, transcendentals=0)

UPDATE_COST = pl.CostEstimate(flops=1, bytes_accessed=1, transcendentals=0)


class Rows:
    def __init__(self, value, rows, count, arrays=1, base=0):
        self.value, self.rows, self.count = value, rows, count
        self.arrays, self.base = arrays, base

    def block(self, array, index):
        at = self.base + (array * self.count + index) * self.rows
        return pl.ds(at if isinstance(at, int) else pl.multiple_of(at, 16), self.rows)


class Copy:
    def __init__(self, start, units, sources):
        self.start, self.units, self.sources = start, units, sources
        self.arrays, self.rows = sources[0].arrays, sources[0].rows

    def write(self, table_ref, refs, out_ref, out):
        for unit in range(self.units):
            for at, source in enumerate(self.sources):
                entry = self.start + (unit * len(self.sources) + at) * 2

                @pl.when(table_ref[entry] != 0)
                def _(unit=unit, source=source, ref=refs[at], entry=entry):
                    index = table_ref[entry + 1]
                    for array in range(self.arrays):
                        out_ref[out.block(array, unit)] = ref[source.block(array, index)]


class Sum:
    def __init__(self, start, units, sources):
        self.start, self.units, self.sources = start, units, sources
        self.arrays, self.rows = 1, sources[0].rows

    def write(self, table_ref, refs, out_ref, out):
        for unit in range(self.units):
            total_here = None
            for at, source in enumerate(self.sources):
                entry = self.start + (unit * len(self.sources) + at) * 2
                block = refs[at][source.block(0, table_ref[entry + 1])].astype(jnp.float32)
                block = jnp.where(table_ref[entry] != 0, block, 0.0)
                total_here = block if total_here is None else total_here + block
            out_ref[out.block(0, unit)] = total_here.astype(out_ref.dtype)


def stage(z, order, table, outputs, name):
    operands, slots = [], {}
    for job in (job for jobs in outputs for job in jobs):
        for source in job.sources:
            if id(source.value) not in slots:
                slots[id(source.value)] = len(operands)
                operands.append(source.value)
    places, shapes = [], []
    for jobs in outputs:
        at, row = [], 0
        for job in jobs:
            at.append(Rows(None, job.rows, job.units, job.arrays, row))
            row += job.arrays * job.units * job.rows
        places.append(at)
        shapes.append(jax.ShapeDtypeStruct((row, z.cols), jnp.bfloat16))

    def kernel(table_ref, *refs):
        out_refs = refs[-len(outputs) :]
        for jobs, at, out_ref in zip(outputs, places, out_refs):
            for job, place in zip(jobs, at):
                inputs = [refs[slots[id(source.value)]] for source in job.sources]
                job.write(table_ref, inputs, out_ref, place)

    call = pl.pallas_call(
        kernel,
        out_shape=tuple(shapes),
        in_specs=[SMEM_SPEC] + [VMEM_SPEC] * len(operands) + order.specs(),
        out_specs=tuple([VMEM_SPEC] * len(outputs)),
        compiler_params=PARAMS,
        cost_estimate=COST,
        name=name,
    )
    return order.then(call(table, *operands, *order.last))


def halve(z, order, place, array, name):
    view = array.reshape(z.slots, CORES, z.half, z.cols)
    straight = array.dtype == jnp.bfloat16

    def kernel(place_ref, array_ref, *refs):
        own_ref, their_ref, sems = refs[-5], refs[-4], refs[-1]
        landed = refs[-3:-1]
        core = lax.rem(place_ref[0], CORES)
        copies = []
        for part, (half, out_ref) in enumerate(((1 - core, their_ref), (core, own_ref))):
            for slot in range(z.slots):
                rows = pl.ds(slot * z.half, z.half)
                target = out_ref if straight else landed[part]
                copy = pltpu.make_async_copy(
                    array_ref.at[slot, half], target.at[rows], sems.at[part, slot]
                )
                copy.start()
                copies.append((copy, part, out_ref, slot))
        for copy, part, out_ref, slot in copies:
            copy.wait()
            if not straight:

                @pl.loop(0, z.half // z.block)
                def _(at, part=part, out_ref=out_ref, slot=slot):
                    rows = pl.ds(pl.multiple_of(slot * z.half + at * z.block, 16), z.block)
                    out_ref[rows] = landed[part][rows].astype(jnp.bfloat16)

    out = jax.ShapeDtypeStruct((z.slots * z.half, z.cols), jnp.bfloat16)
    scratch = (16, z.cols) if straight else out.shape
    call = pl.pallas_call(
        kernel,
        out_shape=(out, out),
        in_specs=[SMEM_SPEC, pl.BlockSpec(memory_space=pltpu.HBM)] + order.specs(),
        out_specs=(VMEM_SPEC, VMEM_SPEC),
        scratch_shapes=[
            pltpu.VMEM(scratch, array.dtype),
            pltpu.VMEM(scratch, array.dtype),
            pltpu.SemaphoreType.DMA((2, z.slots)),
        ],
        compiler_params=pltpu.CompilerParams(vmem_limit_bytes=HALVE_VMEM),
        cost_estimate=COST,
        name="halve_" + name,
    )
    return order.then(call(place, view, *order.last))


def update(z, order, table, start, state, rebuilt, mean):
    views = [a.reshape(z.slots * z.rows, z.cols) for a in state]
    halves = [chunk[part] for part in range(2) for chunk in rebuilt]

    def kernel(table_ref, *refs):
        local_refs, mean_refs, half_refs = refs[:3], refs[3:5], refs[5:-3]
        out_w, out_one, out_two = refs[-3:]
        slot, half = pl.program_id(0), pl.program_id(1)
        is_lost = table_ref[start] != 0
        mine = table_ref[start + 1] == half
        found = table_ref[start + 2 + slot] != 0

        def each(source, lost):
            @pl.loop(0, z.half // z.block)
            def _(at):
                one_block(source, lost, at * z.block)

        def one_block(source, lost, at):
            row = pl.ds(pl.multiple_of(at, 16), z.block)
            from_row = pl.ds(pl.multiple_of(slot * z.half + at, 16), z.block)
            grad = mean_refs[source][from_row].astype(jnp.float32)
            grad = grad * (1.0 / z.pipes)
            if lost:
                old = [ref[from_row] for ref in half_refs[source * 3 : source * 3 + 3]]
            else:
                local_row = pl.multiple_of(slot * z.rows + half * z.half + at, 16)
                old = [ref[pl.ds(local_row, z.block)] for ref in local_refs]
            weight, one, two = [value.astype(jnp.float32) for value in old]
            next_one = BETA_ONE * one + (1.0 - BETA_ONE) * grad
            next_two = BETA_TWO * two + (1.0 - BETA_TWO) * grad * grad
            move = next_one / (jnp.sqrt(next_two) + EPSILON) + DECAY_RATE * weight
            out_w[0, 0, row] = (weight - LEARN_RATE * move).astype(out_w.dtype)
            out_one[0, 0, row] = next_one
            out_two[0, 0, row] = next_two

        for source in range(2):
            ours = both(found, mine == (source == 0))

            @pl.when(both(ours, is_lost))
            def _(source=source):
                each(source, True)

            @pl.when(both(ours, jnp.logical_not(is_lost)))
            def _(source=source):
                each(source, False)

        @pl.when(jnp.logical_not(found))
        def _():
            for ref in (out_w, out_one, out_two):
                ref[...] = jnp.zeros(ref.shape, ref.dtype)

    block = (1, 1, z.half, z.cols)
    out_spec = pl.BlockSpec(block, lambda slot, half, table_ref: (slot, half, 0, 0))
    shape = (z.slots, CORES, z.half, z.cols)
    call = pl.pallas_call(
        kernel,
        grid_spec=pltpu.PrefetchScalarGridSpec(
            num_scalar_prefetch=1,
            grid=(z.slots, CORES),
            in_specs=[VMEM_SPEC] * (5 + len(halves)) + order.specs(),
            out_specs=[out_spec] * 3,
        ),
        out_shape=(
            jax.ShapeDtypeStruct(shape, jnp.bfloat16),
            jax.ShapeDtypeStruct(shape, jnp.float32),
            jax.ShapeDtypeStruct(shape, jnp.float32),
        ),
        compiler_params=PARAMS,
        cost_estimate=UPDATE_COST,
        name="update",
    )
    return order.then(call(table, *views, *mean, *halves, *order.last))


class Gradients:
    def __init__(self, z, order, grads):
        self.z, self.order, self.grads = z, order, grads

    def run(self, outputs, name):
        return stage(self.z, self.order, self.table, outputs, name)

    def rows(self, value):
        return Rows(value, self.z.grad_band, self.z.layers)

    def enter(self, place):
        z = self.z
        own, theirs = halve(z, self.order, place, self.grads, "gradients")
        theirs = self.order.arrived(z.to_core(theirs))
        self.held = [Rows(flat, z.grad_band, z.slots * z.groups) for flat in (own, theirs)]

    def scatter(self):
        z = self.z
        shifts = range(1, z.groups)
        jobs = [[Sum(self.starts["grad_out", s], z.layers, self.held)] for s in shifts]
        parts = self.run(jobs, "grad_out")
        self.held += [
            self.rows(self.order.arrived(z.to_group(part, s))) for s, part in zip(shifts, parts)
        ]

    def exchange(self):
        z = self.z
        (part,) = self.run([[Sum(self.starts["grad_sum"], z.layers, self.held)]], "grad_sum")
        others = [self.order.arrived(z.to_section(part, s)) for s in range(1, z.sections)]
        self.held = [self.rows(value) for value in (part, *others)]

    def gather(self):
        z = self.z
        (part,) = self.run([[Sum(self.starts["grad_mean"], z.layers, self.held)]], "grad_mean")
        others = [self.order.arrived(z.to_group(part, s)) for s in range(1, z.groups)]
        self.held = [self.rows(value) for value in (part, *others)]

    def finish(self):
        z = self.z
        theirs, mine = self.run(
            [
                [Copy(self.starts[name], z.slots * z.groups, self.held)]
                for name in ("sibling", "mine")
            ],
            "mean",
        )
        self.mean = (mine, self.order.arrived(z.to_core(theirs)))


class Chunk:
    def __init__(self, z, order, array):
        self.z, self.order, self.array = z, order, array

    def run(self, outputs, name):
        return stage(self.z, self.order, self.table, outputs, name)

    def enter(self, place):
        z = self.z
        own, theirs = halve(z, self.order, place, self.array, "state")
        held = z.slots * z.sections
        theirs = self.order.arrived(z.to_core(theirs))
        self.held = [Rows(flat, z.band, held) for flat in (own, theirs)]

    def spread(self):
        z = self.z
        shifts = range(1, z.sections)
        jobs = [[Copy(self.starts["spread", s], z.channels, self.held)] for s in shifts]
        parts = self.run(jobs, "spread")
        for s, part in zip(shifts, parts):
            self.held.append(Rows(self.order.arrived(z.to_section(part, s)), z.band, z.channels))

    def across(self):
        z = self.z
        (part,) = self.run([[Copy(self.starts["across"], z.layers, self.held)]], "across")
        for s in range(1, z.groups):
            self.held.append(Rows(self.order.arrived(z.to_group(part, s)), z.band, z.layers))

    def deliver(self):
        z = self.z
        shifts = range(1, z.sections)
        jobs = [[Copy(self.starts["deliver", s], z.slots, self.held)] for s in shifts]
        parts = self.run(jobs, "deliver")
        for s, part in zip(shifts, parts):
            self.held.append(Rows(self.order.arrived(z.to_section(part, s)), z.band, z.slots))

    def collect(self):
        z = self.z
        units = z.slots * z.sections
        (half,) = self.run([[Copy(self.starts["collect"], units, self.held)]], "collect")
        self.halves = (half, self.order.arrived(z.to_core(half)))


def per_device(
    weights,
    first_moment,
    second_moment,
    gradients,
    old_section,
    new_section,
    lost_pipe,
    donor_offset,
):
    z = Sizes(weights, new_section)
    order = Order()
    place = jnp.stack([lax.axis_index("pipe"), lax.axis_index("section")]).astype(jnp.int32)
    state = (weights[0, 0], first_moment[0, 0], second_moment[0, 0])
    grads = Gradients(z, order, gradients[0, 0])
    chunks = [Chunk(z, order, array) for array in state]
    table, starts = make_plan(z, place, old_section, new_section, lost_pipe, donor_offset)
    for part in (grads, *chunks):
        part.table, part.starts = table, starts

    for name in SEQUENCE:
        order.begin(name)
        if name[0] == "g" and name[1] in "esxgf":
            part = grads
            step = dict(e="enter", s="scatter", x="exchange", g="gather", f="finish")[name[1]]
        else:
            part = chunks[int(name[1])]
            step = dict(e="enter", s="spread", a="across", d="deliver", c="collect")[name[0]]
        if step == "enter":
            part.enter(place)
        else:
            getattr(part, step)()
    order.begin("u")
    rebuilt = [chunk.halves for chunk in chunks]
    outs = update(z, order, table, starts["update"], state, rebuilt, grads.mean)
    return tuple(out.reshape((1, 1, z.slots, z.rows, z.cols)) for out in outs)


def solution(mesh):
    split = P("pipe", "section", None, "tp", None)
    return jax.shard_map(
        per_device,
        mesh=mesh,
        in_specs=(split,) * 4 + (P(),) * 4,
        out_specs=(split,) * 3,
        check_vma=False,
    )
```

```python
import jax
import jax.numpy as jnp
from jax import lax
from jax.experimental import pallas as pl
from jax.experimental.pallas import tpu as pltpu
from jax.sharding import PartitionSpec as P

LEARN_RATE = 0.01
BETA_ONE = 0.9
BETA_TWO = 0.95
EPSILON = 1e-08
DECAY_RATE = 0.1

CORES = 2
SEQUENCE = (
    *("ge", "e0", "gs", "s0", "e1", "e2", "s1", "s2", "gx", "a0", "a1", "a2"),
    *("gg", "d0", "d1", "d2", "gf", "c0", "c1", "c2"),
)
AFTER = {}
VMEM = 24 * 1024 * 1024
AXES = ("pipe", "section")


def both(*terms):
    out = terms[0]
    for term in terms[1:]:
        out = jnp.logical_and(out, term)
    return out


def as_int(flag):
    return jnp.where(flag, 1, 0).astype(jnp.int32)


def total(terms):
    out = jnp.int32(0)
    for term in terms:
        out = out + term
    return out


class Sizes:
    def __init__(self, weights, new_section):
        self.pipes = lax.axis_size("pipe")
        self.sections = lax.axis_size("section")
        self.groups = self.pipes // CORES
        self.slots = weights.shape[2]
        self.rows = weights.shape[3]
        self.cols = weights.shape[4]
        self.layers = new_section.shape[0]
        self.half = self.rows // CORES
        self.band = self.half // self.sections
        self.grad_band = self.half // self.groups
        doubles = self.layers - self.sections
        widest = 0
        for at in range(self.sections):
            low = at + max(0, doubles - (self.sections - at))
            high = min(self.layers - self.sections + at, at + min(at, doubles) + 1)
            widest = max(widest, high - low + 1)
        self.channels = min(widest, CORES * self.slots)

    def send(self, value, target):
        pairs = []
        for pipe in range(self.pipes):
            for section in range(self.sections):
                group_to, core, to = target(pipe // CORES, pipe % CORES, section)
                pipe_to = group_to * CORES + core
                pairs.append((pipe * self.sections + section, pipe_to * self.sections + to))
        return lax.ppermute(value, AXES, pairs)

    def to_core(self, value):
        return self.send(value, lambda g, c, s: (g, 1 - c, s))

    def to_group(self, value, shift):
        return self.send(value, lambda g, c, s: ((g + shift) % self.groups, c, s))

    def to_section(self, value, shift):
        return self.send(value, lambda g, c, s: (g, c, (s + shift) % self.sections))


def plan_tables(z, pipe, section, old, new, lost_pipe, offset):
    layers = range(z.layers)
    lost = lost_pipe(0)
    group, core = pipe // CORES, pipe % CORES
    sibling = group * CORES + (1 - core)
    lost_group = lost // CORES
    tables = {}

    def now_of(at):
        return [jnp.where(at == lost, new(l), old(at, l)) for l in layers]

    def slots_of(sections):
        return [total(as_int(sections[k] == sections[l]) for k in range(l)) for l in layers]

    def layer_at(sections, slots, at, slot):
        hits = [both(sections[l] == at, slots[l] == slot) for l in layers]
        index = total(jnp.where(hits[l], l, 0) for l in layers)
        return index, total(as_int(hit) for hit in hits)

    def lookup(values, index):
        out = values[0]
        for l in layers[1:]:
            out = jnp.where(index == l, values[l], out)
        return out

    my_now = now_of(pipe)
    my_slot = slots_of(my_now)
    sib_now = now_of(sibling)
    sib_slot = slots_of(sib_now)
    new_list = [new(l) for l in layers]
    new_slot = slots_of(new_list)

    donor = [lost_pipe(offset(l)) for l in layers]
    source_section = [old(donor[l], l) for l in layers]
    source_slot = [
        total(as_int(old(donor[l], k) == source_section[l]) for k in range(l)) for l in layers
    ]
    source_group = [donor[l] // CORES for l in layers]
    crosses = [as_int(source_group[l] != lost_group) for l in layers]
    rank = [total(crosses[k] for k in range(l)) for l in layers]
    channel = [
        total(
            as_int(both(source_group[k] == source_group[l], source_section[k] == source_section[l]))
            for k in range(l)
        )
        for l in layers
    ]

    def grad_unit(l, band):
        return [
            (as_int(my_now[l] == section), (my_slot[l] * CORES + core) * z.groups + band),
            (as_int(sib_now[l] == section), sib_slot[l] * z.groups + band),
        ]

    for shift in range(1, z.groups):
        band = lax.rem(group + shift, z.groups)
        tables["grad_out", shift] = [grad_unit(l, band) for l in layers]
    tables["grad_sum"] = [grad_unit(l, group) + [(1, l)] * (z.groups - 1) for l in layers]
    tables["grad_mean"] = [[(1, l)] * z.sections for l in layers]
    for name, sections, slots in (("mine", my_now, my_slot), ("sibling", sib_now, sib_slot)):
        units = []
        for slot in range(z.slots):
            index, found = layer_at(sections, slots, section, slot)
            for band in range(z.groups):
                unit = []
                for shift in range(z.groups):
                    sender = lax.rem(group + z.groups - shift, z.groups)
                    unit.append((found * as_int(sender == band), index))
                units.append(unit)
        tables[name] = units

    here = [as_int(source_group[l] == group) for l in layers]
    my_chip = [here[l] * as_int(source_section[l] == section) for l in layers]
    from_me = [as_int(donor[l] == pipe) for l in layers]

    for shift in range(1, z.sections):
        band = lax.rem(section + shift, z.sections)
        units = []
        for k in range(z.channels):
            hit = [my_chip[l] * as_int(channel[l] == k) for l in layers]
            slot = total(hit[l] * source_slot[l] for l in layers)
            mine = total(hit[l] * from_me[l] for l in layers)
            found = total(hit)
            own = (slot * CORES + core) * z.sections + band
            units.append([(mine, own), (found - mine, slot * z.sections + band)])
        tables["spread", shift] = units

    def held(l_my_chip, l_from_me, l_slot, l_here, l_channel, l_section):
        own = (l_slot * CORES + core) * z.sections + section
        index = l_slot * z.sections + section
        unit = [(l_my_chip * l_from_me, own), (l_my_chip * (1 - l_from_me), index)]
        for shift in range(1, z.sections):
            sender = lax.rem(section + z.sections - shift, z.sections)
            unit.append((l_here * as_int(l_section == sender), l_channel))
        return unit

    def held_at(index):
        return held(
            *(
                lookup(values, index)
                for values in (my_chip, from_me, source_slot, here, channel, source_section)
            )
        )

    units = []
    for u in range(z.layers):
        hit = [crosses[l] * as_int(rank[l] == u) for l in layers]
        index = total(hit[l] * l for l in layers)
        found = total(hit)
        units.append([(flag * found, at) for flag, at in held_at(index)])
    tables["across"] = units

    def arrived(index, found):
        found = found * as_int(group == lost_group)
        unit = [(flag * found, at) for flag, at in held_at(index)]
        from_group = lookup(source_group, index)
        for shift in range(1, z.groups):
            sender = lax.rem(group + z.groups - shift, z.groups)
            unit.append((found * as_int(from_group == sender), lookup(rank, index)))
        return unit

    for shift in range(1, z.sections):
        target = lax.rem(section + shift, z.sections)
        tables["deliver", shift] = [
            arrived(*layer_at(new_list, new_slot, target, slot)) for slot in range(z.slots)
        ]
    units = []
    for slot in range(z.slots):
        own = arrived(*layer_at(new_list, new_slot, section, slot))
        for band in range(z.sections):
            mine = as_int(section == band)
            unit = [(flag * mine, at) for flag, at in own]
            for shift in range(1, z.sections):
                sender = lax.rem(section + z.sections - shift, z.sections)
                unit.append((as_int(both(sender == band, group == lost_group)), slot))
            units.append(unit)
    tables["collect"] = units

    last = [as_int(pipe == lost), core]
    for slot in range(z.slots):
        last.append(layer_at(my_now, my_slot, section, slot)[1])
    tables["update"] = [[tuple(last)]]
    return tables


def table_size(z):
    sources = z.sections + z.groups + z.sections + 2
    units = (z.sections + z.groups) * (4 * z.layers + 4 * z.slots)
    units += z.sections * (z.channels + 2 * z.slots) + z.layers
    return -(-(2 * units * sources + z.slots + 8) // 1024) * 1024


def make_plan(z, place, old_section, new_section, lost_pipe, donor_offset):
    starts = {}
    size = table_size(z)
    smem = pl.BlockSpec(memory_space=pltpu.SMEM)

    def kernel(place_ref, old_ref, new_ref, lost_ref, offset_ref, table_ref):
        tables = plan_tables(
            z,
            place_ref[0],
            place_ref[1],
            lambda at, l: old_ref[at, l],
            lambda l: new_ref[l],
            lambda rank: lost_ref[rank],
            lambda l: offset_ref[l],
        )
        at = 0
        for name, units in tables.items():
            starts[name] = at
            for unit in units:
                for entry in unit:
                    for value in entry:
                        table_ref[at] = jnp.int32(value)
                        at += 1
        assert at <= size

    table = pl.pallas_call(
        kernel,
        out_shape=jax.ShapeDtypeStruct((size,), jnp.int32),
        in_specs=[smem] * 5,
        out_specs=smem,
        name="plan",
    )(place, old_section, new_section, lost_pipe, donor_offset)
    return table, starts


SMEM_SPEC = pl.BlockSpec(memory_space=pltpu.SMEM)
VMEM_SPEC = pl.BlockSpec(memory_space=pltpu.VMEM)


def cost(operands, results):
    moved = sum(math.prod(a.shape) * a.dtype.itemsize for a in (*operands, *results))
    return pl.CostEstimate(flops=moved // 4, bytes_accessed=moved, transcendentals=0)


class Order:
    def __init__(self):
        self.results, self.last, self.name = {}, [], None

    def begin(self, name):
        self.name = name
        self.last = [self.results[at] for at in AFTER.get(name, ()) if at in self.results]

    def arrived(self, value):
        self.results[self.name + "r"] = value
        return value

    def specs(self):
        return [pl.BlockSpec(memory_space=pl.ANY)] * len(self.last)

    def then(self, result):
        self.results[self.name] = result[0]
        return result


SMEM_SPEC = pl.BlockSpec(memory_space=pltpu.SMEM)
VMEM_SPEC = pl.BlockSpec(memory_space=pltpu.VMEM)
PARAMS = pltpu.CompilerParams(vmem_limit_bytes=VMEM)
COST = pl.CostEstimate(flops=10**9, bytes_accessed=1, transcendentals=0)

UPDATE_COST = pl.CostEstimate(flops=1, bytes_accessed=1, transcendentals=0)


class Rows:
    def __init__(self, value, rows, count, arrays=1, base=0):
        self.value, self.rows, self.count = value, rows, count
        self.arrays, self.base = arrays, base

    def block(self, array, index):
        at = self.base + (array * self.count + index) * self.rows
        return pl.ds(at if isinstance(at, int) else pl.multiple_of(at, 16), self.rows)


class Copy:
    def __init__(self, start, units, sources):
        self.start, self.units, self.sources = start, units, sources
        self.arrays, self.rows = sources[0].arrays, sources[0].rows

    def write(self, table_ref, refs, out_ref, out):
        for unit in range(self.units):
            for at, source in enumerate(self.sources):
                entry = self.start + (unit * len(self.sources) + at) * 2

                @pl.when(table_ref[entry] != 0)
                def _(unit=unit, source=source, ref=refs[at], entry=entry):
                    index = table_ref[entry + 1]
                    for array in range(self.arrays):
                        block = ref[source.block(array, index)]
                        out_ref[out.block(array, unit)] = block.astype(out_ref.dtype)


class Sum:
    def __init__(self, start, units, sources):
        self.start, self.units, self.sources = start, units, sources
        self.arrays, self.rows = 1, sources[0].rows

    def write(self, table_ref, refs, out_ref, out):
        for unit in range(self.units):
            total_here = None
            for at, source in enumerate(self.sources):
                entry = self.start + (unit * len(self.sources) + at) * 2
                block = refs[at][source.block(0, table_ref[entry + 1])].astype(jnp.float32)
                block = jnp.where(table_ref[entry] != 0, block, 0.0)
                total_here = block if total_here is None else total_here + block
            out_ref[out.block(0, unit)] = total_here.astype(out_ref.dtype)


def stage(z, order, table, outputs, name):
    operands, slots = [], {}
    for job in (job for jobs in outputs for job in jobs):
        for source in job.sources:
            if id(source.value) not in slots:
                slots[id(source.value)] = len(operands)
                operands.append(source.value)
    places, shapes = [], []
    for jobs in outputs:
        at, row = [], 0
        for job in jobs:
            at.append(Rows(None, job.rows, job.units, job.arrays, row))
            row += job.arrays * job.units * job.rows
        places.append(at)
        shapes.append(jax.ShapeDtypeStruct((row, z.cols), jnp.bfloat16))

    def kernel(table_ref, *refs):
        out_refs = refs[-len(outputs) :]
        for jobs, at, out_ref in zip(outputs, places, out_refs):
            for job, place in zip(jobs, at):
                inputs = [refs[slots[id(source.value)]] for source in job.sources]
                job.write(table_ref, inputs, out_ref, place)

    call = pl.pallas_call(
        kernel,
        out_shape=tuple(shapes),
        in_specs=[SMEM_SPEC] + [VMEM_SPEC] * len(operands) + order.specs(),
        out_specs=tuple([VMEM_SPEC] * len(outputs)),
        compiler_params=PARAMS,
        cost_estimate=COST,
        name=name,
    )
    return order.then(call(table, *operands, *order.last))


def sibling_half(z, order, place, array, name):
    view = array.reshape(z.slots, CORES, z.half, z.cols)

    def kernel(place_ref, array_ref, *refs):
        refs[-1][...] = array_ref[0, 0].astype(jnp.bfloat16)

    def half_of(slot, place_ref):
        return (slot, 1 - lax.rem(place_ref[0], CORES), 0, 0)

    out = jax.ShapeDtypeStruct((z.slots * z.half, z.cols), jnp.bfloat16)
    call = pl.pallas_call(
        kernel,
        grid_spec=pltpu.PrefetchScalarGridSpec(
            num_scalar_prefetch=1,
            grid=(z.slots,),
            in_specs=[pl.BlockSpec((1, 1, z.half, z.cols), half_of)] + order.specs(),
            out_specs=pl.BlockSpec((z.half, z.cols), lambda slot, place_ref: (slot, 0)),
        ),
        out_shape=out,
        compiler_params=PARAMS,
        cost_estimate=COST,
        name="halve_" + name,
    )
    return order.then((call(place, view, *order.last),))[0]


def update(z, order, table, start, part, state, rebuilt, mean, outs):
    views = [a.reshape(z.slots * z.rows, z.cols) for a in state]
    outs = [] if outs is None else list(outs)
    rows, cols = 16, min(z.cols, 128)

    def half_now(table_ref):
        core = table_ref[start + 1]
        return core if part == 0 else 1 - core

    def kernel(table_ref, *refs):
        local_refs, lost_refs, mean_ref = refs[:3], refs[3:6], refs[6]
        out_refs = refs[-3:]
        slot = pl.program_id(0)
        is_lost = table_ref[start] != 0
        found = table_ref[start + 2 + slot] != 0

        def each(sources, base):
            @pl.loop(0, z.half // rows)
            def _(at):
                row = pl.ds(pl.multiple_of(at * rows, rows), rows)
                mean_row = pl.ds(pl.multiple_of(slot * z.half + at * rows, rows), rows)
                from_row = pl.ds(pl.multiple_of(base + at * rows, rows), rows)
                for first in range(0, z.cols, cols):
                    lanes = pl.ds(first, cols)
                    weight, one, two = [
                        ref[from_row, lanes].astype(jnp.float32) for ref in sources
                    ]
                    grad = mean_ref[mean_row, lanes].astype(jnp.float32)
                    next_one = BETA_ONE * one + ((1.0 - BETA_ONE) / z.pipes) * grad
                    next_two = BETA_TWO * two + ((1.0 - BETA_TWO) / z.pipes**2) * (grad * grad)
                    move = next_one / (jnp.sqrt(next_two) + EPSILON)
                    next_weight = (1.0 - LEARN_RATE * DECAY_RATE) * weight - LEARN_RATE * move
                    for ref, value in zip(out_refs, (next_weight, next_one, next_two)):
                        ref[0, 0, row, lanes] = value.astype(ref.dtype)

        @pl.when(both(found, is_lost))
        def _():
            each(lost_refs, slot * z.half)

        @pl.when(both(found, jnp.logical_not(is_lost)))
        def _():
            each(local_refs, slot * z.rows + half_now(table_ref) * z.half)

        @pl.when(jnp.logical_not(found))
        def _():
            for ref in out_refs:
                ref[...] = jnp.zeros(ref.shape, ref.dtype)

    block = (1, 1, z.half, z.cols)
    out_spec = pl.BlockSpec(block, lambda slot, table_ref: (slot, half_now(table_ref), 0, 0))
    shape = (z.slots, CORES, z.half, z.cols)
    call = pl.pallas_call(
        kernel,
        grid_spec=pltpu.PrefetchScalarGridSpec(
            num_scalar_prefetch=1,
            grid=(z.slots,),
            in_specs=[VMEM_SPEC] * 7
            + [pl.BlockSpec(memory_space=pl.ANY)] * len(outs)
            + order.specs(),
            out_specs=[out_spec] * 3,
        ),
        out_shape=(
            jax.ShapeDtypeStruct(shape, jnp.bfloat16),
            jax.ShapeDtypeStruct(shape, jnp.float32),
            jax.ShapeDtypeStruct(shape, jnp.float32),
        ),
        input_output_aliases={8 + at: at for at in range(len(outs))},
        compiler_params=PARAMS,
        cost_estimate=UPDATE_COST,
        name="update",
    )
    operands = (*views, *(half[part] for half in rebuilt), mean[part], *outs)
    return order.then(call(table, *operands, *order.last))


class Gradients:
    def __init__(self, z, order, grads):
        self.z, self.order, self.grads = z, order, grads

    def run(self, outputs, name):
        return stage(self.z, self.order, self.table, outputs, name)

    def rows(self, value):
        return Rows(value, self.z.grad_band, self.z.layers)

    def enter(self, place):
        z = self.z
        theirs = z.to_core(sibling_half(z, self.order, place, self.grads, "gradients"))
        own = self.grads.reshape(z.slots * z.rows, z.cols)
        theirs = self.order.arrived(theirs)
        self.held = [
            Rows(own, z.grad_band, z.slots * CORES * z.groups),
            Rows(theirs, z.grad_band, z.slots * z.groups),
        ]

    def scatter(self):
        z = self.z
        shifts = range(1, z.groups)
        jobs = [[Sum(self.starts["grad_out", s], z.layers, self.held)] for s in shifts]
        parts = self.run(jobs, "grad_out")
        self.held += [
            self.rows(self.order.arrived(z.to_group(part, s))) for s, part in zip(shifts, parts)
        ]

    def exchange(self):
        z = self.z
        (part,) = self.run([[Sum(self.starts["grad_sum"], z.layers, self.held)]], "grad_sum")
        others = [self.order.arrived(z.to_section(part, s)) for s in range(1, z.sections)]
        self.held = [self.rows(value) for value in (part, *others)]

    def gather(self):
        z = self.z
        (part,) = self.run([[Sum(self.starts["grad_mean"], z.layers, self.held)]], "grad_mean")
        others = [self.order.arrived(z.to_group(part, s)) for s in range(1, z.groups)]
        self.held = [self.rows(value) for value in (part, *others)]

    def finish(self):
        z = self.z
        theirs, mine = self.run(
            [
                [Copy(self.starts[name], z.slots * z.groups, self.held)]
                for name in ("sibling", "mine")
            ],
            "mean",
        )
        self.mean = (mine, self.order.arrived(z.to_core(theirs)))


class Chunk:
    def __init__(self, z, order, array):
        self.z, self.order, self.array = z, order, array

    def run(self, outputs, name):
        return stage(self.z, self.order, self.table, outputs, name)

    def enter(self, place):
        z = self.z
        theirs = z.to_core(sibling_half(z, self.order, place, self.array, "state"))
        own = self.array.reshape(z.slots * z.rows, z.cols)
        theirs = self.order.arrived(theirs)
        held = z.slots * z.sections
        self.held = [Rows(own, z.band, CORES * held), Rows(theirs, z.band, held)]

    def spread(self):
        z = self.z
        shifts = range(1, z.sections)
        jobs = [[Copy(self.starts["spread", s], z.channels, self.held)] for s in shifts]
        parts = self.run(jobs, "spread")
        for s, part in zip(shifts, parts):
            self.held.append(Rows(self.order.arrived(z.to_section(part, s)), z.band, z.channels))

    def across(self):
        z = self.z
        (part,) = self.run([[Copy(self.starts["across"], z.layers, self.held)]], "across")
        for s in range(1, z.groups):
            self.held.append(Rows(self.order.arrived(z.to_group(part, s)), z.band, z.layers))

    def deliver(self):
        z = self.z
        shifts = range(1, z.sections)
        jobs = [[Copy(self.starts["deliver", s], z.slots, self.held)] for s in shifts]
        parts = self.run(jobs, "deliver")
        for s, part in zip(shifts, parts):
            self.held.append(Rows(self.order.arrived(z.to_section(part, s)), z.band, z.slots))

    def collect(self):
        z = self.z
        units = z.slots * z.sections
        (half,) = self.run([[Copy(self.starts["collect"], units, self.held)]], "collect")
        self.halves = (half, self.order.arrived(z.to_core(half)))


def per_device(
    weights,
    first_moment,
    second_moment,
    gradients,
    old_section,
    new_section,
    lost_pipe,
    donor_offset,
):
    z = Sizes(weights, new_section)
    order = Order()
    place = jnp.stack([lax.axis_index("pipe"), lax.axis_index("section")]).astype(jnp.int32)
    state = (weights[0, 0], first_moment[0, 0], second_moment[0, 0])
    grads = Gradients(z, order, gradients[0, 0])
    chunks = [Chunk(z, order, array) for array in state]
    table, starts = make_plan(z, place, old_section, new_section, lost_pipe, donor_offset)
    for part in (grads, *chunks):
        part.table, part.starts = table, starts

    for name in SEQUENCE:
        order.begin(name)
        if name[0] == "g" and name[1] in "esxgf":
            part = grads
            step = dict(e="enter", s="scatter", x="exchange", g="gather", f="finish")[name[1]]
        else:
            part = chunks[int(name[1])]
            step = dict(e="enter", s="spread", a="across", d="deliver", c="collect")[name[0]]
        if step == "enter":
            part.enter(place)
        else:
            getattr(part, step)()
    order.begin("u")
    rebuilt = [chunk.halves for chunk in chunks]
    outs = None
    for part in range(CORES):
        outs = update(z, order, table, starts["update"], part, state, rebuilt, grads.mean, outs)
    return tuple(out.reshape((1, 1, z.slots, z.rows, z.cols)) for out in outs)


def solution(mesh):
    split = P("pipe", "section", None, "tp", None)
    return jax.shard_map(
        per_device,
        mesh=mesh,
        in_specs=(split,) * 4 + (P(),) * 4,
        out_specs=(split,) * 3,
        check_vma=False,
    )
```

```python
import jax
import jax.numpy as jnp
from jax import lax
from jax.experimental import pallas as pl
from jax.experimental.pallas import tpu as pltpu
from jax.sharding import PartitionSpec as P

LEARN_RATE = 0.01
BETA_ONE = 0.9
BETA_TWO = 0.95
EPSILON = 1e-08
DECAY_RATE = 0.1

CORES = 2
SEQUENCE = (
    *("ge", "e0", "gs", "s0", "e1", "e2", "s1", "s2", "gx", "a0", "a1", "a2"),
    *("gg", "d0", "d1", "d2", "gf", "c0", "c1", "c2"),
)
AFTER = {}
VMEM = 24 * 1024 * 1024
AXES = ("pipe", "section")


def both(*terms):
    out = terms[0]
    for term in terms[1:]:
        out = jnp.logical_and(out, term)
    return out


def as_int(flag):
    return jnp.where(flag, 1, 0).astype(jnp.int32)


def total(terms):
    out = jnp.int32(0)
    for term in terms:
        out = out + term
    return out


class Sizes:
    def __init__(self, weights, new_section):
        self.pipes = lax.axis_size("pipe")
        self.sections = lax.axis_size("section")
        self.groups = self.pipes // CORES
        self.slots = weights.shape[2]
        self.rows = weights.shape[3]
        self.cols = weights.shape[4]
        self.layers = new_section.shape[0]
        self.half = self.rows // CORES
        self.band = self.half // self.sections
        self.grad_band = self.half // self.groups
        doubles = self.layers - self.sections
        widest = 0
        for at in range(self.sections):
            low = at + max(0, doubles - (self.sections - at))
            high = min(self.layers - self.sections + at, at + min(at, doubles) + 1)
            widest = max(widest, high - low + 1)
        self.channels = min(widest, CORES * self.slots)

    def send(self, value, target):
        pairs = []
        for pipe in range(self.pipes):
            for section in range(self.sections):
                group_to, core, to = target(pipe // CORES, pipe % CORES, section)
                pipe_to = group_to * CORES + core
                pairs.append((pipe * self.sections + section, pipe_to * self.sections + to))
        return lax.ppermute(value, AXES, pairs)

    def to_core(self, value):
        return self.send(value, lambda g, c, s: (g, 1 - c, s))

    def to_group(self, value, shift):
        return self.send(value, lambda g, c, s: ((g + shift) % self.groups, c, s))

    def to_section(self, value, shift):
        return self.send(value, lambda g, c, s: (g, c, (s + shift) % self.sections))


def plan_tables(z, pipe, section, old, new, lost_pipe, offset):
    layers = range(z.layers)
    lost = lost_pipe(0)
    group, core = pipe // CORES, pipe % CORES
    sibling = group * CORES + (1 - core)
    lost_group = lost // CORES
    tables = {}

    def now_of(at):
        return [jnp.where(at == lost, new(l), old(at, l)) for l in layers]

    def slots_of(sections):
        return [total(as_int(sections[k] == sections[l]) for k in range(l)) for l in layers]

    def layer_at(sections, slots, at, slot):
        hits = [both(sections[l] == at, slots[l] == slot) for l in layers]
        index = total(jnp.where(hits[l], l, 0) for l in layers)
        return index, total(as_int(hit) for hit in hits)

    def lookup(values, index):
        out = values[0]
        for l in layers[1:]:
            out = jnp.where(index == l, values[l], out)
        return out

    my_now = now_of(pipe)
    my_slot = slots_of(my_now)
    sib_now = now_of(sibling)
    sib_slot = slots_of(sib_now)
    new_list = [new(l) for l in layers]
    new_slot = slots_of(new_list)

    donor = [lost_pipe(offset(l)) for l in layers]
    source_section = [old(donor[l], l) for l in layers]
    source_slot = [
        total(as_int(old(donor[l], k) == source_section[l]) for k in range(l)) for l in layers
    ]
    source_group = [donor[l] // CORES for l in layers]
    crosses = [as_int(source_group[l] != lost_group) for l in layers]
    rank = [total(crosses[k] for k in range(l)) for l in layers]
    channel = [
        total(
            as_int(both(source_group[k] == source_group[l], source_section[k] == source_section[l]))
            for k in range(l)
        )
        for l in layers
    ]

    def grad_unit(l, band):
        return [
            (as_int(my_now[l] == section), (my_slot[l] * CORES + core) * z.groups + band),
            (as_int(sib_now[l] == section), sib_slot[l] * z.groups + band),
        ]

    for shift in range(1, z.groups):
        band = lax.rem(group + shift, z.groups)
        tables["grad_out", shift] = [grad_unit(l, band) for l in layers]
    tables["grad_sum"] = [grad_unit(l, group) + [(1, l)] * (z.groups - 1) for l in layers]
    tables["grad_mean"] = [[(1, l)] * z.sections for l in layers]
    for name, sections, slots in (("mine", my_now, my_slot), ("sibling", sib_now, sib_slot)):
        units = []
        for slot in range(z.slots):
            index, found = layer_at(sections, slots, section, slot)
            for band in range(z.groups):
                unit = []
                for shift in range(z.groups):
                    sender = lax.rem(group + z.groups - shift, z.groups)
                    unit.append((found * as_int(sender == band), index))
                units.append(unit)
        tables[name] = units

    here = [as_int(source_group[l] == group) for l in layers]
    my_chip = [here[l] * as_int(source_section[l] == section) for l in layers]
    from_me = [as_int(donor[l] == pipe) for l in layers]

    for shift in range(1, z.sections):
        band = lax.rem(section + shift, z.sections)
        units = []
        for k in range(z.channels):
            hit = [my_chip[l] * as_int(channel[l] == k) for l in layers]
            slot = total(hit[l] * source_slot[l] for l in layers)
            mine = total(hit[l] * from_me[l] for l in layers)
            found = total(hit)
            own = (slot * CORES + core) * z.sections + band
            units.append([(mine, own), (found - mine, slot * z.sections + band)])
        tables["spread", shift] = units

    def held(l_my_chip, l_from_me, l_slot, l_here, l_channel, l_section):
        own = (l_slot * CORES + core) * z.sections + section
        index = l_slot * z.sections + section
        unit = [(l_my_chip * l_from_me, own), (l_my_chip * (1 - l_from_me), index)]
        for shift in range(1, z.sections):
            sender = lax.rem(section + z.sections - shift, z.sections)
            unit.append((l_here * as_int(l_section == sender), l_channel))
        return unit

    def held_at(index):
        return held(
            *(
                lookup(values, index)
                for values in (my_chip, from_me, source_slot, here, channel, source_section)
            )
        )

    units = []
    for u in range(z.layers):
        hit = [crosses[l] * as_int(rank[l] == u) for l in layers]
        index = total(hit[l] * l for l in layers)
        found = total(hit)
        units.append([(flag * found, at) for flag, at in held_at(index)])
    tables["across"] = units

    def arrived(index, found):
        found = found * as_int(group == lost_group)
        unit = [(flag * found, at) for flag, at in held_at(index)]
        from_group = lookup(source_group, index)
        for shift in range(1, z.groups):
            sender = lax.rem(group + z.groups - shift, z.groups)
            unit.append((found * as_int(from_group == sender), lookup(rank, index)))
        return unit

    for shift in range(1, z.sections):
        target = lax.rem(section + shift, z.sections)
        tables["deliver", shift] = [
            arrived(*layer_at(new_list, new_slot, target, slot)) for slot in range(z.slots)
        ]
    units = []
    for slot in range(z.slots):
        own = arrived(*layer_at(new_list, new_slot, section, slot))
        for band in range(z.sections):
            mine = as_int(section == band)
            unit = [(flag * mine, at) for flag, at in own]
            for shift in range(1, z.sections):
                sender = lax.rem(section + z.sections - shift, z.sections)
                unit.append((as_int(both(sender == band, group == lost_group)), slot))
            units.append(unit)
    tables["collect"] = units

    last = [as_int(pipe == lost), core]
    for slot in range(z.slots):
        last.append(layer_at(my_now, my_slot, section, slot)[1])
    tables["update"] = [[tuple(last)]]
    return tables


def table_size(z):
    sources = z.sections + z.groups + z.sections + 2
    units = (z.sections + z.groups) * (4 * z.layers + 4 * z.slots)
    units += z.sections * (z.channels + 2 * z.slots) + z.layers
    return -(-(2 * units * sources + z.slots + 8) // 1024) * 1024


def make_plan(z, place, old_section, new_section, lost_pipe, donor_offset):
    starts = {}
    size = table_size(z)
    smem = pl.BlockSpec(memory_space=pltpu.SMEM)

    def kernel(place_ref, old_ref, new_ref, lost_ref, offset_ref, table_ref):
        tables = plan_tables(
            z,
            place_ref[0],
            place_ref[1],
            lambda at, l: old_ref[at, l],
            lambda l: new_ref[l],
            lambda rank: lost_ref[rank],
            lambda l: offset_ref[l],
        )
        at = 0
        for name, units in tables.items():
            starts[name] = at
            for unit in units:
                for entry in unit:
                    for value in entry:
                        table_ref[at] = jnp.int32(value)
                        at += 1
        assert at <= size

    table = pl.pallas_call(
        kernel,
        out_shape=jax.ShapeDtypeStruct((size,), jnp.int32),
        in_specs=[smem] * 5,
        out_specs=smem,
        name="plan",
    )(place, old_section, new_section, lost_pipe, donor_offset)
    return table, starts


SMEM_SPEC = pl.BlockSpec(memory_space=pltpu.SMEM)
VMEM_SPEC = pl.BlockSpec(memory_space=pltpu.VMEM)


def cost(operands, results):
    moved = sum(math.prod(a.shape) * a.dtype.itemsize for a in (*operands, *results))
    return pl.CostEstimate(flops=moved // 4, bytes_accessed=moved, transcendentals=0)


class Order:
    def __init__(self):
        self.results, self.last, self.name = {}, [], None

    def begin(self, name):
        self.name = name
        self.last = [self.results[at] for at in AFTER.get(name, ()) if at in self.results]

    def arrived(self, value):
        self.results[self.name + "r"] = value
        return value

    def specs(self):
        return [pl.BlockSpec(memory_space=pl.ANY)] * len(self.last)

    def then(self, result):
        self.results[self.name] = result[0]
        return result


SMEM_SPEC = pl.BlockSpec(memory_space=pltpu.SMEM)
VMEM_SPEC = pl.BlockSpec(memory_space=pltpu.VMEM)
PARAMS = pltpu.CompilerParams(vmem_limit_bytes=VMEM)
COST = pl.CostEstimate(flops=10**9, bytes_accessed=1, transcendentals=0)

UPDATE_COST = pl.CostEstimate(flops=1, bytes_accessed=1, transcendentals=0)


class Rows:
    def __init__(self, value, rows, count, arrays=1, base=0):
        self.value, self.rows, self.count = value, rows, count
        self.arrays, self.base = arrays, base

    def block(self, array, index):
        at = self.base + (array * self.count + index) * self.rows
        return pl.ds(at if isinstance(at, int) else pl.multiple_of(at, 16), self.rows)


class Copy:
    def __init__(self, start, units, sources):
        self.start, self.units, self.sources = start, units, sources
        self.arrays, self.rows = sources[0].arrays, sources[0].rows

    def write(self, table_ref, refs, out_ref, out):
        for unit in range(self.units):
            for at, source in enumerate(self.sources):
                entry = self.start + (unit * len(self.sources) + at) * 2

                @pl.when(table_ref[entry] != 0)
                def _(unit=unit, source=source, ref=refs[at], entry=entry):
                    index = table_ref[entry + 1]
                    for array in range(self.arrays):
                        block = ref[source.block(array, index)]
                        out_ref[out.block(array, unit)] = block.astype(out_ref.dtype)


class Sum:
    def __init__(self, start, units, sources):
        self.start, self.units, self.sources = start, units, sources
        self.arrays, self.rows = 1, sources[0].rows

    def write(self, table_ref, refs, out_ref, out):
        for unit in range(self.units):
            total_here = None
            for at, source in enumerate(self.sources):
                entry = self.start + (unit * len(self.sources) + at) * 2
                block = refs[at][source.block(0, table_ref[entry + 1])].astype(jnp.float32)
                block = jnp.where(table_ref[entry] != 0, block, 0.0)
                total_here = block if total_here is None else total_here + block
            out_ref[out.block(0, unit)] = total_here.astype(out_ref.dtype)


def stage(z, order, table, outputs, name):
    operands, slots = [], {}
    for job in (job for jobs in outputs for job in jobs):
        for source in job.sources:
            if id(source.value) not in slots:
                slots[id(source.value)] = len(operands)
                operands.append(source.value)
    places, shapes = [], []
    for jobs in outputs:
        at, row = [], 0
        for job in jobs:
            at.append(Rows(None, job.rows, job.units, job.arrays, row))
            row += job.arrays * job.units * job.rows
        places.append(at)
        shapes.append(jax.ShapeDtypeStruct((row, z.cols), jnp.bfloat16))

    def kernel(table_ref, *refs):
        out_refs = refs[-len(outputs) :]
        for jobs, at, out_ref in zip(outputs, places, out_refs):
            for job, place in zip(jobs, at):
                inputs = [refs[slots[id(source.value)]] for source in job.sources]
                job.write(table_ref, inputs, out_ref, place)

    call = pl.pallas_call(
        kernel,
        out_shape=tuple(shapes),
        in_specs=[SMEM_SPEC] + [VMEM_SPEC] * len(operands) + order.specs(),
        out_specs=tuple([VMEM_SPEC] * len(outputs)),
        compiler_params=PARAMS,
        cost_estimate=COST,
        name=name,
    )
    return order.then(call(table, *operands, *order.last))


def sibling_half(z, order, place, array, name):
    rows = z.half // 2 if z.half % 32 == 0 else z.half

    def kernel(place_ref, array_ref, *refs):
        out_ref = refs[-1]
        half = 1 - lax.rem(place_ref[0], CORES)
        for slot in range(z.slots):
            for first in range(0, z.half, rows):
                at = pl.multiple_of(slot * z.rows + half * z.half + first, 16)
                block = array_ref[pl.ds(at, rows)].astype(jnp.bfloat16)
                out_ref[pl.ds(slot * z.half + first, rows)] = block

    call = pl.pallas_call(
        kernel,
        out_shape=jax.ShapeDtypeStruct((z.slots * z.half, z.cols), jnp.bfloat16),
        in_specs=[SMEM_SPEC, VMEM_SPEC] + order.specs(),
        out_specs=VMEM_SPEC,
        compiler_params=PARAMS,
        cost_estimate=COST,
        name="halve_" + name,
    )
    return order.then((call(place, array, *order.last),))[0]


def update(z, order, table, start, part, state, rebuilt, mean, outs):
    views = [a.reshape(z.slots * z.rows, z.cols) for a in state]
    outs = [] if outs is None else list(outs)
    rows, cols = 16, min(z.cols, 128)

    def half_now(table_ref):
        core = table_ref[start + 1]
        return core if part == 0 else 1 - core

    def kernel(table_ref, *refs):
        local_refs, lost_refs, mean_ref = refs[:3], refs[3:6], refs[6]
        out_refs = refs[-3:]
        slot = pl.program_id(0)
        is_lost = table_ref[start] != 0
        found = table_ref[start + 2 + slot] != 0

        def each(sources, base):
            @pl.loop(0, z.half // rows)
            def _(at):
                row = pl.ds(pl.multiple_of(at * rows, rows), rows)
                mean_row = pl.ds(pl.multiple_of(slot * z.half + at * rows, rows), rows)
                from_row = pl.ds(pl.multiple_of(base + at * rows, rows), rows)
                for first in range(0, z.cols, cols):
                    lanes = pl.ds(first, cols)
                    weight, one, two = [
                        ref[from_row, lanes].astype(jnp.float32) for ref in sources
                    ]
                    grad = mean_ref[mean_row, lanes].astype(jnp.float32)
                    next_one = BETA_ONE * one + ((1.0 - BETA_ONE) / z.pipes) * grad
                    next_two = BETA_TWO * two + ((1.0 - BETA_TWO) / z.pipes**2) * (grad * grad)
                    scale = next_two * lax.rsqrt(next_two) + EPSILON
                    move = next_one * lax.rsqrt(scale * scale)
                    next_weight = (1.0 - LEARN_RATE * DECAY_RATE) * weight - LEARN_RATE * move
                    for ref, value in zip(out_refs, (next_weight, next_one, next_two)):
                        ref[0, 0, row, lanes] = value.astype(ref.dtype)

        @pl.when(both(found, is_lost))
        def _():
            each(lost_refs, slot * z.half)

        @pl.when(both(found, jnp.logical_not(is_lost)))
        def _():
            each(local_refs, slot * z.rows + half_now(table_ref) * z.half)

        @pl.when(jnp.logical_not(found))
        def _():
            for ref in out_refs:
                ref[...] = jnp.zeros(ref.shape, ref.dtype)

    block = (1, 1, z.half, z.cols)
    out_spec = pl.BlockSpec(block, lambda slot, table_ref: (slot, half_now(table_ref), 0, 0))
    shape = (z.slots, CORES, z.half, z.cols)
    call = pl.pallas_call(
        kernel,
        grid_spec=pltpu.PrefetchScalarGridSpec(
            num_scalar_prefetch=1,
            grid=(z.slots,),
            in_specs=[VMEM_SPEC] * 7
            + [pl.BlockSpec(memory_space=pl.ANY)] * len(outs)
            + order.specs(),
            out_specs=[out_spec] * 3,
        ),
        out_shape=(
            jax.ShapeDtypeStruct(shape, jnp.bfloat16),
            jax.ShapeDtypeStruct(shape, jnp.float32),
            jax.ShapeDtypeStruct(shape, jnp.float32),
        ),
        input_output_aliases={8 + at: at for at in range(len(outs))},
        compiler_params=PARAMS,
        cost_estimate=UPDATE_COST,
        name="update",
    )
    operands = (*views, *(half[part] for half in rebuilt), mean[part], *outs)
    return order.then(call(table, *operands, *order.last))


class Gradients:
    def __init__(self, z, order, grads):
        self.z, self.order, self.grads = z, order, grads

    def run(self, outputs, name):
        return stage(self.z, self.order, self.table, outputs, name)

    def rows(self, value):
        return Rows(value, self.z.grad_band, self.z.layers)

    def enter(self, place):
        z = self.z
        own = self.grads.reshape(z.slots * z.rows, z.cols)
        theirs = z.to_core(sibling_half(z, self.order, place, own, "gradients"))
        theirs = self.order.arrived(theirs)
        self.held = [
            Rows(own, z.grad_band, z.slots * CORES * z.groups),
            Rows(theirs, z.grad_band, z.slots * z.groups),
        ]

    def scatter(self):
        z = self.z
        shifts = range(1, z.groups)
        jobs = [[Sum(self.starts["grad_out", s], z.layers, self.held)] for s in shifts]
        parts = self.run(jobs, "grad_out")
        self.held += [
            self.rows(self.order.arrived(z.to_group(part, s))) for s, part in zip(shifts, parts)
        ]

    def exchange(self):
        z = self.z
        (part,) = self.run([[Sum(self.starts["grad_sum"], z.layers, self.held)]], "grad_sum")
        others = [self.order.arrived(z.to_section(part, s)) for s in range(1, z.sections)]
        self.held = [self.rows(value) for value in (part, *others)]

    def gather(self):
        z = self.z
        (part,) = self.run([[Sum(self.starts["grad_mean"], z.layers, self.held)]], "grad_mean")
        others = [self.order.arrived(z.to_group(part, s)) for s in range(1, z.groups)]
        self.held = [self.rows(value) for value in (part, *others)]

    def finish(self):
        z = self.z
        theirs, mine = self.run(
            [
                [Copy(self.starts[name], z.slots * z.groups, self.held)]
                for name in ("sibling", "mine")
            ],
            "mean",
        )
        self.mean = (mine, self.order.arrived(z.to_core(theirs)))


class Chunk:
    def __init__(self, z, order, array):
        self.z, self.order, self.array = z, order, array

    def run(self, outputs, name):
        return stage(self.z, self.order, self.table, outputs, name)

    def enter(self, place):
        z = self.z
        own = self.array.reshape(z.slots * z.rows, z.cols)
        theirs = z.to_core(sibling_half(z, self.order, place, own, "state"))
        theirs = self.order.arrived(theirs)
        held = z.slots * z.sections
        self.held = [Rows(own, z.band, CORES * held), Rows(theirs, z.band, held)]

    def spread(self):
        z = self.z
        shifts = range(1, z.sections)
        jobs = [[Copy(self.starts["spread", s], z.channels, self.held)] for s in shifts]
        parts = self.run(jobs, "spread")
        for s, part in zip(shifts, parts):
            self.held.append(Rows(self.order.arrived(z.to_section(part, s)), z.band, z.channels))

    def across(self):
        z = self.z
        (part,) = self.run([[Copy(self.starts["across"], z.layers, self.held)]], "across")
        for s in range(1, z.groups):
            self.held.append(Rows(self.order.arrived(z.to_group(part, s)), z.band, z.layers))

    def deliver(self):
        z = self.z
        shifts = range(1, z.sections)
        jobs = [[Copy(self.starts["deliver", s], z.slots, self.held)] for s in shifts]
        parts = self.run(jobs, "deliver")
        for s, part in zip(shifts, parts):
            self.held.append(Rows(self.order.arrived(z.to_section(part, s)), z.band, z.slots))

    def collect(self):
        z = self.z
        units = z.slots * z.sections
        (half,) = self.run([[Copy(self.starts["collect"], units, self.held)]], "collect")
        self.halves = (half, self.order.arrived(z.to_core(half)))


def per_device(
    weights,
    first_moment,
    second_moment,
    gradients,
    old_section,
    new_section,
    lost_pipe,
    donor_offset,
):
    z = Sizes(weights, new_section)
    order = Order()
    place = jnp.stack([lax.axis_index("pipe"), lax.axis_index("section")]).astype(jnp.int32)
    state = (weights[0, 0], first_moment[0, 0], second_moment[0, 0])
    grads = Gradients(z, order, gradients[0, 0])
    chunks = [Chunk(z, order, array) for array in state]
    table, starts = make_plan(z, place, old_section, new_section, lost_pipe, donor_offset)
    for part in (grads, *chunks):
        part.table, part.starts = table, starts

    for name in SEQUENCE:
        order.begin(name)
        if name[0] == "g" and name[1] in "esxgf":
            part = grads
            step = dict(e="enter", s="scatter", x="exchange", g="gather", f="finish")[name[1]]
        else:
            part = chunks[int(name[1])]
            step = dict(e="enter", s="spread", a="across", d="deliver", c="collect")[name[0]]
        if step == "enter":
            part.enter(place)
        else:
            getattr(part, step)()
    order.begin("u")
    rebuilt = [chunk.halves for chunk in chunks]
    outs = None
    for part in range(CORES):
        outs = update(z, order, table, starts["update"], part, state, rebuilt, grads.mean, outs)
    return tuple(out.reshape((1, 1, z.slots, z.rows, z.cols)) for out in outs)


def solution(mesh):
    split = P("pipe", "section", None, "tp", None)
    return jax.shard_map(
        per_device,
        mesh=mesh,
        in_specs=(split,) * 4 + (P(),) * 4,
        out_specs=(split,) * 3,
        check_vma=False,
    )
```

```python
import math

import jax
import jax.numpy as jnp
from jax import lax
from jax.experimental import pallas as pl
from jax.experimental.pallas import tpu as pltpu
from jax.sharding import PartitionSpec as P

LEARN_RATE = 0.01
BETA_ONE = 0.9
BETA_TWO = 0.95
EPSILON = 1e-08
DECAY_RATE = 0.1

CORES = 2
SEQUENCE = (
    *("ge", "e0", "gs", "s0", "e1", "e2", "s1", "s2", "gx", "a0", "a1", "a2"),
    *("gg", "d0", "d1", "d2", "gf", "c0", "c1", "c2"),
)
AFTER = {}
VMEM = 24 * 1024 * 1024
AXES = ("pipe", "section")


def both(*terms):
    out = terms[0]
    for term in terms[1:]:
        out = jnp.logical_and(out, term)
    return out


def as_int(flag):
    return jnp.where(flag, 1, 0).astype(jnp.int32)


def total(terms):
    out = jnp.int32(0)
    for term in terms:
        out = out + term
    return out


class Sizes:
    def __init__(self, weights, new_section):
        self.pipes = lax.axis_size("pipe")
        self.sections = lax.axis_size("section")
        self.groups = self.pipes // CORES
        self.slots = weights.shape[2]
        self.rows = weights.shape[3]
        self.cols = weights.shape[4]
        self.layers = new_section.shape[0]
        self.half = self.rows // CORES
        self.band = self.half // self.sections
        self.grad_band = self.half // self.groups
        doubles = self.layers - self.sections
        widest = 0
        for at in range(self.sections):
            low = at + max(0, doubles - (self.sections - at))
            high = min(self.layers - self.sections + at, at + min(at, doubles) + 1)
            widest = max(widest, high - low + 1)
        self.channels = min(widest, CORES * self.slots)

    def send(self, value, target):
        pairs = []
        for pipe in range(self.pipes):
            for section in range(self.sections):
                group_to, core, to = target(pipe // CORES, pipe % CORES, section)
                pipe_to = group_to * CORES + core
                pairs.append((pipe * self.sections + section, pipe_to * self.sections + to))
        return lax.ppermute(value, AXES, pairs)

    def to_core(self, value):
        return self.send(value, lambda g, c, s: (g, 1 - c, s))

    def to_group(self, value, shift):
        return self.send(value, lambda g, c, s: ((g + shift) % self.groups, c, s))

    def to_section(self, value, shift):
        return self.send(value, lambda g, c, s: (g, c, (s + shift) % self.sections))


def plan_tables(z, pipe, section, old, new, lost_pipe, offset):
    layers = range(z.layers)
    lost = lost_pipe(0)
    group, core = pipe // CORES, pipe % CORES
    sibling = group * CORES + (1 - core)
    lost_group = lost // CORES
    tables = {}

    def now_of(at):
        return [jnp.where(at == lost, new(l), old(at, l)) for l in layers]

    def slots_of(sections):
        return [total(as_int(sections[k] == sections[l]) for k in range(l)) for l in layers]

    def layer_at(sections, slots, at, slot):
        hits = [both(sections[l] == at, slots[l] == slot) for l in layers]
        index = total(jnp.where(hits[l], l, 0) for l in layers)
        return index, total(as_int(hit) for hit in hits)

    def lookup(values, index):
        out = values[0]
        for l in layers[1:]:
            out = jnp.where(index == l, values[l], out)
        return out

    my_now = now_of(pipe)
    my_slot = slots_of(my_now)
    sib_now = now_of(sibling)
    sib_slot = slots_of(sib_now)
    new_list = [new(l) for l in layers]
    new_slot = slots_of(new_list)

    donor = [lost_pipe(offset(l)) for l in layers]
    source_section = [old(donor[l], l) for l in layers]
    source_slot = [
        total(as_int(old(donor[l], k) == source_section[l]) for k in range(l)) for l in layers
    ]
    source_group = [donor[l] // CORES for l in layers]
    crosses = [as_int(source_group[l] != lost_group) for l in layers]
    rank = [total(crosses[k] for k in range(l)) for l in layers]
    channel = [
        total(
            as_int(both(source_group[k] == source_group[l], source_section[k] == source_section[l]))
            for k in range(l)
        )
        for l in layers
    ]

    def grad_unit(l, band):
        return [
            (as_int(my_now[l] == section), (my_slot[l] * CORES + core) * z.groups + band),
            (as_int(sib_now[l] == section), sib_slot[l] * z.groups + band),
        ]

    for shift in range(1, z.groups):
        band = lax.rem(group + shift, z.groups)
        tables["grad_out", shift] = [grad_unit(l, band) for l in layers]
    tables["grad_sum"] = [grad_unit(l, group) + [(1, l)] * (z.groups - 1) for l in layers]
    tables["grad_mean"] = [[(1, l)] * z.sections for l in layers]
    for name, sections, slots in (("mine", my_now, my_slot), ("sibling", sib_now, sib_slot)):
        units = []
        for slot in range(z.slots):
            index, found = layer_at(sections, slots, section, slot)
            for band in range(z.groups):
                unit = []
                for shift in range(z.groups):
                    sender = lax.rem(group + z.groups - shift, z.groups)
                    unit.append((found * as_int(sender == band), index))
                units.append(unit)
        tables[name] = units

    here = [as_int(source_group[l] == group) for l in layers]
    my_chip = [here[l] * as_int(source_section[l] == section) for l in layers]
    from_me = [as_int(donor[l] == pipe) for l in layers]

    for shift in range(1, z.sections):
        band = lax.rem(section + shift, z.sections)
        units = []
        for k in range(z.channels):
            hit = [my_chip[l] * as_int(channel[l] == k) for l in layers]
            slot = total(hit[l] * source_slot[l] for l in layers)
            mine = total(hit[l] * from_me[l] for l in layers)
            found = total(hit)
            own = (slot * CORES + core) * z.sections + band
            units.append([(mine, own), (found - mine, slot * z.sections + band)])
        tables["spread", shift] = units

    def held(l_my_chip, l_from_me, l_slot, l_here, l_channel, l_section):
        own = (l_slot * CORES + core) * z.sections + section
        index = l_slot * z.sections + section
        unit = [(l_my_chip * l_from_me, own), (l_my_chip * (1 - l_from_me), index)]
        for shift in range(1, z.sections):
            sender = lax.rem(section + z.sections - shift, z.sections)
            unit.append((l_here * as_int(l_section == sender), l_channel))
        return unit

    def held_at(index):
        return held(
            *(
                lookup(values, index)
                for values in (my_chip, from_me, source_slot, here, channel, source_section)
            )
        )

    units = []
    for u in range(z.layers):
        hit = [crosses[l] * as_int(rank[l] == u) for l in layers]
        index = total(hit[l] * l for l in layers)
        found = total(hit)
        units.append([(flag * found, at) for flag, at in held_at(index)])
    tables["across"] = units

    def arrived(index, found):
        found = found * as_int(group == lost_group)
        unit = [(flag * found, at) for flag, at in held_at(index)]
        from_group = lookup(source_group, index)
        for shift in range(1, z.groups):
            sender = lax.rem(group + z.groups - shift, z.groups)
            unit.append((found * as_int(from_group == sender), lookup(rank, index)))
        return unit

    for shift in range(1, z.sections):
        target = lax.rem(section + shift, z.sections)
        tables["deliver", shift] = [
            arrived(*layer_at(new_list, new_slot, target, slot)) for slot in range(z.slots)
        ]
    units = []
    for slot in range(z.slots):
        own = arrived(*layer_at(new_list, new_slot, section, slot))
        for band in range(z.sections):
            mine = as_int(section == band)
            unit = [(flag * mine, at) for flag, at in own]
            for shift in range(1, z.sections):
                sender = lax.rem(section + z.sections - shift, z.sections)
                unit.append((as_int(both(sender == band, group == lost_group)), slot))
            units.append(unit)
    tables["collect"] = units

    last = [as_int(pipe == lost), core]
    for slot in range(z.slots):
        last.append(layer_at(my_now, my_slot, section, slot)[1])
    tables["update"] = [[tuple(last)]]
    return tables


def table_size(z):
    sources = z.sections + z.groups + z.sections + 2
    units = (z.sections + z.groups) * (4 * z.layers + 4 * z.slots)
    units += z.sections * (z.channels + 2 * z.slots) + z.layers
    return -(-(2 * units * sources + z.slots + 8) // 1024) * 1024


def make_plan(z, place, old_section, new_section, lost_pipe, donor_offset):
    starts = {}
    size = table_size(z)
    smem = pl.BlockSpec(memory_space=pltpu.SMEM)

    def kernel(place_ref, old_ref, new_ref, lost_ref, offset_ref, table_ref):
        tables = plan_tables(
            z,
            place_ref[0],
            place_ref[1],
            lambda at, l: old_ref[at, l],
            lambda l: new_ref[l],
            lambda rank: lost_ref[rank],
            lambda l: offset_ref[l],
        )
        at = 0
        for name, units in tables.items():
            starts[name] = at
            for unit in units:
                for entry in unit:
                    for value in entry:
                        table_ref[at] = jnp.int32(value)
                        at += 1
        assert at <= size

    table = pl.pallas_call(
        kernel,
        out_shape=jax.ShapeDtypeStruct((size,), jnp.int32),
        in_specs=[smem] * 5,
        out_specs=smem,
        name="plan",
    )(place, old_section, new_section, lost_pipe, donor_offset)
    return table, starts


SMEM_SPEC = pl.BlockSpec(memory_space=pltpu.SMEM)
VMEM_SPEC = pl.BlockSpec(memory_space=pltpu.VMEM)


def cost(operands, results):
    moved = sum(math.prod(a.shape) * a.dtype.itemsize for a in (*operands, *results))
    return pl.CostEstimate(flops=moved // 4, bytes_accessed=moved, transcendentals=0)


class Order:
    def __init__(self):
        self.results, self.last, self.name = {}, [], None

    def begin(self, name):
        self.name = name
        self.last = [self.results[at] for at in AFTER.get(name, ()) if at in self.results]

    def arrived(self, value):
        self.results[self.name + "r"] = value
        return value

    def specs(self):
        return [pl.BlockSpec(memory_space=pl.ANY)] * len(self.last)

    def then(self, result):
        self.results[self.name] = result[0]
        return result


SMEM_SPEC = pl.BlockSpec(memory_space=pltpu.SMEM)
VMEM_SPEC = pl.BlockSpec(memory_space=pltpu.VMEM)
PARAMS = pltpu.CompilerParams(vmem_limit_bytes=VMEM)
COST = pl.CostEstimate(flops=10**9, bytes_accessed=1, transcendentals=0)

UPDATE_COST = pl.CostEstimate(flops=1, bytes_accessed=1, transcendentals=0)


class Rows:
    def __init__(self, value, rows, count, arrays=1, base=0):
        self.value, self.rows, self.count = value, rows, count
        self.arrays, self.base = arrays, base

    def part(self, array, index, first, rows):
        at = self.base + (array * self.count + index) * self.rows + first
        return pl.ds(pl.multiple_of(at, 16), rows)


class Copy:
    def __init__(self, start, units, sources):
        self.start, self.units, self.sources = start, units, sources
        self.arrays, self.rows = sources[0].arrays, sources[0].rows

    def write(self, table_ref, refs, out_ref, out):
        for unit in range(self.units):
            for at, source in enumerate(self.sources):
                entry = self.start + (unit * len(self.sources) + at) * 2

                @pl.when(table_ref[entry] != 0)
                def _(unit=unit, source=source, ref=refs[at], entry=entry):
                    index = table_ref[entry + 1]
                    step = math.gcd(self.rows, 64)
                    for array in range(self.arrays):

                        @pl.loop(0, self.rows // step)
                        def _(at):
                            block = ref[source.part(array, index, at * step, step)]
                            place = out.part(array, unit, at * step, step)
                            out_ref[place] = block.astype(out_ref.dtype)


class Sum:
    def __init__(self, start, units, sources):
        self.start, self.units, self.sources = start, units, sources
        self.arrays, self.rows = 1, sources[0].rows

    def write(self, table_ref, refs, out_ref, out):
        step = math.gcd(self.rows, 32)
        for unit in range(self.units):
            entries = [
                self.start + (unit * len(self.sources) + at) * 2
                for at in range(len(self.sources))
            ]
            flags = [table_ref[entry] != 0 for entry in entries]
            places = [table_ref[entry + 1] for entry in entries]

            @pl.loop(0, self.rows // step)
            def _(at, unit=unit, flags=flags, places=places):
                total_here = None
                for source, ref, flag, index in zip(self.sources, refs, flags, places):
                    block = ref[source.part(0, index, at * step, step)].astype(jnp.float32)
                    block = jnp.where(flag, block, 0.0)
                    total_here = block if total_here is None else total_here + block
                out_ref[out.part(0, unit, at * step, step)] = total_here.astype(out_ref.dtype)


def stage(z, order, table, outputs, name):
    operands, slots = [], {}
    for job in (job for jobs in outputs for job in jobs):
        for source in job.sources:
            if id(source.value) not in slots:
                slots[id(source.value)] = len(operands)
                operands.append(source.value)
    places, shapes = [], []
    for jobs in outputs:
        at, row = [], 0
        for job in jobs:
            at.append(Rows(None, job.rows, job.units, job.arrays, row))
            row += job.arrays * job.units * job.rows
        places.append(at)
        shapes.append(jax.ShapeDtypeStruct((row, z.cols), jnp.bfloat16))

    def kernel(table_ref, *refs):
        out_refs = refs[-len(outputs) :]
        for jobs, at, out_ref in zip(outputs, places, out_refs):
            for job, place in zip(jobs, at):
                inputs = [refs[slots[id(source.value)]] for source in job.sources]
                job.write(table_ref, inputs, out_ref, place)

    call = pl.pallas_call(
        kernel,
        out_shape=tuple(shapes),
        in_specs=[SMEM_SPEC] + [VMEM_SPEC] * len(operands) + order.specs(),
        out_specs=tuple([VMEM_SPEC] * len(outputs)),
        compiler_params=PARAMS,
        cost_estimate=COST,
        name=name,
    )
    return order.then(call(table, *operands, *order.last))


def sibling_half(z, order, place, array, name):
    view = array.reshape(z.slots, CORES, z.half, z.cols)

    step = math.gcd(z.half, 64)

    def kernel(place_ref, array_ref, *refs):
        @pl.loop(0, z.half // step)
        def _(at):
            rows = pl.ds(pl.multiple_of(at * step, 16), step)
            refs[-1][rows] = array_ref[0, 0, rows].astype(jnp.bfloat16)

    def half_of(slot, place_ref):
        return (slot, 1 - lax.rem(place_ref[0], CORES), 0, 0)

    out = jax.ShapeDtypeStruct((z.slots * z.half, z.cols), jnp.bfloat16)
    call = pl.pallas_call(
        kernel,
        grid_spec=pltpu.PrefetchScalarGridSpec(
            num_scalar_prefetch=1,
            grid=(z.slots,),
            in_specs=[pl.BlockSpec((1, 1, z.half, z.cols), half_of)] + order.specs(),
            out_specs=pl.BlockSpec((z.half, z.cols), lambda slot, place_ref: (slot, 0)),
        ),
        out_shape=out,
        compiler_params=PARAMS,
        cost_estimate=COST,
        name="halve_" + name,
    )
    return order.then((call(place, view, *order.last),))[0]


def update(z, order, table, start, part, state, rebuilt, mean, outs):
    views = [a.reshape(z.slots * z.rows, z.cols) for a in state]
    outs = [] if outs is None else list(outs)
    rows, cols = 16, min(z.cols, 128)
    unroll = math.gcd(z.half // rows, 4)

    def half_now(table_ref):
        core = table_ref[start + 1]
        return core if part == 0 else 1 - core

    def kernel(table_ref, *refs):
        local_refs, lost_refs, mean_ref = refs[:3], refs[3:6], refs[6]
        out_refs = refs[-3:]
        slot = pl.program_id(0)
        is_lost = table_ref[start] != 0
        found = table_ref[start + 2 + slot] != 0

        def each(sources, base):
            @pl.loop(0, z.half // (rows * unroll))
            def _(at):
                for first in range(unroll):
                    for lane in range(0, z.cols, cols):
                        one_block(sources, base, (at * unroll + first) * rows, lane)

        def one_block(sources, base, at, lane):
            row = pl.ds(pl.multiple_of(at, rows), rows)
            mean_row = pl.ds(pl.multiple_of(slot * z.half + at, rows), rows)
            from_row = pl.ds(pl.multiple_of(base + at, rows), rows)
            lanes = pl.ds(lane, cols)
            weight, one, two = [ref[from_row, lanes].astype(jnp.float32) for ref in sources]
            grad = mean_ref[mean_row, lanes].astype(jnp.float32)
            next_one = BETA_ONE * one + ((1.0 - BETA_ONE) / z.pipes) * grad
            next_two = BETA_TWO * two + ((1.0 - BETA_TWO) / z.pipes**2) * (grad * grad)
            scale = next_two * lax.rsqrt(next_two) + EPSILON
            move = next_one * lax.rsqrt(scale * scale)
            next_weight = (1.0 - LEARN_RATE * DECAY_RATE) * weight - LEARN_RATE * move
            for ref, value in zip(out_refs, (next_weight, next_one, next_two)):
                ref[0, 0, row, lanes] = value.astype(ref.dtype)

        @pl.when(both(found, is_lost))
        def _():
            each(lost_refs, slot * z.half)

        @pl.when(both(found, jnp.logical_not(is_lost)))
        def _():
            each(local_refs, slot * z.rows + half_now(table_ref) * z.half)

        @pl.when(jnp.logical_not(found))
        def _():
            @pl.loop(0, z.half // rows)
            def _(at):
                for ref in out_refs:
                    row = pl.ds(pl.multiple_of(at * rows, rows), rows)
                    ref[0, 0, row] = jnp.zeros((rows, z.cols), ref.dtype)

    block = (1, 1, z.half, z.cols)
    out_spec = pl.BlockSpec(block, lambda slot, table_ref: (slot, half_now(table_ref), 0, 0))
    shape = (z.slots, CORES, z.half, z.cols)
    call = pl.pallas_call(
        kernel,
        grid_spec=pltpu.PrefetchScalarGridSpec(
            num_scalar_prefetch=1,
            grid=(z.slots,),
            in_specs=[VMEM_SPEC] * 7
            + [pl.BlockSpec(memory_space=pl.ANY)] * len(outs)
            + order.specs(),
            out_specs=[out_spec] * 3,
        ),
        out_shape=(
            jax.ShapeDtypeStruct(shape, jnp.bfloat16),
            jax.ShapeDtypeStruct(shape, jnp.float32),
            jax.ShapeDtypeStruct(shape, jnp.float32),
        ),
        input_output_aliases={8 + at: at for at in range(len(outs))},
        compiler_params=PARAMS,
        cost_estimate=UPDATE_COST,
        name="update",
    )
    operands = (*views, *(half[part] for half in rebuilt), mean[part], *outs)
    return order.then(call(table, *operands, *order.last))


class Gradients:
    def __init__(self, z, order, grads):
        self.z, self.order, self.grads = z, order, grads

    def run(self, outputs, name):
        return stage(self.z, self.order, self.table, outputs, name)

    def rows(self, value):
        return Rows(value, self.z.grad_band, self.z.layers)

    def enter(self, place):
        z = self.z
        theirs = z.to_core(sibling_half(z, self.order, place, self.grads, "gradients"))
        own = self.grads.reshape(z.slots * z.rows, z.cols)
        theirs = self.order.arrived(theirs)
        self.held = [
            Rows(own, z.grad_band, z.slots * CORES * z.groups),
            Rows(theirs, z.grad_band, z.slots * z.groups),
        ]

    def scatter(self):
        z = self.z
        shifts = range(1, z.groups)
        jobs = [[Sum(self.starts["grad_out", s], z.layers, self.held)] for s in shifts]
        parts = self.run(jobs, "grad_out")
        self.held += [
            self.rows(self.order.arrived(z.to_group(part, s))) for s, part in zip(shifts, parts)
        ]

    def exchange(self):
        z = self.z
        (part,) = self.run([[Sum(self.starts["grad_sum"], z.layers, self.held)]], "grad_sum")
        others = [self.order.arrived(z.to_section(part, s)) for s in range(1, z.sections)]
        self.held = [self.rows(value) for value in (part, *others)]

    def gather(self):
        z = self.z
        (part,) = self.run([[Sum(self.starts["grad_mean"], z.layers, self.held)]], "grad_mean")
        others = [self.order.arrived(z.to_group(part, s)) for s in range(1, z.groups)]
        self.held = [self.rows(value) for value in (part, *others)]

    def finish(self):
        z = self.z
        theirs, mine = self.run(
            [
                [Copy(self.starts[name], z.slots * z.groups, self.held)]
                for name in ("sibling", "mine")
            ],
            "mean",
        )
        self.mean = (mine, self.order.arrived(z.to_core(theirs)))


class Chunk:
    def __init__(self, z, order, array):
        self.z, self.order, self.array = z, order, array

    def run(self, outputs, name):
        return stage(self.z, self.order, self.table, outputs, name)

    def enter(self, place):
        z = self.z
        theirs = z.to_core(sibling_half(z, self.order, place, self.array, "state"))
        own = self.array.reshape(z.slots * z.rows, z.cols)
        theirs = self.order.arrived(theirs)
        held = z.slots * z.sections
        self.held = [Rows(own, z.band, CORES * held), Rows(theirs, z.band, held)]

    def spread(self):
        z = self.z
        shifts = range(1, z.sections)
        jobs = [[Copy(self.starts["spread", s], z.channels, self.held)] for s in shifts]
        parts = self.run(jobs, "spread")
        for s, part in zip(shifts, parts):
            self.held.append(Rows(self.order.arrived(z.to_section(part, s)), z.band, z.channels))

    def across(self):
        z = self.z
        (part,) = self.run([[Copy(self.starts["across"], z.layers, self.held)]], "across")
        for s in range(1, z.groups):
            self.held.append(Rows(self.order.arrived(z.to_group(part, s)), z.band, z.layers))

    def deliver(self):
        z = self.z
        shifts = range(1, z.sections)
        jobs = [[Copy(self.starts["deliver", s], z.slots, self.held)] for s in shifts]
        parts = self.run(jobs, "deliver")
        for s, part in zip(shifts, parts):
            self.held.append(Rows(self.order.arrived(z.to_section(part, s)), z.band, z.slots))

    def collect(self):
        z = self.z
        units = z.slots * z.sections
        (half,) = self.run([[Copy(self.starts["collect"], units, self.held)]], "collect")
        self.halves = (half, self.order.arrived(z.to_core(half)))


def per_device(
    weights,
    first_moment,
    second_moment,
    gradients,
    old_section,
    new_section,
    lost_pipe,
    donor_offset,
):
    z = Sizes(weights, new_section)
    order = Order()
    place = jnp.stack([lax.axis_index("pipe"), lax.axis_index("section")]).astype(jnp.int32)
    state = (weights[0, 0], first_moment[0, 0], second_moment[0, 0])
    grads = Gradients(z, order, gradients[0, 0])
    chunks = [Chunk(z, order, array) for array in state]
    table, starts = make_plan(z, place, old_section, new_section, lost_pipe, donor_offset)
    for part in (grads, *chunks):
        part.table, part.starts = table, starts

    for name in SEQUENCE:
        order.begin(name)
        if name[0] == "g" and name[1] in "esxgf":
            part = grads
            step = dict(e="enter", s="scatter", x="exchange", g="gather", f="finish")[name[1]]
        else:
            part = chunks[int(name[1])]
            step = dict(e="enter", s="spread", a="across", d="deliver", c="collect")[name[0]]
        if step == "enter":
            part.enter(place)
        else:
            getattr(part, step)()
    order.begin("u")
    rebuilt = [chunk.halves for chunk in chunks]
    outs = None
    for part in range(CORES):
        outs = update(z, order, table, starts["update"], part, state, rebuilt, grads.mean, outs)
    return tuple(out.reshape((1, 1, z.slots, z.rows, z.cols)) for out in outs)


def solution(mesh):
    split = P("pipe", "section", None, "tp", None)
    return jax.shard_map(
        per_device,
        mesh=mesh,
        in_specs=(split,) * 4 + (P(),) * 4,
        out_specs=(split,) * 3,
        check_vma=False,
    )
```

```python
import math

import jax
import jax.numpy as jnp
from jax import lax
from jax.experimental import pallas as pl
from jax.experimental.pallas import tpu as pltpu
from jax.sharding import PartitionSpec as P

LEARN_RATE = 0.01
BETA_ONE = 0.9
BETA_TWO = 0.95
EPSILON = 1e-08
DECAY_RATE = 0.1

CORES = 2
SEQUENCE = (
    *("ge", "e0", "gs", "s0", "e1", "e2", "s1", "s2", "gx", "a0", "a1", "a2"),
    *("gg", "d0", "d1", "d2", "gf", "c0", "c1", "c2"),
)
AFTER = {}
VMEM = 24 * 1024 * 1024
AXES = ("pipe", "section")


def both(*terms):
    out = terms[0]
    for term in terms[1:]:
        out = jnp.logical_and(out, term)
    return out


def as_int(flag):
    return jnp.where(flag, 1, 0).astype(jnp.int32)


def total(terms):
    out = jnp.int32(0)
    for term in terms:
        out = out + term
    return out


class Sizes:
    def __init__(self, weights, new_section):
        self.pipes = lax.axis_size("pipe")
        self.sections = lax.axis_size("section")
        self.groups = self.pipes // CORES
        self.slots = weights.shape[2]
        self.rows = weights.shape[3]
        self.cols = weights.shape[4]
        self.layers = new_section.shape[0]
        self.half = self.rows // CORES
        self.band = self.half // self.sections
        self.grad_band = self.half // self.groups
        doubles = self.layers - self.sections
        widest = 0
        for at in range(self.sections):
            low = at + max(0, doubles - (self.sections - at))
            high = min(self.layers - self.sections + at, at + min(at, doubles) + 1)
            widest = max(widest, high - low + 1)
        self.channels = min(widest, CORES * self.slots)

    def send(self, value, target):
        pairs = []
        for pipe in range(self.pipes):
            for section in range(self.sections):
                group_to, core, to = target(pipe // CORES, pipe % CORES, section)
                pipe_to = group_to * CORES + core
                pairs.append((pipe * self.sections + section, pipe_to * self.sections + to))
        return lax.ppermute(value, AXES, pairs)

    def to_core(self, value):
        return self.send(value, lambda g, c, s: (g, 1 - c, s))

    def to_group(self, value, shift):
        return self.send(value, lambda g, c, s: ((g + shift) % self.groups, c, s))

    def to_section(self, value, shift):
        return self.send(value, lambda g, c, s: (g, c, (s + shift) % self.sections))


def plan_tables(z, pipe, section, old, new, lost_pipe, offset):
    layers = range(z.layers)
    lost = lost_pipe(0)
    group, core = pipe // CORES, pipe % CORES
    sibling = group * CORES + (1 - core)
    lost_group = lost // CORES
    tables = {}

    def now_of(at):
        return [jnp.where(at == lost, new(l), old(at, l)) for l in layers]

    def slots_of(sections):
        return [total(as_int(sections[k] == sections[l]) for k in range(l)) for l in layers]

    def layer_at(sections, slots, at, slot):
        hits = [both(sections[l] == at, slots[l] == slot) for l in layers]
        index = total(jnp.where(hits[l], l, 0) for l in layers)
        return index, total(as_int(hit) for hit in hits)

    def lookup(values, index):
        out = values[0]
        for l in layers[1:]:
            out = jnp.where(index == l, values[l], out)
        return out

    my_now = now_of(pipe)
    my_slot = slots_of(my_now)
    sib_now = now_of(sibling)
    sib_slot = slots_of(sib_now)
    new_list = [new(l) for l in layers]
    new_slot = slots_of(new_list)

    donor = [lost_pipe(offset(l)) for l in layers]
    source_section = [old(donor[l], l) for l in layers]
    source_slot = [
        total(as_int(old(donor[l], k) == source_section[l]) for k in range(l)) for l in layers
    ]
    source_group = [donor[l] // CORES for l in layers]
    crosses = [as_int(source_group[l] != lost_group) for l in layers]
    rank = [total(crosses[k] for k in range(l)) for l in layers]
    channel = [
        total(
            as_int(both(source_group[k] == source_group[l], source_section[k] == source_section[l]))
            for k in range(l)
        )
        for l in layers
    ]

    def grad_unit(l, band):
        return [
            (as_int(my_now[l] == section), my_slot[l] * z.groups + band),
            (as_int(sib_now[l] == section), sib_slot[l] * z.groups + band),
        ]

    for shift in range(1, z.groups):
        band = lax.rem(group + shift, z.groups)
        tables["grad_out", shift] = [grad_unit(l, band) for l in layers]
    tables["grad_sum"] = [grad_unit(l, group) + [(1, l)] * (z.groups - 1) for l in layers]
    tables["grad_mean"] = [[(1, l)] * z.sections for l in layers]
    for name, sections, slots in (("mine", my_now, my_slot), ("sibling", sib_now, sib_slot)):
        units = []
        for slot in range(z.slots):
            index, found = layer_at(sections, slots, section, slot)
            for band in range(z.groups):
                unit = []
                for shift in range(z.groups):
                    sender = lax.rem(group + z.groups - shift, z.groups)
                    unit.append((found * as_int(sender == band), index))
                units.append(unit)
        tables[name] = units

    here = [as_int(source_group[l] == group) for l in layers]
    my_chip = [here[l] * as_int(source_section[l] == section) for l in layers]
    from_me = [as_int(donor[l] == pipe) for l in layers]

    for shift in range(1, z.sections):
        band = lax.rem(section + shift, z.sections)
        units = []
        for k in range(z.channels):
            hit = [my_chip[l] * as_int(channel[l] == k) for l in layers]
            slot = total(hit[l] * source_slot[l] for l in layers)
            mine = total(hit[l] * from_me[l] for l in layers)
            found = total(hit)
            own = (slot * CORES + core) * z.sections + band
            units.append([(mine, own), (found - mine, slot * z.sections + band)])
        tables["spread", shift] = units

    def held(l_my_chip, l_from_me, l_slot, l_here, l_channel, l_section):
        own = (l_slot * CORES + core) * z.sections + section
        index = l_slot * z.sections + section
        unit = [(l_my_chip * l_from_me, own), (l_my_chip * (1 - l_from_me), index)]
        for shift in range(1, z.sections):
            sender = lax.rem(section + z.sections - shift, z.sections)
            unit.append((l_here * as_int(l_section == sender), l_channel))
        return unit

    def held_at(index):
        return held(
            *(
                lookup(values, index)
                for values in (my_chip, from_me, source_slot, here, channel, source_section)
            )
        )

    units = []
    for u in range(z.layers):
        hit = [crosses[l] * as_int(rank[l] == u) for l in layers]
        index = total(hit[l] * l for l in layers)
        found = total(hit)
        units.append([(flag * found, at) for flag, at in held_at(index)])
    tables["across"] = units

    def arrived(index, found):
        found = found * as_int(group == lost_group)
        unit = [(flag * found, at) for flag, at in held_at(index)]
        from_group = lookup(source_group, index)
        for shift in range(1, z.groups):
            sender = lax.rem(group + z.groups - shift, z.groups)
            unit.append((found * as_int(from_group == sender), lookup(rank, index)))
        return unit

    for shift in range(1, z.sections):
        target = lax.rem(section + shift, z.sections)
        tables["deliver", shift] = [
            arrived(*layer_at(new_list, new_slot, target, slot)) for slot in range(z.slots)
        ]
    units = []
    for slot in range(z.slots):
        own = arrived(*layer_at(new_list, new_slot, section, slot))
        for band in range(z.sections):
            mine = as_int(section == band)
            unit = [(flag * mine, at) for flag, at in own]
            for shift in range(1, z.sections):
                sender = lax.rem(section + z.sections - shift, z.sections)
                unit.append((as_int(both(sender == band, group == lost_group)), slot))
            units.append(unit)
    tables["collect"] = units

    last = [as_int(pipe == lost), core]
    for slot in range(z.slots):
        last.append(layer_at(my_now, my_slot, section, slot)[1])
    tables["update"] = [[tuple(last)]]
    return tables


def table_size(z):
    held = z.sections + 1
    arrived = held + z.groups - 1
    entries = z.layers * (2 * (z.groups - 1) + z.groups + 1 + z.sections + held)
    entries += 2 * z.slots * z.groups**2 + 2 * (z.sections - 1) * z.channels
    entries += z.slots * (z.sections - 1) * arrived
    entries += z.slots * z.sections * (arrived + z.sections - 1)
    return -(-(2 * entries + z.slots + 2) // 256) * 256


def make_plan(z, place, old_section, new_section, lost_pipe, donor_offset):
    starts = {}
    size = table_size(z)
    smem = pl.BlockSpec(memory_space=pltpu.SMEM)

    def kernel(place_ref, old_ref, new_ref, lost_ref, offset_ref, table_ref):
        tables = plan_tables(
            z,
            place_ref[0],
            place_ref[1],
            lambda at, l: old_ref[at, l],
            lambda l: new_ref[l],
            lambda rank: lost_ref[rank],
            lambda l: offset_ref[l],
        )
        at = 0
        for name, units in tables.items():
            starts[name] = at
            for unit in units:
                for entry in unit:
                    for value in entry:
                        table_ref[at] = jnp.int32(value)
                        at += 1
        assert at <= size

    table = pl.pallas_call(
        kernel,
        out_shape=jax.ShapeDtypeStruct((size,), jnp.int32),
        in_specs=[smem] * 5,
        out_specs=smem,
        name="plan",
    )(place, old_section, new_section, lost_pipe, donor_offset)
    return table, starts


SMEM_SPEC = pl.BlockSpec(memory_space=pltpu.SMEM)
VMEM_SPEC = pl.BlockSpec(memory_space=pltpu.VMEM)


def cost(operands, results):
    moved = sum(math.prod(a.shape) * a.dtype.itemsize for a in (*operands, *results))
    return pl.CostEstimate(flops=moved // 4, bytes_accessed=moved, transcendentals=0)


class Order:
    def __init__(self):
        self.results, self.last, self.name = {}, [], None

    def begin(self, name):
        self.name = name
        self.last = [self.results[at] for at in AFTER.get(name, ()) if at in self.results]

    def arrived(self, value):
        self.results[self.name + "r"] = value
        return value

    def specs(self):
        return [pl.BlockSpec(memory_space=pl.ANY)] * len(self.last)

    def then(self, result):
        self.results[self.name] = result[0]
        return result


SMEM_SPEC = pl.BlockSpec(memory_space=pltpu.SMEM)
VMEM_SPEC = pl.BlockSpec(memory_space=pltpu.VMEM)
PARAMS = pltpu.CompilerParams(vmem_limit_bytes=VMEM)
COST = pl.CostEstimate(flops=10**9, bytes_accessed=1, transcendentals=0)

UPDATE_COST = pl.CostEstimate(flops=1, bytes_accessed=1, transcendentals=0)


class Rows:
    def __init__(self, value, rows, count, arrays=1, base=0):
        self.value, self.rows, self.count = value, rows, count
        self.arrays, self.base = arrays, base

    def part(self, array, index, first, rows):
        at = self.base + (array * self.count + index) * self.rows + first
        return pl.ds(pl.multiple_of(at, 16), rows)


class Copy:
    def __init__(self, start, units, sources):
        self.start, self.units, self.sources = start, units, sources
        self.arrays, self.rows = sources[0].arrays, sources[0].rows

    def write(self, table_ref, refs, out_ref, out):
        for unit in range(self.units):
            for at, source in enumerate(self.sources):
                entry = self.start + (unit * len(self.sources) + at) * 2

                @pl.when(table_ref[entry] != 0)
                def _(unit=unit, source=source, ref=refs[at], entry=entry):
                    index = table_ref[entry + 1]
                    step = math.gcd(self.rows, 64)
                    for array in range(self.arrays):

                        @pl.loop(0, self.rows // step)
                        def _(at):
                            block = ref[source.part(array, index, at * step, step)]
                            place = out.part(array, unit, at * step, step)
                            out_ref[place] = block.astype(out_ref.dtype)


class Sum:
    def __init__(self, start, units, sources):
        self.start, self.units, self.sources = start, units, sources
        self.arrays, self.rows = 1, sources[0].rows

    def write(self, table_ref, refs, out_ref, out):
        step = math.gcd(self.rows, 32)
        for unit in range(self.units):
            entries = [
                self.start + (unit * len(self.sources) + at) * 2
                for at in range(len(self.sources))
            ]
            flags = [table_ref[entry] != 0 for entry in entries]
            places = [table_ref[entry + 1] for entry in entries]

            @pl.loop(0, self.rows // step)
            def _(at, unit=unit, flags=flags, places=places):
                total_here = None
                for source, ref, flag, index in zip(self.sources, refs, flags, places):
                    block = ref[source.part(0, index, at * step, step)].astype(jnp.float32)
                    block = jnp.where(flag, block, 0.0)
                    total_here = block if total_here is None else total_here + block
                out_ref[out.part(0, unit, at * step, step)] = total_here.astype(out_ref.dtype)


def stage(z, order, table, outputs, name):
    operands, slots = [], {}
    for job in (job for jobs in outputs for job in jobs):
        for source in job.sources:
            if id(source.value) not in slots:
                slots[id(source.value)] = len(operands)
                operands.append(source.value)
    places, shapes = [], []
    for jobs in outputs:
        at, row = [], 0
        for job in jobs:
            at.append(Rows(None, job.rows, job.units, job.arrays, row))
            row += job.arrays * job.units * job.rows
        places.append(at)
        shapes.append(jax.ShapeDtypeStruct((row, z.cols), jnp.bfloat16))

    def kernel(table_ref, *refs):
        out_refs = refs[-len(outputs) :]
        for jobs, at, out_ref in zip(outputs, places, out_refs):
            for job, place in zip(jobs, at):
                inputs = [refs[slots[id(source.value)]] for source in job.sources]
                job.write(table_ref, inputs, out_ref, place)

    call = pl.pallas_call(
        kernel,
        out_shape=tuple(shapes),
        in_specs=[SMEM_SPEC] + [VMEM_SPEC] * len(operands) + order.specs(),
        out_specs=tuple([VMEM_SPEC] * len(outputs)),
        compiler_params=PARAMS,
        cost_estimate=COST,
        name=name,
    )
    return order.then(call(table, *operands, *order.last))


def halves_of(z, order, place, array, parts, name):
    view = array.reshape(z.slots, CORES, z.half, z.cols)
    step = math.gcd(z.half, 64)

    def kernel(place_ref, *refs):
        @pl.loop(0, z.half // step)
        def _(at):
            rows = pl.ds(pl.multiple_of(at * step, 16), step)
            for array_ref, out_ref in zip(refs, refs[-len(parts) :]):
                out_ref[rows] = array_ref[0, 0, rows].astype(jnp.bfloat16)

    def half_of(part):
        def index_map(slot, place_ref):
            core = lax.rem(place_ref[0], CORES)
            return (slot, 1 - core if part else core, 0, 0)

        return index_map

    out = jax.ShapeDtypeStruct((z.slots * z.half, z.cols), jnp.bfloat16)
    out_spec = pl.BlockSpec((z.half, z.cols), lambda slot, place_ref: (slot, 0))
    call = pl.pallas_call(
        kernel,
        grid_spec=pltpu.PrefetchScalarGridSpec(
            num_scalar_prefetch=1,
            grid=(z.slots,),
            in_specs=[pl.BlockSpec((1, 1, z.half, z.cols), half_of(part)) for part in parts]
            + order.specs(),
            out_specs=[out_spec] * len(parts),
        ),
        out_shape=[out] * len(parts),
        compiler_params=PARAMS,
        cost_estimate=COST,
        name="halve_" + name,
    )
    return order.then(call(place, *[view] * len(parts), *order.last))


def update(z, order, table, start, part, state, rebuilt, mean, outs):
    views = [a.reshape(z.slots * z.rows, z.cols) for a in state]
    outs = [] if outs is None else list(outs)
    rows, cols = 16, min(z.cols, 128)
    unroll = math.gcd(z.half // rows, 4)

    def half_now(table_ref):
        core = table_ref[start + 1]
        return core if part == 0 else 1 - core

    def kernel(table_ref, *refs):
        local_refs, lost_refs, mean_ref = refs[:3], refs[3:6], refs[6]
        out_refs = refs[-3:]
        slot = pl.program_id(0)
        is_lost = table_ref[start] != 0
        found = table_ref[start + 2 + slot] != 0

        def each(sources, base):
            @pl.loop(0, z.half // (rows * unroll))
            def _(at):
                for first in range(unroll):
                    for lane in range(0, z.cols, cols):
                        one_block(sources, base, (at * unroll + first) * rows, lane)

        def one_block(sources, base, at, lane):
            row = pl.ds(pl.multiple_of(at, rows), rows)
            mean_row = pl.ds(pl.multiple_of(slot * z.half + at, rows), rows)
            from_row = pl.ds(pl.multiple_of(base + at, rows), rows)
            lanes = pl.ds(lane, cols)
            weight, one, two = [ref[from_row, lanes].astype(jnp.float32) for ref in sources]
            grad = mean_ref[mean_row, lanes].astype(jnp.float32)
            next_one = BETA_ONE * one + ((1.0 - BETA_ONE) / z.pipes) * grad
            next_two = BETA_TWO * two + ((1.0 - BETA_TWO) / z.pipes**2) * (grad * grad)
            scale = next_two * lax.rsqrt(next_two) + EPSILON
            move = next_one * lax.rsqrt(scale * scale)
            next_weight = (1.0 - LEARN_RATE * DECAY_RATE) * weight - LEARN_RATE * move
            for ref, value in zip(out_refs, (next_weight, next_one, next_two)):
                ref[0, 0, row, lanes] = value.astype(ref.dtype)

        @pl.when(both(found, is_lost))
        def _():
            each(lost_refs, slot * z.half)

        @pl.when(both(found, jnp.logical_not(is_lost)))
        def _():
            each(local_refs, slot * z.rows + half_now(table_ref) * z.half)

        @pl.when(jnp.logical_not(found))
        def _():
            @pl.loop(0, z.half // rows)
            def _(at):
                for ref in out_refs:
                    row = pl.ds(pl.multiple_of(at * rows, rows), rows)
                    ref[0, 0, row] = jnp.zeros((rows, z.cols), ref.dtype)

    block = (1, 1, z.half, z.cols)
    out_spec = pl.BlockSpec(block, lambda slot, table_ref: (slot, half_now(table_ref), 0, 0))
    shape = (z.slots, CORES, z.half, z.cols)
    call = pl.pallas_call(
        kernel,
        grid_spec=pltpu.PrefetchScalarGridSpec(
            num_scalar_prefetch=1,
            grid=(z.slots,),
            in_specs=[VMEM_SPEC] * 7
            + [pl.BlockSpec(memory_space=pl.ANY)] * len(outs)
            + order.specs(),
            out_specs=[out_spec] * 3,
        ),
        out_shape=(
            jax.ShapeDtypeStruct(shape, jnp.bfloat16),
            jax.ShapeDtypeStruct(shape, jnp.float32),
            jax.ShapeDtypeStruct(shape, jnp.float32),
        ),
        input_output_aliases={8 + at: at for at in range(len(outs))},
        compiler_params=PARAMS,
        cost_estimate=UPDATE_COST,
        name="update",
    )
    operands = (*views, *(half[part] for half in rebuilt), mean[part], *outs)
    return order.then(call(table, *operands, *order.last))


class Gradients:
    def __init__(self, z, order, grads):
        self.z, self.order, self.grads = z, order, grads

    def run(self, outputs, name):
        return stage(self.z, self.order, self.table, outputs, name)

    def rows(self, value):
        return Rows(value, self.z.grad_band, self.z.layers)

    def enter(self, place):
        z = self.z
        theirs, own = halves_of(z, self.order, place, self.grads, (1, 0), "gradients")
        theirs = self.order.arrived(z.to_core(theirs))
        self.held = [Rows(half, z.grad_band, z.slots * z.groups) for half in (own, theirs)]

    def scatter(self):
        z = self.z
        shifts = range(1, z.groups)
        jobs = [[Sum(self.starts["grad_out", s], z.layers, self.held)] for s in shifts]
        parts = self.run(jobs, "grad_out")
        self.held += [
            self.rows(self.order.arrived(z.to_group(part, s))) for s, part in zip(shifts, parts)
        ]

    def exchange(self):
        z = self.z
        (part,) = self.run([[Sum(self.starts["grad_sum"], z.layers, self.held)]], "grad_sum")
        others = [self.order.arrived(z.to_section(part, s)) for s in range(1, z.sections)]
        self.held = [self.rows(value) for value in (part, *others)]

    def gather(self):
        z = self.z
        (part,) = self.run([[Sum(self.starts["grad_mean"], z.layers, self.held)]], "grad_mean")
        others = [self.order.arrived(z.to_group(part, s)) for s in range(1, z.groups)]
        self.held = [self.rows(value) for value in (part, *others)]

    def finish(self):
        z = self.z
        theirs, mine = self.run(
            [
                [Copy(self.starts[name], z.slots * z.groups, self.held)]
                for name in ("sibling", "mine")
            ],
            "mean",
        )
        self.mean = (mine, self.order.arrived(z.to_core(theirs)))


class Chunk:
    def __init__(self, z, order, array):
        self.z, self.order, self.array = z, order, array

    def run(self, outputs, name):
        return stage(self.z, self.order, self.table, outputs, name)

    def enter(self, place):
        z = self.z
        (theirs,) = halves_of(z, self.order, place, self.array, (1,), "state")
        theirs = z.to_core(theirs)
        own = self.array.reshape(z.slots * z.rows, z.cols)
        theirs = self.order.arrived(theirs)
        held = z.slots * z.sections
        self.held = [Rows(own, z.band, CORES * held), Rows(theirs, z.band, held)]

    def spread(self):
        z = self.z
        shifts = range(1, z.sections)
        jobs = [[Copy(self.starts["spread", s], z.channels, self.held)] for s in shifts]
        parts = self.run(jobs, "spread")
        for s, part in zip(shifts, parts):
            self.held.append(Rows(self.order.arrived(z.to_section(part, s)), z.band, z.channels))

    def across(self):
        z = self.z
        (part,) = self.run([[Copy(self.starts["across"], z.layers, self.held)]], "across")
        for s in range(1, z.groups):
            self.held.append(Rows(self.order.arrived(z.to_group(part, s)), z.band, z.layers))

    def deliver(self):
        z = self.z
        shifts = range(1, z.sections)
        jobs = [[Copy(self.starts["deliver", s], z.slots, self.held)] for s in shifts]
        parts = self.run(jobs, "deliver")
        for s, part in zip(shifts, parts):
            self.held.append(Rows(self.order.arrived(z.to_section(part, s)), z.band, z.slots))

    def collect(self):
        z = self.z
        units = z.slots * z.sections
        (half,) = self.run([[Copy(self.starts["collect"], units, self.held)]], "collect")
        self.halves = (half, self.order.arrived(z.to_core(half)))


def per_device(
    weights,
    first_moment,
    second_moment,
    gradients,
    old_section,
    new_section,
    lost_pipe,
    donor_offset,
):
    z = Sizes(weights, new_section)
    order = Order()
    place = jnp.stack([lax.axis_index("pipe"), lax.axis_index("section")]).astype(jnp.int32)
    state = (weights[0, 0], first_moment[0, 0], second_moment[0, 0])
    grads = Gradients(z, order, gradients[0, 0])
    chunks = [Chunk(z, order, array) for array in state]
    table, starts = make_plan(z, place, old_section, new_section, lost_pipe, donor_offset)
    for part in (grads, *chunks):
        part.table, part.starts = table, starts

    for name in SEQUENCE:
        order.begin(name)
        if name[0] == "g" and name[1] in "esxgf":
            part = grads
            step = dict(e="enter", s="scatter", x="exchange", g="gather", f="finish")[name[1]]
        else:
            part = chunks[int(name[1])]
            step = dict(e="enter", s="spread", a="across", d="deliver", c="collect")[name[0]]
        if step == "enter":
            part.enter(place)
        else:
            getattr(part, step)()
    order.begin("u")
    rebuilt = [chunk.halves for chunk in chunks]
    outs = None
    for part in range(CORES):
        outs = update(z, order, table, starts["update"], part, state, rebuilt, grads.mean, outs)
    return tuple(out.reshape((1, 1, z.slots, z.rows, z.cols)) for out in outs)


def solution(mesh):
    split = P("pipe", "section", None, "tp", None)
    return jax.shard_map(
        per_device,
        mesh=mesh,
        in_specs=(split,) * 4 + (P(),) * 4,
        out_specs=(split,) * 3,
        check_vma=False,
    )
```
